128 devices in a mesh: lon: 8 (over y, x_hi), lat: 16 (over x_lo, z, core).
Axes of the slice: x: 4 (x_hi: 2, x_lo: 2; x = x_hi * 2 + x_lo), y: 4, z: 4, core: 2. Of those that a mesh axis runs over, the one named last changes fastest.
Arguments:
- tokens: bfloat16 [4, 192, 384, 192], P(None, 'lat', 'lon'), may hold values from -6 to 6
- cotangent: bfloat16 [4, 192, 384, 192], P(None, 'lat', 'lon'), may hold values from -6 to 6
- region_ids: int32 [192], P('lat'), may hold values from 0 to 47, never falling along the last dimension, each value on 1 to 12 neighbouring positions
- norm_gains: float32 [2, 192], replicated, may hold values from 0.5 to 1.5
- w_qkv: bfloat16 [192, 576], replicated, may hold values from -0.4375 to 0.4375
- w_proj: bfloat16 [192, 192], replicated, may hold values from -0.4375 to 0.4375
- w_up: bfloat16 [192, 768], replicated, may hold values from -0.4375 to 0.4375
- w_down: bfloat16 [768, 192], replicated, may hold values from -0.21875 to 0.21875
- earth_bias: float32 [2, 32, 6, 144, 144], P(None, 'lat'), may hold values from -2 to 250
Outputs:
- grad_tokens: bfloat16 [4, 192, 384, 192], P(None, 'lat', 'lon')
- grad_qkv: float32 [192, 576], replicated
- grad_proj: float32 [192, 192], replicated
- grad_up: float32 [192, 768], replicated
- grad_down: float32 [768, 192], replicated
- grad_gains: float32 [2, 192], replicated
- grad_bias: float32 [2, 32, 6, 144, 144], P(None, 'lat', None, 'lon')
The draws below stay inside these ranges and needn't reach their ends.
Inputs may be any that keep to these rules, and one draw needn't show every extreme that they name: `region_ids`: never falls from one latitude row to the next; a run of equal ids spans 1 to 12 rows.
All inputs are finite; a program needn't handle non-finite values.
Results may differ from the reference program's by a relative error of at most 0.015.
Values may be sent and summed in bfloat16 or wider, within the bound.
No kernel may reach another device: no remote copies, remote signals or barrier semaphores. Data moves between devices by JAX's collectives and lax.ppermute only.
A program may use at most 192 MiB of HBM per device.

```python
import math
import jax
import jax.numpy as jnp
import numpy as np
from jax import lax

C = 192
HEADS = 6
FF = 768
HD = 32
WLEV = 2
WLAT = 6
WLON = 12
M = 144
LEV = 4
NLAT = 192
NLON = 384
LEVW = 2
NLATW = 32
TOKENS = 294912


def draw_earth_bias(key, part):
    key = jax.random.fold_in(key, 11)
    shape_all = (LEVW, NLATW, HEADS, M, M)
    subkeys = jax.random.split(key, 1)
    return 0.5 * jnp.clip(jax.random.normal(subkeys[0], shape_all, jnp.float32), -4.0, 4.0)


def shard_levels(stream_key, extent, shards, low, high):
    level, own = 1.0, jax.random.fold_in(stream_key, 6)
    for axis_at, parts in shards:
        steps = jnp.exp(jax.random.uniform(jax.random.fold_in(own, axis_at), (parts,), jnp.float32, low / len(shards), high / len(shards)))
        level = level * jnp.repeat(steps, extent[axis_at] // parts).reshape([-1 if axis == axis_at else 1 for axis in range(len(extent))])
    return level


def profile(count, total, limit, skew):
    weights = [(1 << 20) // math.isqrt(standing ** skew) + 1 for standing in range(2, count + 1)]
    surplus, given = total - limit - (count - 1), [1] * (count - 1)
    while surplus > 0:
        candidates = [i for i in range(count - 1) if given[i] < limit]
        mass, remaining = sum([weights[i] for i in candidates]), surplus
        for i in candidates:
            more = min(limit - given[i], max(1, remaining * weights[i] // mass), surplus)
            given[i] = given[i] + more
            surplus = surplus - more
    return np.array([limit] + given)


def uneven_parts(stream_key, number_of, total, most, slope):
    if number_of == 2:
        one = jax.random.randint(stream_key, (), max(1, total - most), min(most, total - 1) + 1)
        return jnp.stack([one, total - one])
    tallies = jnp.asarray(profile(number_of, total, most, slope), jnp.int32)
    twos = (number_of - 1) // 2
    giver, sink = tallies[1:1 + 2 * twos:2], tallies[2:2 + 2 * twos:2]
    margin = jnp.minimum(giver - 1, most - sink)
    moved = jax.random.randint(jax.random.fold_in(stream_key, 1), (twos,), 0, 1 << 20) % (margin + 1)
    tallies = tallies.at[1:1 + 2 * twos:2].set(giver - moved).at[2:2 + 2 * twos:2].set(sink + moved)
    return tallies[jax.random.permutation(jax.random.fold_in(stream_key, 2), number_of)]


def bell_draw(rng, dims, width, bound, pieces=(), dtype=jnp.bfloat16):
    entries = jax.random.normal(rng, dims, jnp.float32) * width
    if len(pieces) > 0:
        entries = shard_levels(rng, dims, pieces, -0.22, 0.18) * entries
    return jnp.clip(entries, min=-bound, max=bound).astype(dtype)


def setup_inputs(seed: int = 0) -> dict:
    key_list = jax.random.split(jax.random.key(seed), 10)
    tokens = bell_draw(key_list[0], (LEV, NLAT, NLON, C), 1.0, 6.0, ((1, 16), (2, 8)))
    cotangent = bell_draw(key_list[1], (LEV, NLAT, NLON, C), 1.0, 6.0, ((1, 16), (2, 8)))
    region_ids = jnp.searchsorted(jnp.cumsum(uneven_parts(key_list[2], NLAT // 4, NLAT, 12, 1)), jnp.arange(NLAT), side="right").astype(jnp.int32)
    norm_gains = jnp.clip(1.0 + 0.1 * jax.random.normal(key_list[3], (2, C), jnp.float32), 0.5, 1.5)
    w_qkv = bell_draw(key_list[4], (C, 3 * C), C ** -0.5, 0.4375)
    w_proj = bell_draw(key_list[5], (C, C), C ** -0.5, 0.4375)
    w_up = bell_draw(key_list[6], (C, FF), C ** -0.5, 0.4375)
    w_down = bell_draw(key_list[7], (FF, C), FF ** -0.5, 0.21875)
    earth_bias = draw_earth_bias(jax.random.fold_in(key_list[9], 71), 0)
    return {"tokens": tokens, "cotangent": cotangent, "region_ids": region_ids, "norm_gains": norm_gains, "w_qkv": w_qkv, "w_proj": w_proj, "w_up": w_up, "w_down": w_down, "earth_bias": earth_bias}


epsilon = 1e-05
inv_root_two = 0.7071067811865476
inv_root_tau = 0.3989422804014327

def mult(form, left, right):
    return jnp.einsum(form, left.astype(jnp.float32), right.astype(jnp.float32))

def contract_rows(left, right):
    return jnp.dot(left.T, right, preferred_element_type=jnp.float32)

def contract_cols(left, right):
    return jnp.dot(left, right.T, preferred_element_type=jnp.float32)

def normalize(values):
    centred = values - lax.optimization_barrier(jnp.mean(values, axis=-1, keepdims=True))
    inverse = lax.rsqrt(lax.optimization_barrier(jnp.mean(centred * centred, axis=-1, keepdims=True)) + epsilon)
    return (centred * inverse, inverse)

def norm_back(normed, inverse, gain_row, upstream):
    scaled = upstream * gain_row
    return inverse * (scaled - lax.optimization_barrier(jnp.mean(scaled, axis=-1, keepdims=True)) - normed * lax.optimization_barrier(jnp.mean(scaled * normed, axis=-1, keepdims=True)))

def to_windows(layer_in):
    levels, row_count, col_count, channels = layer_in.shape
    grouped = layer_in.reshape(levels // WLEV, WLEV, row_count // WLAT, WLAT, col_count // WLON, WLON, channels)
    return grouped.transpose(0, 2, 4, 1, 3, 5, 6).reshape(levels // WLEV, row_count // WLAT, col_count // WLON, WLEV * WLAT * WLON, channels)

def from_windows(windows, levels, row_count, col_count):
    channels = windows.shape[-1]
    grouped = windows.reshape(levels // WLEV, row_count // WLAT, col_count // WLON, WLEV, WLAT, WLON, channels)
    return grouped.transpose(0, 3, 1, 4, 2, 5, 6).reshape(levels, row_count, col_count, channels)

def region_mask(row_ids):
    lookup = np.arange(WLEV * WLAT * WLON) // WLON % WLAT
    per_token = row_ids.reshape(-1, WLAT)[:, lookup]
    return per_token[:, :, None] == per_token[:, None, :]

def attend_forward(shifted, allowed, bias, w_qkv, w_proj, scaling):
    levels, row_count, col_count, channels = shifted.shape
    head_size = channels // HEADS
    windows = to_windows(shifted)
    mixed = mult('abnmc,cd->abnmd', windows, w_qkv)
    mixed = mixed.reshape(mixed.shape[:4] + (3, HEADS, head_size))
    queries = (mixed[..., 0, :, :] * scaling).astype(jnp.bfloat16)
    keys_low = mixed[..., 1, :, :].astype(jnp.bfloat16)
    values = mixed[..., 2, :, :].astype(jnp.bfloat16)
    scores = mult('abnmhd,abnkhd->abnhmk', queries, keys_low) + bias[:, :, None]
    scores = jnp.where(allowed[None, :, None, None], scores, -1e+30)
    largest = lax.optimization_barrier(jnp.max(scores, axis=-1, keepdims=True))
    powers = jnp.exp(scores - largest)
    weights = powers / lax.optimization_barrier(jnp.sum(powers, axis=-1, keepdims=True))
    rounded = weights.astype(jnp.bfloat16)
    merged = mult('abnhmk,abnkhd->abnmhd', rounded, values).astype(jnp.bfloat16).reshape(windows.shape)
    projected = mult('abnmc,ce->abnme', merged, w_proj).astype(jnp.bfloat16)
    attended = from_windows(projected, levels, row_count, col_count)
    return (attended, (windows, queries, keys_low, values, weights, rounded, merged))

def attend_backward(saved, upstream, w_qkv, w_proj, scaling):
    windows, queries, keys_low, values, weights, rounded, merged = saved
    levels, row_count, col_count, channels = upstream.shape
    grad_windows = to_windows(upstream)
    grad_proj = mult('abnmc,abnme->ce', merged, grad_windows)
    grad_merged = mult('abnme,ce->abnmc', grad_windows, w_proj).astype(jnp.bfloat16).reshape(queries.shape)
    grad_values = mult('abnhmk,abnmhd->abnkhd', rounded, grad_merged)
    grad_weights = mult('abnmhd,abnkhd->abnhmk', grad_merged, values)
    grad_scores = weights * (grad_weights - lax.optimization_barrier(jnp.sum(weights * grad_weights, axis=-1, keepdims=True)))
    grad_bias = lax.optimization_barrier(jnp.sum(grad_scores, axis=2))
    scores_low = grad_scores.astype(jnp.bfloat16)
    grad_queries = mult('abnhmk,abnkhd->abnmhd', scores_low, keys_low) * scaling
    grad_keys = mult('abnhmk,abnmhd->abnkhd', scores_low, queries)
    grad_mixed = jnp.stack([grad_queries, grad_keys, grad_values], axis=4).astype(jnp.bfloat16)
    grad_mixed = grad_mixed.reshape(windows.shape[:4] + (3 * channels,))
    grad_qkv = mult('abnmc,abnmd->cd', windows, grad_mixed)
    grad_shifted = mult('abnmd,cd->abnmc', grad_mixed, w_qkv).astype(jnp.bfloat16)
    return (from_windows(grad_shifted, levels, row_count, col_count), grad_qkv, grad_proj, grad_bias)

def feed_forward(tokens, attended, upstream, gain_row, w_up, w_down):
    shape_in = tokens.shape
    channels = shape_in[-1]
    residual = tokens.astype(jnp.float32).reshape(-1, channels) + attended.astype(jnp.float32).reshape(-1, channels)
    normed, inverse = normalize(residual)
    inner_in = (normed * gain_row).astype(jnp.bfloat16)
    hidden = jnp.dot(inner_in, w_up, preferred_element_type=jnp.float32)
    normal_cdf = 0.5 * (1.0 + jax.scipy.special.erf(hidden * inv_root_two))
    activated = (hidden * normal_cdf).astype(jnp.bfloat16)
    grad_out = upstream.reshape(-1, channels)
    grad_down = contract_rows(activated, grad_out)
    grad_act = contract_cols(grad_out, w_down)
    derivative = normal_cdf + hidden * jnp.exp(-0.5 * hidden * hidden) * inv_root_tau
    grad_hidden = (grad_act * derivative).astype(jnp.bfloat16)
    grad_up = contract_rows(inner_in, grad_hidden)
    grad_inner = contract_cols(grad_hidden, w_up)
    second_gain = lax.optimization_barrier(jnp.sum(grad_inner * normed, axis=0))
    grad_resid = grad_out.astype(jnp.float32) + norm_back(normed, inverse, gain_row, grad_inner)
    return (grad_resid.reshape(shape_in), grad_up, grad_down, second_gain)

def run_block(tokens, cotangent, row_ids, bias, norm_gains, w_qkv, w_proj, w_up, w_down, scaling):
    normed, inverse = normalize(tokens.astype(jnp.float32))
    shifted = (normed * norm_gains[0]).astype(jnp.bfloat16)
    attended, saved = attend_forward(shifted, region_mask(row_ids), bias, w_qkv, w_proj, scaling)
    attended = lax.optimization_barrier(attended)
    grad_resid, grad_up, grad_down, second_gain = feed_forward(tokens, attended, cotangent, norm_gains[1], w_up, w_down)
    grad_back, grad_qkv, grad_proj, grad_bias = attend_backward(saved, grad_resid.astype(jnp.bfloat16), w_qkv, w_proj, scaling)
    grad_back = lax.optimization_barrier(grad_back)
    back_float = grad_back.astype(jnp.float32)
    grad_tokens = (grad_resid + norm_back(normed, inverse, norm_gains[0], back_float)).astype(jnp.bfloat16)
    first_gain = lax.optimization_barrier(jnp.sum(back_float * normed, axis=(0, 1, 2)))
    return (grad_tokens, (grad_qkv, grad_proj, grad_up, grad_down, jnp.stack([first_gain, second_gain])), grad_bias)

def reference(tokens, cotangent, region_ids, norm_gains, w_qkv, w_proj, w_up, w_down, earth_bias):
    half_lat = WLAT // 2
    half_lon = WLON // 2
    scaling = float(HD) ** (-0.5)
    rolled = jnp.roll(tokens, (-half_lat, -half_lon), axis=(1, 2))
    rolled_grad = jnp.roll(cotangent, (-half_lat, -half_lon), axis=(1, 2))
    rolled_ids = jnp.roll(region_ids, -half_lat)
    band_tokens = rolled.reshape(LEV, NLATW, WLAT, NLON, C).transpose(1, 0, 2, 3, 4)
    band_grads = rolled_grad.reshape(LEV, NLATW, WLAT, NLON, C).transpose(1, 0, 2, 3, 4)
    band_ids = rolled_ids.reshape(NLATW, WLAT)
    band_bias = earth_bias.transpose(1, 0, 2, 3, 4)[:, :, None]

    def band_step(totals, inputs):
        block_tokens, block_grads, block_ids, block_bias = inputs
        grad_block, partial_sums, bias_part = run_block(block_tokens, block_grads, block_ids, block_bias, norm_gains, w_qkv, w_proj, w_up, w_down, scaling)
        return (jax.tree.map(jnp.add, totals, partial_sums), (grad_block, bias_part))
    initial = (jnp.zeros((C, 3 * C), jnp.float32), jnp.zeros((C, C), jnp.float32), jnp.zeros((C, FF), jnp.float32), jnp.zeros((FF, C), jnp.float32), jnp.zeros((2, C), jnp.float32))
    totals, (grad_bands, bias_bands) = lax.scan(band_step, initial, (band_tokens, band_grads, band_ids, band_bias))
    grad_rolled = grad_bands.transpose(1, 0, 2, 3, 4).reshape(LEV, NLAT, NLON, C)
    grad_tokens = jnp.roll(grad_rolled, (half_lat, half_lon), axis=(1, 2))
    grad_bias = bias_bands[:, :, 0].transpose(1, 0, 2, 3, 4)
    rescale = 1.0 / math.sqrt(TOKENS)
    grad_qkv, grad_proj, grad_up, grad_down, grad_gains = totals
    return (grad_tokens, grad_qkv * rescale, grad_proj * rescale, grad_up * rescale, grad_down * rescale, grad_gains * rescale, grad_bias)
```

```python
import functools
import math

import jax
import jax.numpy as jnp
import numpy as np
from jax import lax
from jax.experimental import pallas as pl
from jax.experimental.pallas import tpu as pltpu
from jax.sharding import PartitionSpec as P

HEADS = 6
HEAD = 32
WLEV = 2
WLAT = 6
WLON = 12
C = HEADS * HEAD
FF = 4 * C
M = WLEV * WLAT * WLON
MAIN = 128
REST = M - MAIN
LANES = (HEADS + 1) * 128
SLABS = WLEV * WLAT

BF = jnp.bfloat16
F32 = jnp.float32
epsilon = 1e-05
inv_root_two = 0.7071067811865476
inv_root_tau = 0.3989422804014327


def perm(value, axis, steps):
    count = lax.axis_size(axis)
    pairs = [(source, (source + steps) % count) for source in range(count)]
    return lax.ppermute(value, axis, pairs)


def dot(left, right):
    return jnp.dot(left, right, preferred_element_type=F32)


def dot_nt(left, right):
    return lax.dot_general(left, right, (((1,), (1,)), ((), ())), preferred_element_type=F32)


def dot_tn(left, right):
    return lax.dot_general(left, right, (((0,), (0,)), ((), ())), preferred_element_type=F32)


def normalize(values):
    centred = values - jnp.mean(values, axis=-1, keepdims=True)
    inverse = lax.rsqrt(jnp.mean(centred * centred, axis=-1, keepdims=True) + epsilon)
    return centred * inverse, inverse


def norm_back(normed, inverse, gain_row, upstream):
    scaled = upstream * gain_row
    return inverse * (
        scaled
        - jnp.mean(scaled, axis=-1, keepdims=True)
        - normed * jnp.mean(scaled * normed, axis=-1, keepdims=True)
    )


def gelu_parts(u):
    bell = jnp.exp(u * u * -0.5)
    under = 1.0 + jnp.abs(u) * (0.3275911 * inv_root_two)
    t = pl.reciprocal(under, approx=True)
    t = t * (2.0 - under * t)
    tail = t * (
        0.5 * 0.254829592
        + t
        * (
            0.5 * -0.284496736
            + t * (0.5 * 1.421413741 + t * (0.5 * -1.453152027 + t * (0.5 * 1.061405429)))
        )
    )
    tail = tail * bell
    cdf = jnp.where(u >= 0.0, 1.0 - tail, tail)
    return cdf, cdf + u * (bell * inv_root_tau)


CHUNKS = ((0, 256), (256, 512), (512, 768), (768, 896))


def spread_heads(rows, mask):
    first, last = rows[:MAIN], rows[MAIN:]
    return jnp.concatenate([first] * HEADS + [last] * 8, axis=0) * mask


def per_query(weights_ref, right, right_t, rest_mask):
    parts = [
        dot(
            right_t[HEAD * e : HEAD * (e + 1), :],
            weights_ref[:, 128 * e : 128 * (e + 1)],
        )
        for e in range(HEADS)
    ]
    first = jnp.concatenate(parts, axis=0).T
    last = dot_tn(weights_ref[:, HEADS * 128 :], right) * rest_mask
    total = last[0:REST]
    for e in range(1, HEADS):
        total = total + last[REST * e : REST * (e + 1)]
    return jnp.concatenate([first, total], axis=0)


def block_kernel(
    tok_ref, cot_ref, bias_ref, kid_ref, qid_ref, gains_ref, mask_ref,
    wq_ref, wk_ref, wv_ref, wp_ref, wup_ref, wqt_ref, wkt_ref, wvt_ref, wpt_ref, wupt_ref, wdt_ref,
    gtok_ref, gbias_ref, pack_ref,
    grid_ref, grid2_ref, x_ref, c_ref, cb_ref, h_ref, n1_ref, r1_ref, biast_ref, gbt_ref,
    p_ref, pb_ref, ds_ref, qbd_ref, dobd_ref, o_ref, dys_ref, dq_ref, dk_ref, dv_ref,
    g_ref, act_ref, du_ref, gt_ref, acc_ref, gacc_ref,
):
    cols = tok_ref.shape[2]
    windows = cols // WLON
    rows = windows * M
    step = pl.program_id(0) * pl.num_programs(1) + pl.program_id(1)
    last_step = pl.num_programs(0) * pl.num_programs(1) - 1

    @pl.when(step == 0)
    def _():
        acc_ref[...] = jnp.zeros_like(acc_ref)
        gacc_ref[...] = jnp.zeros_like(gacc_ref)

    grid_ref[...] = tok_ref[...].reshape(rows, C).astype(F32)
    grid2_ref[...] = cot_ref[...].reshape(rows, C).astype(F32)
    for n in range(windows):
        for s in range(SLABS):
            to = n * M + s * WLON
            at = s * cols + n * WLON
            x_ref[to : to + WLON, :] = grid_ref[at : at + WLON, :]
            c_ref[to : to + WLON, :] = grid2_ref[at : at + WLON, :]

    gain0 = gains_ref[0:1, :]
    gain1 = gains_ref[1:2, :]

    rest_pad = jnp.zeros((128 - HEADS * REST, M), F32)
    rest = jnp.concatenate([bias_ref[0, 0, e, MAIN:, :] for e in range(HEADS)] + [rest_pad], axis=0)
    kid = kid_ref[0]
    for e in range(HEADS + 1):
        block = bias_ref[0, 0, e, :MAIN, :] if e < HEADS else rest
        lanes = slice(128 * e, 128 * (e + 1))
        biast_ref[:, lanes] = jnp.where(kid == qid_ref[0, :, lanes], block.T, -1e30)
    gbt_ref[...] = jnp.zeros_like(gbt_ref)

    scaling = float(HEAD) ** -0.5

    def window(n, carry):
        here = pl.ds(pl.multiple_of(n * M, M), M)
        x = x_ref[here, :]
        n1, r1 = normalize(x)
        n1_ref[here, :] = n1
        r1_ref[here, :] = r1
        h = (n1 * gain0).astype(BF)
        h_ref[here, :] = h
        q = (dot(h, wq_ref[...]) * scaling).astype(BF)
        k32 = dot(h, wk_ref[...])
        v32 = dot(h, wv_ref[...])
        k = k32.astype(BF)
        v = v32.astype(BF)
        kt = k32.T.astype(BF)
        vt = v32.T.astype(BF)
        qbd_ref[...] = spread_heads(q, mask_ref[...])
        for lo, hi in CHUNKS:
            scores = dot_nt(k, qbd_ref[lo:hi, :]) + biast_ref[:, lo:hi]
            powers = jnp.exp(scores - jnp.max(scores, axis=0, keepdims=True))
            weights = powers * (1.0 / jnp.sum(powers, axis=0, keepdims=True))
            p_ref[:, lo:hi] = weights
            pb_ref[:, lo:hi] = weights.astype(BF)
        rest_mask = mask_ref[HEADS * 128 :, :].astype(F32)
        o = per_query(pb_ref, v, vt, rest_mask).astype(BF)
        o_ref[here, :] = o
        attended = dot(o, wp_ref[...]).astype(BF).astype(F32)
        n2, r2 = normalize(x + attended)
        g = (n2 * gain1).astype(BF)
        g_ref[here, :] = g
        c32 = c_ref[here, :]
        cb = c32.astype(BF)
        cb_ref[here, :] = cb
        dg = jnp.zeros((M, C), F32)
        for lo in range(0, FF, 256):
            part = slice(lo, lo + 256)
            u = dot(g, wup_ref[:, part])
            cdf, slope = gelu_parts(u)
            act_ref[here, part] = (u * cdf).astype(BF)
            du = (dot(cb, wdt_ref[:, part]) * slope).astype(BF)
            du_ref[here, part] = du
            dg = dg + dot(du, wupt_ref[part, :])
        gacc_ref[8:16, :] += jnp.sum((dg * n2).reshape(M // 8, 8, C), axis=0)
        dy = c32 + norm_back(n2, r2, gain1, dg)
        gt_ref[here, :] = dy
        dys = dy.astype(BF)
        dys_ref[here, :] = dys
        do = dot(dys, wpt_ref[...]).astype(BF)
        dobd_ref[...] = spread_heads(do, mask_ref[...])
        for lo, hi in CHUNKS:
            weights = p_ref[:, lo:hi]
            dp = dot_nt(v, dobd_ref[lo:hi, :]) * weights
            ds = dp - weights * jnp.sum(dp, axis=0, keepdims=True)
            gbt_ref[:, lo:hi] += ds
            ds_ref[:, lo:hi] = ds.astype(BF)
        dv = dot(pb_ref[...], dobd_ref[...]).astype(BF)
        dk = dot(ds_ref[...], qbd_ref[...]).astype(BF)
        dq = (per_query(ds_ref, k, kt, rest_mask) * scaling).astype(BF)
        dq_ref[here, :] = dq
        dk_ref[here, :] = dk
        dv_ref[here, :] = dv
        dh = dot(dq, wqt_ref[...]) + dot(dk, wkt_ref[...]) + dot(dv, wvt_ref[...])
        dh = dh.astype(BF).astype(F32)
        n1 = n1_ref[here, :]
        gacc_ref[0:8, :] += jnp.sum((dh * n1).reshape(M // 8, 8, C), axis=0)
        gt_ref[here, :] += norm_back(n1, r1_ref[here, :], gain0, dh)
        return carry

    lax.fori_loop(0, windows, window, 0)

    for n in range(windows):
        for s in range(SLABS):
            at = n * M + s * WLON
            to = s * cols + n * WLON
            grid_ref[to : to + WLON, :] = gt_ref[at : at + WLON, :]
    gtok_ref[...] = grid_ref[...].astype(BF).reshape(gtok_ref.shape)

    for e in range(HEADS):
        gbias_ref[0, 0, e, :MAIN, :] = gbt_ref[:, 128 * e : 128 * (e + 1)].T.astype(BF)
    rest = gbt_ref[:, HEADS * 128 :].T.astype(BF)
    for e in range(HEADS):
        gbias_ref[0, 0, e, MAIN:, :] = rest[REST * e : REST * (e + 1), :]

    h = h_ref[...]
    small = [
        dot_tn(h, dq_ref[...]),
        dot_tn(h, dk_ref[...]),
        dot_tn(h, dv_ref[...]),
        dot_tn(o_ref[...], dys_ref[...]),
    ]
    for i in range(2):
        one, two = small[2 * i], small[2 * i + 1]
        acc_ref[3 * i] += one[:, :128]
        acc_ref[3 * i + 1] += two[:, :128]
        acc_ref[3 * i + 2] += jnp.concatenate([one[:, 128:], two[:, 128:]], axis=1)
    up = dot_tn(g_ref[...], du_ref[...])
    down = dot_tn(cb_ref[...], act_ref[...])
    for i in range(FF // 128):
        acc_ref[6 + i] += up[:, 128 * i : 128 * (i + 1)]
        acc_ref[12 + i] += down[:, 128 * i : 128 * (i + 1)]

    @pl.when(step == last_step)
    def _():
        for i in range(18):
            pack_ref[C * i : C * (i + 1), :] = acc_ref[i].astype(BF)
        gains = jnp.concatenate(
            [
                jnp.sum(gacc_ref[0:8, :], axis=0, keepdims=True),
                jnp.sum(gacc_ref[8:16, :], axis=0, keepdims=True),
                jnp.zeros((6, C), F32),
            ],
            axis=0,
        )
        wide = jnp.concatenate(
            [gains[:, :128], jnp.concatenate([gains[:, 128:], jnp.zeros((8, 64), F32)], axis=1)],
            axis=0,
        )
        pack_ref[18 * C : 18 * C + 16, :] = wide.astype(BF)


def run_block(tokens, cotangent, bias, row_ids, gains, w_qkv, w_proj, w_up, w_down):
    levels, nrows, cols, channels = tokens.shape
    blocks = levels // WLEV
    bands = nrows // WLAT
    rows = (cols // WLON) * M
    cell_row = np.arange(M) // WLON % WLAT
    rest = np.concatenate([np.tile(np.arange(MAIN, M), HEADS), np.zeros(128 - HEADS * REST, int)])
    lane_cell = np.concatenate([np.tile(np.arange(MAIN), HEADS), rest])
    band_ids = row_ids.reshape(bands, WLAT)
    kid = band_ids[:, cell_row][:, :, None]
    qid = band_ids[:, cell_row[lane_cell]][:, None, :]
    head_of_row = np.concatenate(
        [
            np.repeat(np.arange(HEADS), MAIN),
            np.repeat(np.arange(HEADS), REST),
            np.full(128 - HEADS * REST, -1),
        ]
    )
    mask = jnp.asarray(head_of_row[:, None] == np.arange(C)[None, :] // HEAD, BF)
    wq, wk, wv = (w_qkv[:, C * i : C * (i + 1)] for i in range(3))
    weights = (wq, wk, wv, w_proj, w_up, wq.T, wk.T, wv.T, w_proj.T, w_up.T, w_down.T)

    def whole(shape):
        zeros = (0,) * len(shape)
        return pl.BlockSpec(shape, lambda p, w: zeros)

    field = pl.BlockSpec((WLEV, WLAT, cols, C), lambda p, w: (p, w, 0, 0))
    biases = pl.BlockSpec((1, 1, HEADS, M, M), lambda p, w: (p, w, 0, 0, 0))
    v32 = lambda *shape: pltpu.VMEM(shape, F32)
    v16 = lambda *shape: pltpu.VMEM(shape, BF)
    return pl.pallas_call(
        block_kernel,
        grid=(blocks, bands),
        in_specs=[
            field,
            field,
            biases,
            pl.BlockSpec((1, M, 1), lambda p, w: (w, 0, 0)),
            pl.BlockSpec((1, 1, LANES), lambda p, w: (w, 0, 0)),
            whole(gains.shape),
            whole(mask.shape),
        ]
        + [whole(w.shape) for w in weights],
        out_specs=[field, biases, whole((4096, 128))],
        out_shape=[
            jax.ShapeDtypeStruct(tokens.shape, BF),
            jax.ShapeDtypeStruct(bias.shape, BF),
            jax.ShapeDtypeStruct((4096, 128), BF),
        ],
        scratch_shapes=[
            v32(rows, C), v32(rows, C), v32(rows, C), v32(rows, C), v16(rows, C), v16(rows, C),
            v32(rows, C), v32(rows, 1), v32(M, LANES), v32(M, LANES),
            v32(M, LANES), v16(M, LANES), v16(M, LANES), v16(LANES, C), v16(LANES, C),
            v16(rows, C), v16(rows, C), v16(rows, C), v16(rows, C), v16(rows, C),
            v16(rows, C), v16(rows, FF), v16(rows, FF), v32(rows, C), v32(18, C, 128), v32(16, C),
        ],
        compiler_params=pltpu.CompilerParams(
            vmem_limit_bytes=48 * 1024 * 1024,
            dimension_semantics=("arbitrary", "arbitrary"),
        ),
        cost_estimate=pl.CostEstimate(flops=14_000_000_000, bytes_accessed=10_000_000, transcendentals=5_000_000),
        name="window_block",
    )(tokens, cotangent, bias, kid, qid, gains, mask, *weights)


def unpack_kernel(scale, in_ref, qkv_ref, proj_ref, up_ref, down_ref, gains_ref):
    def tile(i):
        return in_ref[C * i : C * (i + 1), :].astype(F32) * scale

    half_qk, half_vp = tile(2), tile(5)
    qkv_ref[...] = jnp.concatenate(
        [tile(0), half_qk[:, :64], tile(1), half_qk[:, 64:], tile(3), half_vp[:, :64]], axis=1
    )
    proj_ref[...] = jnp.concatenate([tile(4), half_vp[:, 64:]], axis=1)
    for i in range(FF // 128):
        up_ref[:, 128 * i : 128 * (i + 1)] = tile(6 + i)
        down_ref[128 * i : 128 * (i + 1), :] = tile(12 + i).T
    wide = in_ref[18 * C : 18 * C + 16, :].astype(F32) * scale
    gains_ref[...] = jnp.concatenate([wide[0:2, :], wide[8:10, :64]], axis=1)


def unpack(packed, scale):
    shapes = ((C, 3 * C), (C, C), (C, FF), (FF, C), (2, C))
    return pl.pallas_call(
        functools.partial(unpack_kernel, scale),
        out_shape=[jax.ShapeDtypeStruct(s, F32) for s in shapes],
        compiler_params=pltpu.CompilerParams(vmem_limit_bytes=32 * 1024 * 1024),
        name="unpack_sums",
    )(packed)


def local(tokens, cotangent, region_ids, norm_gains, w_qkv, w_proj, w_up, w_down, earth_bias):
    levels, nrows, cols, channels = tokens.shape
    half_lat = WLAT // 2
    half_lon = WLON // 2
    both = ("lon", "lat")
    devices = lax.axis_size("lon") * lax.axis_size("lat")

    pair = jnp.stack([tokens, cotangent])
    ids_in = perm(region_ids[:half_lat], "lat", -1)
    row_ids = jnp.concatenate([region_ids[half_lat:], ids_in], axis=0)
    rows_in = perm(pair[:, :, :half_lat], "lat", -1)
    pair = jnp.concatenate([pair[:, :, half_lat:], rows_in], axis=2)
    cols_in = perm(pair[:, :, :, :half_lon], "lon", -1)
    pair = jnp.concatenate([pair[:, :, :, half_lon:], cols_in], axis=3)

    grad_rolled, grad_bias, packed = run_block(
        pair[0], pair[1], earth_bias, row_ids, norm_gains, w_qkv, w_proj, w_up, w_down
    )

    cols_back = perm(grad_rolled[:, :, -half_lon:], "lon", 1)
    grad_rolled = jnp.concatenate([cols_back, grad_rolled[:, :, :-half_lon]], axis=2)
    rows_back = perm(grad_rolled[:, -half_lat:], "lat", 1)
    grad_tokens = jnp.concatenate([rows_back, grad_rolled[:, :-half_lat]], axis=1)

    pieces = lax.all_to_all(packed.reshape(devices, -1, 128), both, 0, 0, tiled=True)
    summed = jnp.sum(pieces.astype(F32), axis=0).astype(BF)
    spread = jnp.broadcast_to(summed[None], (devices,) + summed.shape)
    packed = lax.all_to_all(spread, both, 0, 0, tiled=True).reshape(-1, 128)
    cell_count = levels * nrows * cols * devices
    grads = unpack(packed, 1.0 / math.sqrt(cell_count))

    lons = lax.axis_size("lon")
    blocks, bands = earth_bias.shape[:2]
    share = M // lons
    by_lon = grad_bias.reshape(blocks * bands * HEADS, lons, share, M).transpose(1, 0, 2, 3)
    shares = lax.all_to_all(by_lon.reshape(lons, -1, M), "lon", 0, 0, tiled=True)
    bias_total = jnp.sum(shares.astype(F32), axis=0).reshape(blocks, bands, HEADS, share, M)
    return (grad_tokens, *grads, bias_total)


def solution(mesh):
    placed = (
        P(None, "lat", "lon", None),
        P(None, "lat", "lon", None),
        P("lat"),
        P(),
        P(),
        P(),
        P(),
        P(),
        P(None, "lat", None, None, None),
    )
    return jax.shard_map(
        local,
        mesh=mesh,
        in_specs=placed,
        out_specs=(
            P(None, "lat", "lon", None),
            P(),
            P(),
            P(),
            P(),
            P(),
            P(None, "lat", None, "lon", None),
        ),
        check_vma=False,
    )
```

```python
import functools
import math

import jax
import jax.numpy as jnp
import numpy as np
from jax import lax
from jax.experimental import pallas as pl
from jax.experimental.pallas import tpu as pltpu
from jax.sharding import PartitionSpec as P

HEADS = 6
HEAD = 32
WLEV = 2
WLAT = 6
WLON = 12
C = HEADS * HEAD
FF = 4 * C
M = WLEV * WLAT * WLON
MAIN = 128
REST = M - MAIN
LANES = (HEADS + 1) * 128
SLABS = WLEV * WLAT

BF = jnp.bfloat16
F32 = jnp.float32
epsilon = 1e-05
inv_root_two = 0.7071067811865476
inv_root_tau = 0.3989422804014327


def perm(value, axis, steps):
    count = lax.axis_size(axis)
    pairs = [(source, (source + steps) % count) for source in range(count)]
    return lax.ppermute(value, axis, pairs)


def dot(left, right):
    return jnp.dot(left, right, preferred_element_type=F32)


def dot_nt(left, right):
    return lax.dot_general(left, right, (((1,), (1,)), ((), ())), preferred_element_type=F32)


def dot_tn(left, right):
    return lax.dot_general(left, right, (((0,), (0,)), ((), ())), preferred_element_type=F32)


def normalize(values):
    centred = values - jnp.mean(values, axis=-1, keepdims=True)
    inverse = lax.rsqrt(jnp.mean(centred * centred, axis=-1, keepdims=True) + epsilon)
    return centred * inverse, inverse


def norm_back(normed, inverse, gain_row, upstream):
    scaled = upstream * gain_row
    return inverse * (
        scaled
        - jnp.mean(scaled, axis=-1, keepdims=True)
        - normed * jnp.mean(scaled * normed, axis=-1, keepdims=True)
    )


def gelu_parts(u):
    bell = jnp.exp2(u * u * (-0.5 * math.log2(math.e)))
    under = 1.0 + jnp.abs(u) * (0.3275911 * inv_root_two)
    t = pl.reciprocal(under, approx=True)
    t = t * (2.0 - under * t)
    tail = t * (
        0.5 * 0.254829592
        + t
        * (
            0.5 * -0.284496736
            + t * (0.5 * 1.421413741 + t * (0.5 * -1.453152027 + t * (0.5 * 1.061405429)))
        )
    )
    tail = tail * bell
    cdf = jnp.where(u >= 0.0, 1.0 - tail, tail)
    return cdf, cdf + u * (bell * inv_root_tau)


CHUNKS = ((0, 256), (256, 512), (512, 768), (768, 896))


def spread_heads(rows, mask):
    first, last = rows[:MAIN], rows[MAIN:]
    return jnp.concatenate([first] * HEADS + [last] * 8, axis=0) * mask


def per_query(weights_ref, right, right_t, rest_mask):
    parts = []
    for e in range(HEADS):
        parts.append(
            dot(
                right_t[HEAD * e : HEAD * (e + 1), :],
                weights_ref[:, 128 * e : 128 * (e + 1)],
            )
        )
        if e % 2:
            yield None
    first = jnp.concatenate(parts, axis=0).T
    yield None
    last = dot_tn(weights_ref[:, HEADS * 128 :], right) * rest_mask
    total = last[0:REST]
    for e in range(1, HEADS):
        total = total + last[REST * e : REST * (e + 1)]
    yield jnp.concatenate([first, total], axis=0)


def in_turn(*streams):
    streams = [[0, count, pieces] for count, pieces in streams]
    while streams:
        stream = min(streams, key=lambda entry: entry[0] / entry[1])
        stream[0] += 1
        if next(stream[2], streams) is streams:
            streams.remove(stream)


INNER = ((0, 0), (0, 1), (0, 2))
EDGE = ((0, 3), (1, 0), (1, 1), (1, 2), (1, 3))
STATE = ("ds", "q", "k", "h", "dv", "xb", "dy")
HALF_LAT = WLAT // 2
HALF_LON = WLON // 2
HALO_COLS = 8


class Refs:
    pass


def named(names, refs):
    r = Refs()
    for name, ref in zip(names, refs):
        setattr(r, name, ref)
    return r


def window_pieces(w, n, local_rows, cols):
    for a in range(WLEV):
        for b in range(WLAT):
            slab = (a * WLAT + b) * WLON
            i = HALF_LAT + w * WLAT + b
            j = HALF_LON + n * WLON
            own = min(WLON, cols - j)
            if i < local_rows:
                yield "own", None, (a * local_rows + i) * cols + j, own, slab
                if own < WLON:
                    yield "lon", a * local_rows + i, 0, WLON - own, slab + own
            else:
                i = i - local_rows
                yield "lat", None, (a * HALF_LAT + i) * cols + j, own, slab
                if own < WLON:
                    yield "corner", a * HALF_LAT + i, 0, WLON - own, slab + own


def forward_kernel(names, places, cols, *refs):
    r = named(names, refs)
    edge = hasattr(r, "halo_lat")
    bands = sorted({w for w, n in places})
    step = pl.program_id(0)
    last_step = pl.num_programs(0) - 1

    @pl.when(step == 0)
    def _():
        if edge:
            r.acc[...] = r.acc_in[...]
            r.proj[...] = r.proj_in[...]
            r.share32[...] = jnp.zeros_like(r.share32)
        else:
            r.acc[...] = jnp.zeros_like(r.acc)
            r.proj[...] = jnp.zeros_like(r.proj)
        r.wq[...] = r.wqkv[:, 0:C]
        r.wk[...] = r.wqkv[:, C : 2 * C]
        r.wv[...] = r.wqkv[:, 2 * C : 3 * C]

    gain0 = r.gains[0:1, :]
    gain1 = r.gains[1:2, :]
    scaling = float(HEAD) ** -0.5

    local_rows = r.tok.shape[1]
    for at, ref in enumerate((r.tok, r.cot)):
        r.own32[at] = ref[...].reshape(WLEV * local_rows * cols, C).astype(F32)
        if edge:
            r.lat32[at] = r.halo_lat[at].reshape(WLEV * HALF_LAT * cols, C).astype(F32)
            for a in range(WLEV):
                for i in range(local_rows):
                    r.lon32[at, a * local_rows + i] = r.halo_lon[at, a, i].astype(F32)
                for i in range(HALF_LAT):
                    r.corner32[at, a * HALF_LAT + i] = r.halo_corner[at, a, i].astype(F32)

    def bias_rows(at, w):
        kid = jnp.zeros((M, 1), jnp.int32)
        qid = jnp.zeros((1, LANES), jnp.int32)
        for b in range(WLAT):
            kid = jnp.where(r.krow[...] == b, r.ids[w * WLAT + b], kid)
            qid = jnp.where(r.qrow[...] == b, r.ids[w * WLAT + b], qid)
        rest_pad = jnp.zeros((128 - HEADS * REST, M), F32)
        rest = jnp.concatenate([r.bias[0, at, e, MAIN:, :] for e in range(HEADS)] + [rest_pad], axis=0)
        for e in range(HEADS + 1):
            block = r.bias[0, at, e, :MAIN, :] if e < HEADS else rest
            lanes = slice(128 * e, 128 * (e + 1))
            r.biast[at, :, lanes] = jnp.where(kid == qid[:, lanes], block.T, -1e30)
            yield None
        if edge and w == 0:
            r.gbt[at] = r.gbt_in[0]
        else:
            r.gbt[at] = jnp.zeros((M, LANES), F32)
        yield None

    rest_mask = r.mask[HEADS * 128 :, :].astype(F32)

    def front(t):
        w, n = places[t]
        band = bands.index(w)
        here = slice(t * M, (t + 1) * M)
        for at, to in ((0, r.x), (1, r.c)):
            for name, lead, start, length, slab in window_pieces(w, n, local_rows, cols):
                source = getattr(r, name + "32")
                index = (at,) if lead is None else (at, lead)
                to[t * M + slab : t * M + slab + length, :] = source[index + (slice(start, start + length),)]
            yield None
        x = r.x[here, :]
        r.xb[0, t] = x.astype(BF)
        h = (normalize(x)[0] * gain0).astype(BF)
        r.h[0, t] = h
        yield None
        q = (dot(h, r.wq[...]) * scaling).astype(BF)
        r.q[0, t] = q
        r.qbd[t] = spread_heads(q, r.mask[...])
        yield None
        r.k[0, t] = dot(h, r.wk[...]).astype(BF)
        yield None
        v32 = dot(h, r.wv[...])
        r.v[here, :] = v32.astype(BF)
        vt = v32.T.astype(BF)
        yield None
        for lo, hi in CHUNKS:
            scores = dot_nt(r.k[0, t], r.qbd[t, lo:hi, :]) + r.biast[band, :, lo:hi]
            powers = jnp.exp(scores - jnp.max(scores, axis=0, keepdims=True))
            weights = powers * (1.0 / jnp.sum(powers, axis=0, keepdims=True))
            r.p[t, :, lo:hi] = weights
            r.pb[t, :, lo:hi] = weights.astype(BF)
            yield None
        for o in per_query(r.pb.at[t], r.v[here, :], vt, rest_mask):
            yield None
        o = o.astype(BF)
        r.o[here, :] = o
        y = r.x[here, :] + dot(o, r.wp[...]).astype(BF).astype(F32)
        yield None
        n2, r2 = normalize(y)
        r.n2[here, :] = n2
        r.r2[here, :] = r2
        r.g[here, :] = (n2 * gain1).astype(BF)
        r.cb[here, :] = r.c[here, :].astype(BF)
        yield None

    def middle(t):
        here = slice(t * M, (t + 1) * M)
        for lo in range(0, FF, 256):
            part = slice(lo, lo + 256)
            u = dot(r.g[here, :], r.wup[:, part])
            cdf, slope = gelu_parts(u)
            r.act[here, part] = (u * cdf).astype(BF)
            yield None
            r.du[here, part] = (dot_nt(r.cb[here, :], r.wdown[part, :]) * slope).astype(BF)
            yield None

    def back(t):
        w, n = places[t]
        band = bands.index(w)
        here = slice(t * M, (t + 1) * M)
        dg = dot_nt(r.du[here, :], r.wup[...])
        yield None
        dy = r.c[here, :] + norm_back(r.n2[here, :], r.r2[here, :], gain1, dg)
        r.dy[0, t] = dy
        dys = dy.astype(BF)
        r.dys[here, :] = dys
        yield None
        do = dot_nt(dys, r.wp[...]).astype(BF)
        r.dobd[t] = spread_heads(do, r.mask[...])
        yield None
        for lo, hi in CHUNKS:
            weights = r.p[t, :, lo:hi]
            dp = dot_nt(r.v[here, :], r.dobd[t, lo:hi, :]) * weights
            ds = dp - weights * jnp.sum(dp, axis=0, keepdims=True)
            r.gbt[band, :, lo:hi] += ds
            r.ds[0, t, :, lo:hi] = ds.astype(BF)
            yield None
        r.dv[0, t] = dot(r.pb[t], r.dobd[t]).astype(BF)
        yield None

    def dense_sums():
        for first, left, right in ((0, r.g, r.du), (6, r.cb, r.act)):
            left_t = left[...].T
            for lo in range(0, FF, 256):
                part = dot(left_t, right[:, lo : lo + 256])
                r.acc[first + lo // 128] += part[:, :128]
                r.acc[first + lo // 128 + 1] += part[:, 128:]
                yield None

    def proj_sum():
        r.proj[...] += dot_tn(r.o[...], r.dys[...])
        yield None

    def share_bias(at):
        share = M // r.share_out.shape[0]
        gbt = r.gbt.at[at]
        last = gbt[:, HEADS * 128 :].T
        for e in range(HEADS):
            r.bias32[at, M * e : M * e + MAIN, :] = gbt[:, 128 * e : 128 * (e + 1)].T[:, :MAIN]
            r.bias32[at, M * e + MAIN : M * (e + 1), :] = last[REST * e : REST * (e + 1), :MAIN]
            yield None
        far = jnp.concatenate(
            [gbt[MAIN:, 128 * e : 128 * (e + 1)] for e in range(HEADS)]
            + [jnp.zeros((128 - HEADS * REST, 128), F32)],
            axis=0,
        )
        r.bias32[at, M * HEADS : M * HEADS + MAIN, :] = far.T
        r.bias32[at, M * HEADS + MAIN : M * (HEADS + 1), :] = jnp.concatenate(
            [last[REST * e : REST * (e + 1), MAIN:] for e in range(HEADS)]
            + [jnp.zeros((REST, 128 - HEADS * REST), F32)],
            axis=1,
        )
        yield None
        for d in range(r.share_out.shape[0]):
            for e in range(HEADS + 1):
                r.share32[at, d, share * e : share * (e + 1), :] = r.bias32[
                    at, M * e + share * d : M * e + share * (d + 1), :
                ]
            r.share_out[d, 0, at] = r.share32[at, d].astype(BF)
            yield None

    count = len(places)
    for slot in range(count + 2):
        streams = []
        if slot == 0:
            in_turn((8, bias_rows(0, bands[0])))
            streams += [(8, bias_rows(at, bands[at])) for at in range(1, len(bands))]
        if slot < count:
            streams.append((16, front(slot)))
        if 0 <= slot - 1 < count:
            streams.append((6, middle(slot - 1)))
        if 0 <= slot - 2 < count:
            streams.append((9, back(slot - 2)))
        if slot == count + 1:
            streams.append((6, dense_sums()))
        in_turn(*streams)
    ends = [(1, proj_sum())]
    if edge:
        ends += [(15, share_bias(at)) for at in range(len(bands))]
    in_turn(*ends)

    if not edge:
        r.gbt_out[0] = r.gbt[0]

    @pl.when(step == last_step)
    def _():
        r.acc_out[...] = r.acc[...]
        r.proj_out[...] = r.proj[...]


def whole(shape):
    zeros = (0,) * len(shape)
    return pl.BlockSpec(tuple(shape), lambda p: zeros)


def by_level(shape, at, blocks=2):
    block = list(shape)
    block[at] = shape[at] // blocks
    return pl.BlockSpec(tuple(block), lambda p: tuple(p if i == at else 0 for i in range(len(shape))))


def call(kernel, blocks, ins, outs, scratch, name, share_of, limit, *fixed):
    names = [i[0] for i in ins] + [o[0] for o in outs] + [s[0] for s in scratch]
    return pl.pallas_call(
        functools.partial(kernel, names, *fixed),
        grid=(blocks,),
        in_specs=[i[2] for i in ins],
        out_specs=[o[3] for o in outs],
        out_shape=[jax.ShapeDtypeStruct(tuple(o[1]), o[2]) for o in outs],
        scratch_shapes=[pltpu.VMEM(tuple(s[1]), s[2]) for s in scratch],
        compiler_params=pltpu.CompilerParams(
            vmem_limit_bytes=limit * 1024 * 1024,
            dimension_semantics=("arbitrary",),
        ),
        cost_estimate=pl.CostEstimate(
            flops=int(14e9 * share_of), bytes_accessed=int(10e6 * share_of), transcendentals=int(5e6 * share_of)
        ),
        name=name,
    )(*[i[1] for i in ins])


def head_mask():
    head_of_row = np.concatenate(
        [
            np.repeat(np.arange(HEADS), MAIN),
            np.repeat(np.arange(HEADS), REST),
            np.full(128 - HEADS * REST, -1),
        ]
    )
    return jnp.asarray(head_of_row[:, None] == np.arange(C)[None, :] // HEAD, BF)


def run_forward(places, tokens, cotangent, bias, row_ids, weights, halos=None, before=None, lons=8):
    levels, local_rows, cols, channels = tokens.shape
    blocks = levels // WLEV
    count = len(places)
    rows = count * M
    bands = len({w for w, n in places})
    cell_row = (np.arange(M) // WLON % WLAT).astype(np.int32)
    rest = np.concatenate([np.tile(np.arange(MAIN, M), HEADS), np.zeros(128 - HEADS * REST, int)])
    lane_cell = np.concatenate([np.tile(np.arange(MAIN), HEADS), rest])
    edge = halos is not None
    ins = [
        ("tok", tokens, by_level(tokens.shape, 0)),
        ("cot", cotangent, by_level(tokens.shape, 0)),
        ("bias", bias, pl.BlockSpec((1, bands, HEADS, M, M), lambda p: (p, 0, 0, 0, 0))),
        ("ids", row_ids, pl.BlockSpec(memory_space=pltpu.SMEM)),
        ("krow", jnp.asarray(cell_row[:, None]), whole((M, 1))),
        ("qrow", jnp.asarray(cell_row[lane_cell][None, :]), whole((1, LANES))),
        ("mask", head_mask(), whole((LANES, C))),
    ] + [(name, w, whole(w.shape)) for name, w in weights.items()]
    flat = WLEV * local_rows * cols
    acc = (12, C, 128)
    scratch = [
        ("own32", (2, flat, C), F32),
        ("x", (rows, C), F32),
        ("c", (rows, C), F32),
        ("n2", (rows, C), F32),
        ("r2", (rows, 1), F32),
        ("biast", (bands, M, LANES), F32),
        ("gbt", (bands, M, LANES), F32),
        ("p", (count, M, LANES), F32),
        ("pb", (count, M, LANES), BF),
        ("qbd", (count, LANES, C), BF),
        ("dobd", (count, LANES, C), BF),
        ("acc", acc, F32),
        ("proj", (C, C), F32),
        ("act", (rows, FF), BF),
        ("du", (rows, FF), BF),
    ] + [(name, (rows, C), BF) for name in ("v", "o", "g", "cb", "dys")]
    scratch += [(name, (C, C), BF) for name in ("wq", "wk", "wv")]
    outs = []
    for name in STATE:
        shape = (blocks, count, M, LANES if name == "ds" else C)
        outs.append((name, shape, F32 if name == "dy" else BF, by_level(shape, 0)))
    outs += [("acc_out", acc, F32, whole(acc)), ("proj_out", (C, C), F32, whole((C, C)))]
    if edge:
        for name, value in zip(("halo_lat", "halo_lon", "halo_corner"), halos):
            ins.append((name, value, by_level(value.shape, 1)))
        for name, value in zip(("acc_in", "proj_in", "gbt_in"), before):
            ins.append((name, value, by_level(value.shape, 0) if name == "gbt_in" else whole(value.shape)))
        share = (lons, blocks, bands, 128, 128)
        outs.append(("share_out", share, BF, by_level(share, 1)))
        scratch += [
            ("lat32", (2, WLEV * HALF_LAT * cols, C), F32),
            ("lon32", (2, WLEV * local_rows, HALO_COLS, C), F32),
            ("corner32", (2, WLEV * HALF_LAT, HALO_COLS, C), F32),
            ("bias32", (bands, M * (HEADS + 1), 128), F32),
            ("share32", (bands, lons, 128, 128), F32),
        ]
    else:
        outs.append(("gbt_out", (blocks, M, LANES), F32, by_level((blocks, M, LANES), 0)))
    name = "edge_windows" if edge else "inner_windows"
    got = call(forward_kernel, blocks, ins, outs, scratch, name, count * blocks / 20, 60, places, cols)
    return got[: len(STATE)], got[len(STATE) :]


def attention_kernel(names, parts, *refs):
    r = named(names, refs)
    step = pl.program_id(0)
    last_step = pl.num_programs(0) - 1
    scaling = float(HEAD) ** -0.5
    rest_mask = r.mask[HEADS * 128 :, :].astype(F32)

    @pl.when(step == 0)
    def _():
        r.acc[...] = jnp.zeros_like(r.acc)

    def window(at, part, t):
        here = slice(at * M, (at + 1) * M)
        get = lambda name: getattr(r, name + str(part)).at[0, t]
        r.h[here, :] = get("h")[...]
        r.dv[here, :] = get("dv")[...]
        r.qbd[at % 4] = spread_heads(get("q")[...], r.mask[...])
        yield None
        k = get("k")[...]
        kt = k.astype(F32).T.astype(BF)
        yield None
        dk = dot(get("ds")[...], r.qbd[at % 4]).astype(BF)
        r.dk[here, :] = dk
        getattr(r, "dk_out" + str(part))[0, t] = dk
        yield None
        for dq in per_query(get("ds"), k, kt, rest_mask):
            yield None
        dq = (dq * scaling).astype(BF)
        r.dq[here, :] = dq
        getattr(r, "dq_out" + str(part))[0, t] = dq
        yield None

    order = [(part, t) for part, count in enumerate(parts) for t in range(count)]
    for at in range(0, len(order), 2):
        in_turn(*[(9, window(at + i, *order[at + i])) for i in range(2)])
    ht = r.h[...].T
    for i, right in enumerate((r.dq, r.dk, r.dv)):
        r.acc[i] += dot(ht, right[...])

    @pl.when(step == last_step)
    def _():
        per = r.pack_out.shape[1]

        def put(i, tile):
            r.pack_out[C // per * i : C // per * (i + 1)] = tile.astype(BF).reshape(C // per, per, 128)

        small = (r.acc[0], r.acc[1], r.acc[2], r.proj[...])
        for i in range(2):
            one, two = small[2 * i], small[2 * i + 1]
            put(3 * i, one[:, :128])
            put(3 * i + 1, two[:, :128])
            put(3 * i + 2, jnp.concatenate([one[:, 128:], two[:, 128:]], axis=1))
        for i in range(12):
            put(6 + i, r.dense[i])
        first = jnp.zeros((C, C), F32)
        for i in range(3):
            first = first + r.acc[i] * r.wqkv[:, C * i : C * (i + 1)].astype(F32)
        second = jnp.zeros((C, 128), F32)
        for i in range(6):
            second = second + r.dense[i] * r.wup[:, 128 * i : 128 * (i + 1)].astype(F32)
        sums = [jnp.sum(part.T, axis=0, keepdims=True) for part in (first, second)]
        gains = jnp.concatenate([sums[0] / r.gains[0:1, :], sums[1] / r.gains[1:2, :], jnp.zeros((6, C), F32)], axis=0)
        wide = jnp.concatenate(
            [gains[:, :128], jnp.concatenate([gains[:, 128:], jnp.zeros((8, 64), F32)], axis=1)],
            axis=0,
        )
        r.pack_out[18 * C // per, 0:16, :] = wide.astype(BF)


def run_attention(states, sums, weights, devices):
    ins, outs = [], []
    blocks = states[0][0].shape[0]
    parts = [state[0].shape[1] for state in states]
    for part, state in enumerate(states):
        for name, value in zip(STATE, state):
            if name not in ("xb", "dy"):
                ins.append((name + str(part), value, by_level(value.shape, 0)))
    mask = head_mask()
    ins += [
        ("dense", sums[0], whole(sums[0].shape)),
        ("proj", sums[1], whole(sums[1].shape)),
        ("mask", mask, whole(mask.shape)),
    ] + [(name, weights[name], whole(weights[name].shape)) for name in ("wqkv", "wup", "gains")]
    for part, count in enumerate(parts):
        shape = (blocks, count, M, C)
        for name in ("dq_out", "dk_out"):
            outs.append((name + str(part), shape, BF, by_level(shape, 0)))
    pack = (devices, 4096 // devices, 128)
    outs.append(("pack_out", pack, BF, whole(pack)))
    rows = sum(parts) * M
    scratch = [("acc", (3, C, C), F32), ("qbd", (4, LANES, C), BF)]
    scratch += [(name, (rows, C), BF) for name in ("h", "dq", "dk", "dv")]
    got = call(attention_kernel, blocks, ins, outs, scratch, "query_key_grads", 0.3, 60, parts)
    return [got[0:2], got[2:4]], got[-1]


def finish_kernel(names, parts, cols, *refs):
    r = named(names, refs)
    local_rows = r.gt_out.shape[1]
    gain0 = r.gains[0:1, :]

    @pl.when(pl.program_id(0) == 0)
    def _():
        for i in range(3):
            r.w[i] = r.wqkv[:, C * i : C * (i + 1)]
        for name in ("own32", "lat32", "lon32", "corner32"):
            ref = getattr(r, name)
            ref[...] = jnp.zeros_like(ref)

    def window(at, part, t, place):
        get = lambda name: getattr(r, name + str(part)).at[0, t]
        dh = dot_nt(get("dq")[...], r.w[0]) + dot_nt(get("dk")[...], r.w[1]) + dot_nt(get("dv")[...], r.w[2])
        dh = dh.astype(BF).astype(F32)
        yield None
        n1, r1 = normalize(get("xb")[...].astype(F32))
        yield None
        r.gt[at] = get("dy")[...] + norm_back(n1, r1, gain0, dh)
        yield None
        for name, lead, start, length, slab in window_pieces(*place, local_rows, cols):
            target = getattr(r, name + "32")
            index = () if lead is None else (lead,)
            target[index + (slice(start, start + length),)] = r.gt[at, slab : slab + length, :]
        yield None

    order = [(part, t, place) for part, places in enumerate(parts) for t, place in enumerate(places)]
    for at in range(0, len(order), 2):
        in_turn(*[(4, window(at + i, *order[at + i])) for i in range(2)])
    r.gt_out[...] = r.own32[...].astype(BF).reshape(r.gt_out.shape)
    r.lat_out[...] = r.lat32[...].astype(BF).reshape(r.lat_out.shape)
    for a in range(WLEV):
        for i in range(local_rows):
            r.lon_out[a, i] = r.lon32[a * local_rows + i].astype(BF)
        for i in range(HALF_LAT):
            r.corner_out[a, i] = r.corner32[a * HALF_LAT + i].astype(BF)


def run_finish(parts, states, grads, weights, shape):
    levels, local_rows, cols, channels = shape
    blocks = levels // WLEV
    ins = []
    for part, (state, grad) in enumerate(zip(states, grads)):
        for name in ("dv", "xb", "dy"):
            value = state[STATE.index(name)]
            ins.append((name + str(part), value, by_level(value.shape, 0)))
        for name, value in zip(("dq", "dk"), grad):
            ins.append((name + str(part), value, by_level(value.shape, 0)))
    ins += [(name, weights[name], whole(weights[name].shape)) for name in ("wqkv", "gains")]
    outs = []
    for name, out in (
        ("gt_out", shape),
        ("lat_out", (levels, HALF_LAT, cols, C)),
        ("lon_out", (levels, local_rows, HALO_COLS, C)),
        ("corner_out", (levels, HALF_LAT, HALO_COLS, C)),
    ):
        outs.append((name, out, BF, by_level(out, 0)))
    count = sum(len(places) for places in parts)
    scratch = [
        ("w", (3, C, C), BF),
        ("gt", (count, M, C), F32),
        ("own32", (WLEV * local_rows * cols, C), F32),
        ("lat32", (WLEV * HALF_LAT * cols, C), F32),
        ("lon32", (WLEV * local_rows, HALO_COLS, C), F32),
        ("corner32", (WLEV * HALF_LAT, HALO_COLS, C), F32),
    ]
    return call(finish_kernel, blocks, ins, outs, scratch, "token_grads", 0.1, 60, parts, cols)


def assemble_kernel(own_ref, lat_ref, lon_ref, corner_ref, out_ref):
    levels, local_rows, cols, channels = out_ref.shape
    keep = lax.broadcasted_iota(jnp.int32, (16, C), 0) >= HALF_LON
    pad = jnp.zeros((16 - HALO_COLS, C), F32)
    for a in range(levels):
        for i in range(local_rows):
            row = own_ref.at[a, i] if i >= HALF_LAT else lat_ref.at[a, i]
            left = lon_ref[a, i] if i >= HALF_LAT else corner_ref[a, i]
            left = jnp.concatenate([left.astype(F32), pad], axis=0)
            out_ref[a, i, 0:16, :] = jnp.where(keep, row[0:16, :].astype(F32), left).astype(BF)
            out_ref[a, i, 16:, :] = row[16:, :]


def assemble(own, *received):
    return pl.pallas_call(
        assemble_kernel,
        out_shape=jax.ShapeDtypeStruct(own.shape, BF),
        compiler_params=pltpu.CompilerParams(vmem_limit_bytes=32 * 1024 * 1024),
        name="assemble",
    )(own, *received)


def sum_kernel(in_ref, out_ref):
    total = jnp.sum(in_ref[...].astype(F32), axis=0, keepdims=True).astype(BF)
    out_ref[...] = jnp.broadcast_to(total, out_ref.shape)


def sum_pieces(pieces):
    return pl.pallas_call(
        sum_kernel,
        out_shape=jax.ShapeDtypeStruct(pieces.shape, BF),
        compiler_params=pltpu.CompilerParams(vmem_limit_bytes=32 * 1024 * 1024),
        name="sum_pieces",
    )(pieces)


def sum_bias_kernel(in_ref, out_ref):
    blocks, bands, heads, share, cells = out_ref.shape
    for p in range(blocks):
        for w in range(bands):
            total = jnp.sum(in_ref[:, p, w].astype(F32), axis=0)
            far = total[share * heads : share * (heads + 1)]
            for e in range(heads):
                near = total[share * e : share * (e + 1)]
                out_ref[p, w, e] = jnp.concatenate([near, far[:, REST * e : REST * (e + 1)]], axis=1)


def sum_bias(pieces, shape):
    return pl.pallas_call(
        sum_bias_kernel,
        out_shape=jax.ShapeDtypeStruct(shape, F32),
        compiler_params=pltpu.CompilerParams(vmem_limit_bytes=32 * 1024 * 1024),
        name="sum_bias",
    )(pieces)


def unpack_kernel(scale, in_ref, qkv_ref, proj_ref, up_ref, down_ref, gains_ref):
    def tile(i):
        return in_ref[C * i : C * (i + 1), :].astype(F32) * scale

    half_qk, half_vp = tile(2), tile(5)
    qkv_ref[...] = jnp.concatenate(
        [tile(0), half_qk[:, :64], tile(1), half_qk[:, 64:], tile(3), half_vp[:, :64]], axis=1
    )
    proj_ref[...] = jnp.concatenate([tile(4), half_vp[:, 64:]], axis=1)
    for i in range(FF // 128):
        up_ref[:, 128 * i : 128 * (i + 1)] = tile(6 + i)
        down_ref[128 * i : 128 * (i + 1), :] = tile(12 + i).T
    wide = in_ref[18 * C : 18 * C + 16, :].astype(F32) * scale
    gains_ref[...] = jnp.concatenate([wide[0:2, :], wide[8:10, :64]], axis=1)


def unpack(packed, scale):
    shapes = ((C, 3 * C), (C, C), (C, FF), (FF, C), (2, C))
    return pl.pallas_call(
        functools.partial(unpack_kernel, scale),
        out_shape=[jax.ShapeDtypeStruct(s, F32) for s in shapes],
        compiler_params=pltpu.CompilerParams(vmem_limit_bytes=60 * 1024 * 1024),
        name="unpack_sums",
    )(packed)


def local(tokens, cotangent, region_ids, norm_gains, w_qkv, w_proj, w_up, w_down, earth_bias):
    levels, nrows, cols, channels = tokens.shape
    both = ("lon", "lat")
    lons, lats = lax.axis_size("lon"), lax.axis_size("lat")
    devices = lons * lats

    def corner_perm(value, steps):
        pairs = [
            (a * lats + b, (a + steps) % lons * lats + (b + steps) % lats)
            for a in range(lons)
            for b in range(lats)
        ]
        return lax.ppermute(value, both, pairs)

    def both_fields(cut):
        return jnp.stack([cut(tokens), cut(cotangent)])

    halos = (
        perm(both_fields(lambda f: f[:, :HALF_LAT]), "lat", -1),
        perm(both_fields(lambda f: f[:, :, :HALO_COLS]), "lon", -1),
        corner_perm(both_fields(lambda f: f[:, :HALF_LAT, :HALO_COLS]), -1),
    )
    ids_in = perm(region_ids[:HALF_LAT], "lat", -1)
    row_ids = jnp.concatenate([region_ids[HALF_LAT:], ids_in], axis=0)

    weights = {"wqkv": w_qkv, "wp": w_proj, "wup": w_up, "wdown": w_down, "gains": norm_gains}
    inner, sums = run_forward(INNER, tokens, cotangent, earth_bias, region_ids[HALF_LAT:], weights)
    edge, sums = run_forward(EDGE, tokens, cotangent, earth_bias, row_ids, weights, halos, sums, lons)

    shares = lax.all_to_all(sums[2], "lon", 0, 0, tiled=True)
    states = (inner, edge)
    grads, packed = run_attention(states, sums, weights, devices)
    packed, shares = lax.optimization_barrier((packed, shares))
    pieces = lax.all_to_all(packed, both, 0, 0, tiled=True)
    own, *sent = run_finish((INNER, EDGE), states, grads, weights, tokens.shape)
    lat_in = perm(sent[0], "lat", 1)
    lon_in = perm(sent[1], "lon", 1)
    corner_in = corner_perm(sent[2], 1)
    summed, own = lax.optimization_barrier((sum_pieces(pieces), own))
    packed = lax.all_to_all(summed, both, 0, 0, tiled=True).reshape(-1, 128)
    cell_count = levels * nrows * cols * devices
    weight_grads = unpack(packed, 1.0 / math.sqrt(cell_count))
    bias_total = sum_bias(shares, earth_bias.shape[:3] + (M // lons, M))
    return (assemble(own, lat_in, lon_in, corner_in), *weight_grads, bias_total)


def solution(mesh):
    placed = (
        P(None, "lat", "lon", None),
        P(None, "lat", "lon", None),
        P("lat"),
        P(),
        P(),
        P(),
        P(),
        P(),
        P(None, "lat", None, None, None),
    )
    return jax.shard_map(
        local,
        mesh=mesh,
        in_specs=placed,
        out_specs=(
            P(None, "lat", "lon", None),
            P(),
            P(),
            P(),
            P(),
            P(),
            P(None, "lat", None, "lon", None),
        ),
        check_vma=False,
    )
```

```python
import functools
import math

import jax
import jax.numpy as jnp
import numpy as np
from jax import lax
from jax.experimental import pallas as pl
from jax.experimental.pallas import tpu as pltpu
from jax.sharding import PartitionSpec as P

HEADS = 6
HEAD = 32
WLEV = 2
WLAT = 6
WLON = 12
C = HEADS * HEAD
FF = 4 * C
M = WLEV * WLAT * WLON
MAIN = 128
REST = M - MAIN
LANES = (HEADS + 1) * 128
SLABS = WLEV * WLAT

BF = jnp.bfloat16
F32 = jnp.float32
epsilon = 1e-05
inv_root_two = 0.7071067811865476
inv_root_tau = 0.3989422804014327


def perm(value, axis, steps):
    count = lax.axis_size(axis)
    pairs = [(source, (source + steps) % count) for source in range(count)]
    return lax.ppermute(value, axis, pairs)


def dot(left, right):
    return jnp.dot(left, right, preferred_element_type=F32)


def dot_nt(left, right):
    return lax.dot_general(left, right, (((1,), (1,)), ((), ())), preferred_element_type=F32)


def dot_tn(left, right):
    return lax.dot_general(left, right, (((0,), (0,)), ((), ())), preferred_element_type=F32)


def normalize(values):
    centred = values - jnp.mean(values, axis=-1, keepdims=True)
    inverse = lax.rsqrt(jnp.mean(centred * centred, axis=-1, keepdims=True) + epsilon)
    return centred * inverse, inverse


def norm_back(normed, inverse, gain_row, upstream):
    scaled = upstream * gain_row
    return inverse * (
        scaled
        - jnp.mean(scaled, axis=-1, keepdims=True)
        - normed * jnp.mean(scaled * normed, axis=-1, keepdims=True)
    )


def gelu_parts(u):
    bell = jnp.exp2(u * u * (-0.5 * math.log2(math.e)))
    under = 1.0 + jnp.abs(u) * (0.3275911 * inv_root_two)
    t = pl.reciprocal(under, approx=True)
    tail = t * (
        0.5 * 0.254829592
        + t
        * (
            0.5 * -0.284496736
            + t * (0.5 * 1.421413741 + t * (0.5 * -1.453152027 + t * (0.5 * 1.061405429)))
        )
    )
    tail = tail * bell
    cdf = jnp.where(u >= 0.0, 1.0 - tail, tail)
    return cdf, cdf + u * (bell * inv_root_tau)


CHUNKS = ((0, 256), (256, 512), (512, 768), (768, 896))


def spread_heads(rows, mask):
    first, last = rows[:MAIN], rows[MAIN:]
    return jnp.concatenate([first] * HEADS + [last] * 8, axis=0) * mask


def per_query(weights_ref, right, right_t, rest_mask):
    parts = []
    for e in range(HEADS):
        parts.append(
            dot(
                right_t[HEAD * e : HEAD * (e + 1), :],
                weights_ref[:, 128 * e : 128 * (e + 1)],
            )
        )
        if e % 2:
            yield None
    first = jnp.concatenate(parts, axis=0).T
    yield None
    last = dot_tn(weights_ref[:, HEADS * 128 :], right) * rest_mask
    total = last[0:REST]
    for e in range(1, HEADS):
        total = total + last[REST * e : REST * (e + 1)]
    yield jnp.concatenate([first, total], axis=0)


def in_turn(*streams):
    streams = [[0, count, pieces] for count, pieces in streams]
    while streams:
        stream = min(streams, key=lambda entry: entry[0] / entry[1])
        stream[0] += 1
        if next(stream[2], streams) is streams:
            streams.remove(stream)


def chain(*streams):
    for stream in streams:
        for piece in stream:
            yield None


def run_events(events):
    tick = 0
    while events:
        for event in list(events):
            start, pieces, stream = event
            for i in range(pieces if start <= tick else 0):
                if next(stream, events) is events:
                    events.remove(event)
                    break
        tick += 1


STAGGER = 3
INNER = ((0, 0), (0, 1), (0, 2))
EDGE = ((0, 3), (1, 0), (1, 1), (1, 2), (1, 3))
STATE = ("ds", "q", "k", "h", "dv", "xb", "dy")
HALF_LAT = WLAT // 2
HALF_LON = WLON // 2
HALO_COLS = 8


class Refs:
    pass


def named(names, refs):
    r = Refs()
    for name, ref in zip(names, refs):
        setattr(r, name, ref)
    return r


def window_pieces(w, n, local_rows, cols):
    for a in range(WLEV):
        for b in range(WLAT):
            slab = (a * WLAT + b) * WLON
            i = HALF_LAT + w * WLAT + b
            j = HALF_LON + n * WLON
            own = min(WLON, cols - j)
            if i < local_rows:
                yield "own", None, (a * local_rows + i) * cols + j, own, slab
                if own < WLON:
                    yield "lon", a * local_rows + i, 0, WLON - own, slab + own
            else:
                i = i - local_rows
                yield "lat", None, (a * HALF_LAT + i) * cols + j, own, slab
                if own < WLON:
                    yield "corner", a * HALF_LAT + i, 0, WLON - own, slab + own


def forward_kernel(names, places, cols, *refs):
    r = named(names, refs)
    edge = hasattr(r, "halo_lat")
    bands = sorted({w for w, n in places})
    step = pl.program_id(0)
    last_step = pl.num_programs(0) - 1

    @pl.when(step == 0)
    def _():
        if edge:
            r.acc[...] = r.acc_in[...]
            r.proj[...] = r.proj_in[...]
            r.share32[...] = jnp.zeros_like(r.share32)
        else:
            r.acc[...] = jnp.zeros_like(r.acc)
            r.proj[...] = jnp.zeros_like(r.proj)
        r.wq[...] = r.wqkv[:, 0:C]
        r.wk[...] = r.wqkv[:, C : 2 * C]
        r.wv[...] = r.wqkv[:, 2 * C : 3 * C]

    gain0 = r.gains[0:1, :]
    gain1 = r.gains[1:2, :]
    scaling = float(HEAD) ** -0.5

    local_rows = r.tok.shape[1]

    def widen(w):
        for at, ref in enumerate((r.tok, r.cot)):
            first = HALF_LAT + w * WLAT
            stop = min(first + WLAT, local_rows)
            for a in range(WLEV):
                for i in range(first, stop):
                    row = a * local_rows + i
                    r.own32[at, row * cols : (row + 1) * cols, :] = ref[a, i].astype(F32)
                    if edge:
                        r.lon32[at, row] = r.halo_lon[at, a, i].astype(F32)
                yield None
            if stop < first + WLAT:
                r.lat32[at] = r.halo_lat[at].reshape(WLEV * HALF_LAT * cols, C).astype(F32)
                for a in range(WLEV):
                    for i in range(HALF_LAT):
                        r.corner32[at, a * HALF_LAT + i] = r.halo_corner[at, a, i].astype(F32)
                yield None

    def row_id(w, b):
        i = HALF_LAT + w * WLAT + b
        if i < local_rows:
            return r.ids[i].astype(F32)
        return r.halo_lat[0, 0, i - local_rows, 0:1, 0:1].astype(F32)

    def bias_rows(at, w):
        kid = jnp.zeros((M, 1), F32)
        qid = jnp.zeros((1, LANES), F32)
        for b in range(WLAT):
            kid = jnp.where(r.krow[...] == b, row_id(w, b), kid)
            qid = jnp.where(r.qrow[...] == b, row_id(w, b), qid)
        rest_pad = jnp.zeros((128 - HEADS * REST, M), F32)
        rest = jnp.concatenate([r.bias[0, at, e, MAIN:, :] for e in range(HEADS)] + [rest_pad], axis=0)
        for e in range(HEADS + 1):
            block = r.bias[0, at, e, :MAIN, :] if e < HEADS else rest
            lanes = slice(128 * e, 128 * (e + 1))
            r.biast[at, :, lanes] = jnp.where(kid == qid[:, lanes], block.T, -1e30)
            yield None
        if edge and w == 0:
            r.gbt[at] = r.gbt_in[0]
        else:
            r.gbt[at] = jnp.zeros((M, LANES), F32)
        yield None

    rest_mask = r.mask[HEADS * 128 :, :].astype(F32)

    def front(t):
        w, n = places[t]
        band = bands.index(w)
        here = slice(t * M, (t + 1) * M)
        for at, to in ((0, r.x), (1, r.c)):
            for name, lead, start, length, slab in window_pieces(w, n, local_rows, cols):
                source = getattr(r, name + "32")
                index = (at,) if lead is None else (at, lead)
                to[t * M + slab : t * M + slab + length, :] = source[index + (slice(start, start + length),)]
            yield None
        x = r.x[here, :]
        r.xb[0, t] = x.astype(BF)
        h = (normalize(x)[0] * gain0).astype(BF)
        r.h[0, t] = h
        yield None
        q = (dot(h, r.wq[...]) * scaling).astype(BF)
        r.q[0, t] = q
        r.qbd[t] = spread_heads(q, r.mask[...])
        yield None
        r.k[0, t] = dot(h, r.wk[...]).astype(BF)
        yield None
        v32 = dot(h, r.wv[...])
        r.v[here, :] = v32.astype(BF)
        vt = v32.T.astype(BF)
        yield None
        for lo, hi in CHUNKS:
            scores = dot_nt(r.k[0, t], r.qbd[t, lo:hi, :]) + r.biast[band, :, lo:hi]
            powers = jnp.exp(scores - jnp.max(scores, axis=0, keepdims=True))
            weights = powers * pl.reciprocal(jnp.sum(powers, axis=0, keepdims=True), approx=True)
            r.p[t, :, lo:hi] = weights
            r.pb[t, :, lo:hi] = weights.astype(BF)
            yield None
        for o in per_query(r.pb.at[t], r.v[here, :], vt, rest_mask):
            yield None
        o = o.astype(BF)
        r.o[here, :] = o
        y = r.x[here, :] + dot(o, r.wp[...]).astype(BF).astype(F32)
        yield None
        n2, r2 = normalize(y)
        r.n2[here, :] = n2
        r.r2[here, :] = r2
        r.g[here, :] = (n2 * gain1).astype(BF)
        r.cb[here, :] = r.c[here, :].astype(BF)
        yield None

    def middle(t):
        here = slice(t * M, (t + 1) * M)
        for lo in range(0, FF, 256):
            part = slice(lo, lo + 256)
            u = dot(r.g[here, :], r.wup[:, part])
            cdf, slope = gelu_parts(u)
            r.act[here, part] = (u * cdf).astype(BF)
            yield None
            r.du[here, part] = (dot(r.cb[here, :], r.wdt[:, part]) * slope).astype(BF)
            yield None

    def back(t):
        w, n = places[t]
        band = bands.index(w)
        here = slice(t * M, (t + 1) * M)
        dg = dot_nt(r.du[here, :], r.wup[...])
        yield None
        dy = r.c[here, :] + norm_back(r.n2[here, :], r.r2[here, :], gain1, dg)
        r.dy[0, t] = dy
        dys = dy.astype(BF)
        r.dys[here, :] = dys
        yield None
        do = dot_nt(dys, r.wp[...]).astype(BF)
        r.dobd[t] = spread_heads(do, r.mask[...])
        yield None
        for lo, hi in CHUNKS:
            weights = r.p[t, :, lo:hi]
            dp = dot_nt(r.v[here, :], r.dobd[t, lo:hi, :]) * weights
            ds = dp - weights * jnp.sum(dp, axis=0, keepdims=True)
            r.gbt[band, :, lo:hi] += ds
            r.ds[0, t, :, lo:hi] = ds.astype(BF)
            yield None
        r.dv[0, t] = dot(r.pb[t], r.dobd[t]).astype(BF)
        yield None

    def sums(t):
        here = slice(t * M, (t + 1) * M)
        for first, left, right in ((0, r.g, r.du), (6, r.cb, r.act)):
            left_t = left[here, :].T
            for lo in range(0, FF, 256):
                part = dot(left_t, right[here, lo : lo + 256])
                r.acc[first + lo // 128] += part[:, :128]
                r.acc[first + lo // 128 + 1] += part[:, 128:]
                yield None

    def proj_sum():
        r.proj[...] += dot_tn(r.o[...], r.dys[...])
        yield None

    def share_bias(at):
        share = M // r.share_out.shape[0]
        gbt = r.gbt.at[at]
        last = gbt[:, HEADS * 128 :].T
        for e in range(HEADS):
            r.bias32[at, M * e : M * e + MAIN, :] = gbt[:, 128 * e : 128 * (e + 1)].T[:, :MAIN]
            r.bias32[at, M * e + MAIN : M * (e + 1), :] = last[REST * e : REST * (e + 1), :MAIN]
            yield None
        far = jnp.concatenate(
            [gbt[MAIN:, 128 * e : 128 * (e + 1)] for e in range(HEADS)]
            + [jnp.zeros((128 - HEADS * REST, 128), F32)],
            axis=0,
        )
        r.bias32[at, M * HEADS : M * HEADS + MAIN, :] = far.T
        r.bias32[at, M * HEADS + MAIN : M * (HEADS + 1), :] = jnp.concatenate(
            [last[REST * e : REST * (e + 1), MAIN:] for e in range(HEADS)]
            + [jnp.zeros((REST, 128 - HEADS * REST), F32)],
            axis=1,
        )
        yield None
        for d in range(r.share_out.shape[0]):
            for e in range(HEADS + 1):
                r.share32[at, d, share * e : share * (e + 1), :] = r.bias32[
                    at, M * e + share * d : M * e + share * (d + 1), :
                ]
            r.share_out[d, 0, at] = r.share32[at, d].astype(BF)
            yield None

    count = len(places)
    length = 31
    events = [(0, 2, widen(bands[0])), (0, 3, bias_rows(0, bands[0]))]
    events += [(1, 2, widen(w)) for w in bands[1:]]
    events += [(2, 2, bias_rows(at, bands[at])) for at in range(1, len(bands))]
    start = [3 + STAGGER * t for t in range(count)]
    for t in range(count):
        events.append((start[t], 1, chain(front(t), middle(t), back(t))))
        events.append((start[t] + 22, 1, sums(t)))
    for at in range(len(bands)):
        last = max(t for t, place in enumerate(places) if place[0] == bands[at])
        if edge:
            events.append((start[last] + length + 1, 2, share_bias(at)))
    events.append((start[-1] + length + 1, 1, proj_sum()))
    run_events(events)

    if not edge:
        r.gbt_out[0] = r.gbt[0]

    @pl.when(step == last_step)
    def _():
        r.acc_out[...] = r.acc[...]
        r.proj_out[...] = r.proj[...]


def whole(shape):
    zeros = (0,) * len(shape)
    return pl.BlockSpec(tuple(shape), lambda p: zeros)


def by_level(shape, at, blocks=2):
    block = list(shape)
    block[at] = shape[at] // blocks
    return pl.BlockSpec(tuple(block), lambda p: tuple(p if i == at else 0 for i in range(len(shape))))


def call(kernel, blocks, ins, outs, scratch, name, share_of, limit, *fixed):
    names = [i[0] for i in ins] + [o[0] for o in outs] + [s[0] for s in scratch]
    return pl.pallas_call(
        functools.partial(kernel, names, *fixed),
        grid=(blocks,),
        in_specs=[i[2] for i in ins],
        out_specs=[o[3] for o in outs],
        out_shape=[jax.ShapeDtypeStruct(tuple(o[1]), o[2]) for o in outs],
        scratch_shapes=[pltpu.VMEM(tuple(s[1]), s[2]) for s in scratch],
        compiler_params=pltpu.CompilerParams(
            vmem_limit_bytes=limit * 1024 * 1024,
            dimension_semantics=("arbitrary",),
        ),
        cost_estimate=pl.CostEstimate(
            flops=int(14e9 * share_of), bytes_accessed=int(10e6 * share_of), transcendentals=int(5e6 * share_of)
        ),
        name=name,
    )(*[i[1] for i in ins])


def head_mask():
    head_of_row = np.concatenate(
        [
            np.repeat(np.arange(HEADS), MAIN),
            np.repeat(np.arange(HEADS), REST),
            np.full(128 - HEADS * REST, -1),
        ]
    )
    return jnp.asarray(head_of_row[:, None] == np.arange(C)[None, :] // HEAD, BF)


def run_forward(places, tokens, cotangent, bias, region_ids, weights, halos=None, before=None, lons=8):
    levels, local_rows, cols, channels = tokens.shape
    blocks = levels // WLEV
    count = len(places)
    rows = count * M
    bands = len({w for w, n in places})
    cell_row = (np.arange(M) // WLON % WLAT).astype(np.int32)
    rest = np.concatenate([np.tile(np.arange(MAIN, M), HEADS), np.zeros(128 - HEADS * REST, int)])
    lane_cell = np.concatenate([np.tile(np.arange(MAIN), HEADS), rest])
    edge = halos is not None
    ins = [
        ("tok", tokens, by_level(tokens.shape, 0)),
        ("cot", cotangent, by_level(tokens.shape, 0)),
        ("bias", bias, pl.BlockSpec((1, bands, HEADS, M, M), lambda p: (p, 0, 0, 0, 0))),
        ("ids", region_ids, pl.BlockSpec(memory_space=pltpu.SMEM)),
        ("krow", jnp.asarray(cell_row[:, None]), whole((M, 1))),
        ("qrow", jnp.asarray(cell_row[lane_cell][None, :]), whole((1, LANES))),
        ("mask", head_mask(), whole((LANES, C))),
    ] + [(name, w, whole(w.shape)) for name, w in weights.items()]
    flat = WLEV * local_rows * cols
    acc = (12, C, 128)
    scratch = [
        ("own32", (2, flat, C), F32),
        ("x", (rows, C), F32),
        ("c", (rows, C), F32),
        ("n2", (rows, C), F32),
        ("r2", (rows, 1), F32),
        ("biast", (bands, M, LANES), F32),
        ("gbt", (bands, M, LANES), F32),
        ("p", (count, M, LANES), F32),
        ("pb", (count, M, LANES), BF),
        ("qbd", (count, LANES, C), BF),
        ("dobd", (count, LANES, C), BF),
        ("acc", acc, F32),
        ("proj", (C, C), F32),
        ("act", (rows, FF), BF),
        ("du", (rows, FF), BF),
    ] + [(name, (rows, C), BF) for name in ("v", "o", "g", "cb", "dys")]
    scratch += [(name, (C, C), BF) for name in ("wq", "wk", "wv")]
    outs = []
    for name in STATE:
        shape = (blocks, count, M, LANES if name == "ds" else C)
        outs.append((name, shape, F32 if name == "dy" else BF, by_level(shape, 0)))
    outs += [("acc_out", acc, F32, whole(acc)), ("proj_out", (C, C), F32, whole((C, C)))]
    if edge:
        for name, value in zip(("halo_lat", "halo_lon", "halo_corner"), halos):
            ins.append((name, value, by_level(value.shape, 1)))
        for name, value in zip(("acc_in", "proj_in", "gbt_in"), before):
            ins.append((name, value, by_level(value.shape, 0) if name == "gbt_in" else whole(value.shape)))
        share = (lons, blocks, bands, 128, 128)
        outs.append(("share_out", share, BF, by_level(share, 1)))
        scratch += [
            ("lat32", (2, WLEV * HALF_LAT * cols, C), F32),
            ("lon32", (2, WLEV * local_rows, HALO_COLS, C), F32),
            ("corner32", (2, WLEV * HALF_LAT, HALO_COLS, C), F32),
            ("bias32", (bands, M * (HEADS + 1), 128), F32),
            ("share32", (bands, lons, 128, 128), F32),
        ]
    else:
        outs.append(("gbt_out", (blocks, M, LANES), F32, by_level((blocks, M, LANES), 0)))
    name = "edge_windows" if edge else "inner_windows"
    got = call(forward_kernel, blocks, ins, outs, scratch, name, count * blocks / 20, 60, places, cols)
    return got[: len(STATE)], got[len(STATE) :]


def attention_kernel(names, parts, *refs):
    r = named(names, refs)
    step = pl.program_id(0)
    last_step = pl.num_programs(0) - 1
    scaling = float(HEAD) ** -0.5
    rest_mask = r.mask[HEADS * 128 :, :].astype(F32)

    @pl.when(step == 0)
    def _():
        r.acc[...] = jnp.zeros_like(r.acc)

    def window(at, part, t):
        here = slice(at * M, (at + 1) * M)
        get = lambda name: getattr(r, name + str(part)).at[0, t]
        r.h[here, :] = get("h")[...]
        r.dv[here, :] = get("dv")[...]
        r.qbd[at % 4] = spread_heads(get("q")[...], r.mask[...])
        yield None
        k = get("k")[...]
        kt = k.astype(F32).T.astype(BF)
        yield None
        dk = dot(get("ds")[...], r.qbd[at % 4]).astype(BF)
        r.dk[here, :] = dk
        getattr(r, "dk_out" + str(part))[0, t] = dk
        yield None
        for dq in per_query(get("ds"), k, kt, rest_mask):
            yield None
        dq = (dq * scaling).astype(BF)
        r.dq[here, :] = dq
        getattr(r, "dq_out" + str(part))[0, t] = dq
        yield None

    order = [(part, t) for part, count in enumerate(parts) for t in range(count)]
    for at in range(0, len(order), 2):
        in_turn(*[(9, window(at + i, *order[at + i])) for i in range(2)])
    ht = r.h[...].T
    for i, right in enumerate((r.dq, r.dk, r.dv)):
        r.acc[i] += dot(ht, right[...])

    @pl.when(step == last_step)
    def _():
        per = r.pack_out.shape[1]

        def put(i, tile):
            r.pack_out[C // per * i : C // per * (i + 1)] = tile.astype(BF).reshape(C // per, per, 128)

        small = (r.acc[0], r.acc[1], r.acc[2], r.proj[...])
        for i in range(2):
            one, two = small[2 * i], small[2 * i + 1]
            put(3 * i, one[:, :128])
            put(3 * i + 1, two[:, :128])
            put(3 * i + 2, jnp.concatenate([one[:, 128:], two[:, 128:]], axis=1))
        for i in range(12):
            put(6 + i, r.dense[i])
        first = jnp.zeros((C, C), F32)
        for i in range(3):
            first = first + r.acc[i] * r.wqkv[:, C * i : C * (i + 1)].astype(F32)
        second = jnp.zeros((C, 128), F32)
        for i in range(6):
            second = second + r.dense[i] * r.wup[:, 128 * i : 128 * (i + 1)].astype(F32)
        sums = [jnp.sum(part.T, axis=0, keepdims=True) for part in (first, second)]
        gains = jnp.concatenate([sums[0] / r.gains[0:1, :], sums[1] / r.gains[1:2, :], jnp.zeros((6, C), F32)], axis=0)
        wide = jnp.concatenate(
            [gains[:, :128], jnp.concatenate([gains[:, 128:], jnp.zeros((8, 64), F32)], axis=1)],
            axis=0,
        )
        r.pack_out[18 * C // per, 0:16, :] = wide.astype(BF)


def run_attention(states, sums, weights, devices):
    ins, outs = [], []
    blocks = states[0][0].shape[0]
    parts = [state[0].shape[1] for state in states]
    for part, state in enumerate(states):
        for name, value in zip(STATE, state):
            if name not in ("xb", "dy"):
                ins.append((name + str(part), value, by_level(value.shape, 0)))
    mask = head_mask()
    ins += [
        ("dense", sums[0], whole(sums[0].shape)),
        ("proj", sums[1], whole(sums[1].shape)),
        ("mask", mask, whole(mask.shape)),
    ] + [(name, weights[name], whole(weights[name].shape)) for name in ("wqkv", "wup", "gains")]
    for part, count in enumerate(parts):
        shape = (blocks, count, M, C)
        for name in ("dq_out", "dk_out"):
            outs.append((name + str(part), shape, BF, by_level(shape, 0)))
    pack = (devices, 4096 // devices, 128)
    outs.append(("pack_out", pack, BF, whole(pack)))
    rows = sum(parts) * M
    scratch = [("acc", (3, C, C), F32), ("qbd", (4, LANES, C), BF)]
    scratch += [(name, (rows, C), BF) for name in ("h", "dq", "dk", "dv")]
    got = call(attention_kernel, blocks, ins, outs, scratch, "query_key_grads", 0.3, 60, parts)
    return [got[0:2], got[2:4]], got[-1]


def finish_kernel(names, parts, cols, *refs):
    r = named(names, refs)
    local_rows = r.gt_out.shape[1]
    gain0 = r.gains[0:1, :]

    @pl.when(pl.program_id(0) == 0)
    def _():
        for i in range(3):
            r.w[i] = r.wqkv[:, C * i : C * (i + 1)]
        for name in ("own32", "lat32", "lon32", "corner32"):
            ref = getattr(r, name)
            ref[...] = jnp.zeros_like(ref)

    def window(at, part, t, place):
        get = lambda name: getattr(r, name + str(part)).at[0, t]
        dh = dot_nt(get("dq")[...], r.w[0]) + dot_nt(get("dk")[...], r.w[1]) + dot_nt(get("dv")[...], r.w[2])
        dh = dh.astype(BF).astype(F32)
        yield None
        n1, r1 = normalize(get("xb")[...].astype(F32))
        yield None
        r.gt[at] = get("dy")[...] + norm_back(n1, r1, gain0, dh)
        yield None
        for name, lead, start, length, slab in window_pieces(*place, local_rows, cols):
            target = getattr(r, name + "32")
            index = () if lead is None else (lead,)
            target[index + (slice(start, start + length),)] = r.gt[at, slab : slab + length, :]
        yield None

    order = [(part, t, place) for part, places in enumerate(parts) for t, place in enumerate(places)]
    for at in range(0, len(order), 2):
        in_turn(*[(4, window(at + i, *order[at + i])) for i in range(2)])
    r.gt_out[...] = r.own32[...].astype(BF).reshape(r.gt_out.shape)
    r.lat_out[...] = r.lat32[...].astype(BF).reshape(r.lat_out.shape)
    for a in range(WLEV):
        for i in range(local_rows):
            r.lon_out[a, i] = r.lon32[a * local_rows + i].astype(BF)
        for i in range(HALF_LAT):
            r.corner_out[a, i] = r.corner32[a * HALF_LAT + i].astype(BF)


def run_finish(parts, states, grads, weights, shape):
    levels, local_rows, cols, channels = shape
    blocks = levels // WLEV
    ins = []
    for part, (state, grad) in enumerate(zip(states, grads)):
        for name in ("dv", "xb", "dy"):
            value = state[STATE.index(name)]
            ins.append((name + str(part), value, by_level(value.shape, 0)))
        for name, value in zip(("dq", "dk"), grad):
            ins.append((name + str(part), value, by_level(value.shape, 0)))
    ins += [(name, weights[name], whole(weights[name].shape)) for name in ("wqkv", "gains")]
    outs = []
    for name, out in (
        ("gt_out", shape),
        ("lat_out", (levels, HALF_LAT, cols, C)),
        ("lon_out", (levels, local_rows, HALO_COLS, C)),
        ("corner_out", (levels, HALF_LAT, HALO_COLS, C)),
    ):
        outs.append((name, out, BF, by_level(out, 0)))
    count = sum(len(places) for places in parts)
    scratch = [
        ("w", (3, C, C), BF),
        ("gt", (count, M, C), F32),
        ("own32", (WLEV * local_rows * cols, C), F32),
        ("lat32", (WLEV * HALF_LAT * cols, C), F32),
        ("lon32", (WLEV * local_rows, HALO_COLS, C), F32),
        ("corner32", (WLEV * HALF_LAT, HALO_COLS, C), F32),
    ]
    return call(finish_kernel, blocks, ins, outs, scratch, "token_grads", 0.1, 60, parts, cols)


def cut_kernel(ids_ref, tok_rows, cot_rows, tok_cols, cot_cols, lat_ref, lon_ref, corner_ref):
    cell = lax.broadcasted_iota(jnp.int32, (16, C), 0)
    for at, (rows, cols) in enumerate(((tok_rows, tok_cols), (cot_rows, cot_cols))):
        lat_ref[at] = rows[...]
        lon_ref[at] = cols[:, :, :HALO_COLS, :]
        corner_ref[at] = cols[:, :HALF_LAT, :HALO_COLS, :]
    for a in range(lat_ref.shape[1]):
        for i in range(HALF_LAT):
            first = tok_rows[a, i, 0:16, :].astype(F32)
            lat_ref[0, a, i, 0:16, :] = jnp.where(cell == 0, ids_ref[i].astype(F32), first).astype(BF)


def cut_halos(tokens, cotangent, region_ids):
    levels, local_rows, cols, channels = tokens.shape
    row_spec = pl.BlockSpec((levels, HALF_LAT, cols, C), lambda i: (0, 0, 0, 0))
    col_spec = pl.BlockSpec((levels, local_rows, 16, C), lambda i: (0, 0, 0, 0))
    shapes = ((2, levels, HALF_LAT, cols, C), (2, levels, local_rows, HALO_COLS, C), (2, levels, HALF_LAT, HALO_COLS, C))
    return pl.pallas_call(
        cut_kernel,
        grid=(1,),
        in_specs=[pl.BlockSpec(memory_space=pltpu.SMEM), row_spec, row_spec, col_spec, col_spec],
        out_specs=[whole(shape) for shape in shapes],
        out_shape=[jax.ShapeDtypeStruct(shape, BF) for shape in shapes],
        compiler_params=pltpu.CompilerParams(vmem_limit_bytes=60 * 1024 * 1024),
        name="cut_halos",
    )(region_ids, tokens, cotangent, tokens, cotangent)


def assemble_kernel(own_ref, lat_ref, lon_ref, corner_ref, out_ref):
    levels, local_rows, cols, channels = out_ref.shape
    keep = lax.broadcasted_iota(jnp.int32, (16, C), 0) >= HALF_LON
    pad = jnp.zeros((16 - HALO_COLS, C), F32)
    for a in range(levels):
        for i in range(local_rows):
            row = own_ref.at[a, i] if i >= HALF_LAT else lat_ref.at[a, i]
            left = lon_ref[a, i] if i >= HALF_LAT else corner_ref[a, i]
            left = jnp.concatenate([left.astype(F32), pad], axis=0)
            out_ref[a, i, 0:16, :] = jnp.where(keep, row[0:16, :].astype(F32), left).astype(BF)
            out_ref[a, i, 16:, :] = row[16:, :]


def assemble(own, *received):
    return pl.pallas_call(
        assemble_kernel,
        out_shape=jax.ShapeDtypeStruct(own.shape, BF),
        compiler_params=pltpu.CompilerParams(vmem_limit_bytes=32 * 1024 * 1024),
        name="assemble",
    )(own, *received)


def sum_kernel(in_ref, out_ref):
    total = jnp.sum(in_ref[...].astype(F32), axis=0, keepdims=True).astype(BF)
    out_ref[...] = jnp.broadcast_to(total, out_ref.shape)


def sum_pieces(pieces):
    return pl.pallas_call(
        sum_kernel,
        out_shape=jax.ShapeDtypeStruct(pieces.shape, BF),
        compiler_params=pltpu.CompilerParams(vmem_limit_bytes=32 * 1024 * 1024),
        name="sum_pieces",
    )(pieces)


def sum_bias_kernel(in_ref, out_ref):
    blocks, bands, heads, share, cells = out_ref.shape
    for p in range(blocks):
        for w in range(bands):
            total = jnp.sum(in_ref[:, p, w].astype(F32), axis=0)
            far = total[share * heads : share * (heads + 1)]
            for e in range(heads):
                near = total[share * e : share * (e + 1)]
                out_ref[p, w, e] = jnp.concatenate([near, far[:, REST * e : REST * (e + 1)]], axis=1)


def sum_bias(pieces, shape):
    return pl.pallas_call(
        sum_bias_kernel,
        out_shape=jax.ShapeDtypeStruct(shape, F32),
        compiler_params=pltpu.CompilerParams(vmem_limit_bytes=32 * 1024 * 1024),
        name="sum_bias",
    )(pieces)


def unpack_kernel(scale, in_ref, qkv_ref, proj_ref, up_ref, down_ref, gains_ref):
    def tile(i):
        return in_ref[C * i : C * (i + 1), :].astype(F32) * scale

    half_qk, half_vp = tile(2), tile(5)
    qkv_ref[...] = jnp.concatenate(
        [tile(0), half_qk[:, :64], tile(1), half_qk[:, 64:], tile(3), half_vp[:, :64]], axis=1
    )
    proj_ref[...] = jnp.concatenate([tile(4), half_vp[:, 64:]], axis=1)
    for i in range(FF // 128):
        up_ref[:, 128 * i : 128 * (i + 1)] = tile(6 + i)
        down_ref[:, 128 * i : 128 * (i + 1)] = tile(12 + i)
    wide = in_ref[18 * C : 18 * C + 16, :].astype(F32) * scale
    gains_ref[...] = jnp.concatenate([wide[0:2, :], wide[8:10, :64]], axis=1)


def unpack(packed, scale):
    shapes = ((C, 3 * C), (C, C), (C, FF), (C, FF), (2, C))
    return pl.pallas_call(
        functools.partial(unpack_kernel, scale),
        out_shape=[jax.ShapeDtypeStruct(s, F32) for s in shapes],
        compiler_params=pltpu.CompilerParams(vmem_limit_bytes=32 * 1024 * 1024),
        name="unpack_sums",
    )(packed)


def local(tokens, cotangent, region_ids, norm_gains, w_qkv, w_proj, w_up, w_down, earth_bias):
    levels, nrows, cols, channels = tokens.shape
    both = ("lon", "lat")
    lons, lats = lax.axis_size("lon"), lax.axis_size("lat")
    devices = lons * lats

    def corner_perm(value, steps):
        pairs = [
            (a * lats + b, (a + steps) % lons * lats + (b + steps) % lats)
            for a in range(lons)
            for b in range(lats)
        ]
        return lax.ppermute(value, both, pairs)

    lat_cut, lon_cut, corner_cut = cut_halos(tokens, cotangent, region_ids)
    halos = (perm(lat_cut, "lat", -1), perm(lon_cut, "lon", -1), corner_perm(corner_cut, -1))

    weights = {"wqkv": w_qkv, "wp": w_proj, "wup": w_up, "wdt": w_down.T, "gains": norm_gains}
    inner, sums = run_forward(INNER, tokens, cotangent, earth_bias, region_ids, weights)
    edge, sums = run_forward(EDGE, tokens, cotangent, earth_bias, region_ids, weights, halos, sums, lons)

    shares = lax.all_to_all(sums[2], "lon", 0, 0, tiled=True)
    states = (inner, edge)
    grads, packed = run_attention(states, sums, weights, devices)
    packed, shares = lax.optimization_barrier((packed, shares))
    pieces = lax.all_to_all(packed, both, 0, 0, tiled=True)
    own, *sent = run_finish((INNER, EDGE), states, grads, weights, tokens.shape)
    lat_in = perm(sent[0], "lat", 1)
    lon_in = perm(sent[1], "lon", 1)
    corner_in = corner_perm(sent[2], 1)
    summed, lat_in, lon_in, corner_in = lax.optimization_barrier((sum_pieces(pieces), lat_in, lon_in, corner_in))
    packed = lax.all_to_all(summed, both, 0, 0, tiled=True).reshape(-1, 128)
    cell_count = levels * nrows * cols * devices
    weight_grads = unpack(packed, 1.0 / math.sqrt(cell_count))
    bias_total = sum_bias(shares, earth_bias.shape[:3] + (M // lons, M))
    qkv, proj, up, down, gains = weight_grads
    return (assemble(own, lat_in, lon_in, corner_in), qkv, proj, up, down.T, gains, bias_total)


def solution(mesh):
    placed = (
        P(None, "lat", "lon", None),
        P(None, "lat", "lon", None),
        P("lat"),
        P(),
        P(),
        P(),
        P(),
        P(),
        P(None, "lat", None, None, None),
    )
    return jax.shard_map(
        local,
        mesh=mesh,
        in_specs=placed,
        out_specs=(
            P(None, "lat", "lon", None),
            P(),
            P(),
            P(),
            P(),
            P(),
            P(None, "lat", None, "lon", None),
        ),
        check_vma=False,
    )
```

```python
import functools
import math

import jax
import jax.numpy as jnp
import numpy as np
from jax import lax
from jax.experimental import pallas as pl
from jax.experimental.pallas import tpu as pltpu
from jax.sharding import PartitionSpec as P

HEADS = 6
HEAD = 32
WLEV = 2
WLAT = 6
WLON = 12
C = HEADS * HEAD
FF = 4 * C
M = WLEV * WLAT * WLON
MAIN = 128
REST = M - MAIN
LANES = (HEADS + 1) * 128
SLABS = WLEV * WLAT

BF = jnp.bfloat16
F32 = jnp.float32
epsilon = 1e-05
inv_root_two = 0.7071067811865476
inv_root_tau = 0.3989422804014327


def perm(value, axis, steps):
    count = lax.axis_size(axis)
    pairs = [(source, (source + steps) % count) for source in range(count)]
    return lax.ppermute(value, axis, pairs)


def dot(left, right):
    return jnp.dot(left, right, preferred_element_type=F32)


def dot_nt(left, right):
    return lax.dot_general(left, right, (((1,), (1,)), ((), ())), preferred_element_type=F32)


def dot_tn(left, right):
    return lax.dot_general(left, right, (((0,), (0,)), ((), ())), preferred_element_type=F32)


def normalize(values):
    centred = values - jnp.mean(values, axis=-1, keepdims=True)
    inverse = lax.rsqrt(jnp.mean(centred * centred, axis=-1, keepdims=True) + epsilon)
    return centred * inverse, inverse


def norm_back(normed, inverse, gain_row, upstream):
    scaled = upstream * gain_row
    return inverse * (
        scaled
        - jnp.mean(scaled, axis=-1, keepdims=True)
        - normed * jnp.mean(scaled * normed, axis=-1, keepdims=True)
    )


def gelu_parts(u):
    cdf = 0.5 + 0.5 * lax.erf(u * inv_root_two)
    bell = jnp.exp2(u * u * (-0.5 * math.log2(math.e)))
    return cdf, cdf + u * (bell * inv_root_tau)


CHUNKS = ((0, 256), (256, 512), (512, 768), (768, 896))


def spread_heads(rows, mask):
    first, last = rows[:MAIN], rows[MAIN:]
    return jnp.concatenate([first] * HEADS + [last] * 8, axis=0) * mask


def per_query(weights_ref, right, right_t, rest_mask):
    parts = []
    for e in range(HEADS):
        parts.append(
            dot(
                right_t[HEAD * e : HEAD * (e + 1), :],
                weights_ref[:, 128 * e : 128 * (e + 1)],
            )
        )
        if e % 2:
            yield None
    first = jnp.concatenate(parts, axis=0).T
    yield None
    last = dot_tn(weights_ref[:, HEADS * 128 :], right) * rest_mask
    total = last[0:REST]
    for e in range(1, HEADS):
        total = total + last[REST * e : REST * (e + 1)]
    yield jnp.concatenate([first, total], axis=0)


def in_turn(*streams):
    streams = [[0, count, pieces] for count, pieces in streams]
    while streams:
        stream = min(streams, key=lambda entry: entry[0] / entry[1])
        stream[0] += 1
        if next(stream[2], streams) is streams:
            streams.remove(stream)


def chain(*streams):
    for stream in streams:
        for piece in stream:
            yield None


def run_events(events):
    tick = 0
    while events:
        for event in list(events):
            start, pieces, stream = event
            for i in range(pieces if start <= tick else 0):
                if next(stream, events) is events:
                    events.remove(event)
                    break
        tick += 1


STAGGER = 3
INNER = ((0, 0), (0, 1), (0, 2))
EDGE = ((0, 3), (1, 0), (1, 1), (1, 2), (1, 3))
STATE = ("ds", "q", "k", "h", "dv", "xb", "dy")
HALF_LAT = WLAT // 2
HALF_LON = WLON // 2
HALO_COLS = 8


HALO_ROWS = 3 * HALO_COLS


class Refs:
    pass


def pack(cells):
    half = cells.shape[0] // 2
    ends = jnp.concatenate([cells[:half, 128:], cells[half:, 128:]], axis=1)
    return jnp.concatenate([cells[:, :128], ends], axis=0).astype(BF)


def unpack_cells(packed):
    packed = packed.astype(F32)
    first = packed.shape[0] * 2 // 3
    ends = jnp.concatenate([packed[first:, :64], packed[first:, 64:]], axis=0)
    return jnp.concatenate([packed[:first], ends], axis=1)


def named(names, refs):
    r = Refs()
    for name, ref in zip(names, refs):
        setattr(r, name, ref)
    return r


def window_pieces(w, n, local_rows, cols):
    for a in range(WLEV):
        for b in range(WLAT):
            slab = (a * WLAT + b) * WLON
            i = HALF_LAT + w * WLAT + b
            j = HALF_LON + n * WLON
            own = min(WLON, cols - j)
            if i < local_rows:
                yield "own", None, (a * local_rows + i) * cols + j, own, slab
                if own < WLON:
                    yield "lon", a * local_rows + i, 0, WLON - own, slab + own
            else:
                i = i - local_rows
                yield "lat", None, (a * HALF_LAT + i) * cols + j, own, slab
                if own < WLON:
                    yield "corner", a * HALF_LAT + i, 0, WLON - own, slab + own


def forward_kernel(names, places, cols, *refs):
    r = named(names, refs)
    edge = hasattr(r, "halo_lat")
    bands = sorted({w for w, n in places})
    step = pl.program_id(0)
    last_step = pl.num_programs(0) - 1

    @pl.when(step == 0)
    def _():
        if edge:
            r.acc[...] = r.acc_in[...]
            r.proj[...] = r.proj_in[...]
            r.share32[...] = jnp.zeros_like(r.share32)
        else:
            r.acc[...] = jnp.zeros_like(r.acc)
            r.proj[...] = jnp.zeros_like(r.proj)
        r.wq[...] = r.wqkv[:, 0:C]
        r.wk[...] = r.wqkv[:, C : 2 * C]
        r.wv[...] = r.wqkv[:, 2 * C : 3 * C]

    gain0 = r.gains[0:1, :]
    gain1 = r.gains[1:2, :]
    scaling = float(HEAD) ** -0.5

    local_rows = r.tok.shape[1]

    def widen(w):
        for at, ref in enumerate((r.tok, r.cot)):
            first = HALF_LAT + w * WLAT
            stop = min(first + WLAT, local_rows)
            for a in range(WLEV):
                for i in range(first, stop):
                    row = a * local_rows + i
                    r.own32[at, row * cols : (row + 1) * cols, :] = ref[a, i].astype(F32)
                yield None
            for i in range(first, stop if edge else first):
                both = unpack_cells(r.halo_lon[at, 0, i - HALF_LAT])
                for a in range(WLEV):
                    r.lon32[at, a * local_rows + i] = both[HALO_COLS * a : HALO_COLS * (a + 1)]
            if stop < first + WLAT:
                for i in range(HALF_LAT):
                    both = unpack_cells(r.halo_corner[at, 0, i])
                    for a in range(WLEV):
                        row = a * HALF_LAT + i
                        r.lat32[at, row * cols : (row + 1) * cols, :] = unpack_cells(r.halo_lat[at, a, i])
                        r.corner32[at, row] = both[HALO_COLS * a : HALO_COLS * (a + 1)]
                yield None

    def row_id(w, b):
        i = HALF_LAT + w * WLAT + b
        if i < local_rows:
            return r.ids[i].astype(F32)
        return r.halo_lat[0, 0, i - local_rows, 0:1, 0:1].astype(F32)

    def bias_rows(at, w):
        kid = jnp.zeros((M, 1), F32)
        qid = jnp.zeros((1, LANES), F32)
        for b in range(WLAT):
            kid = jnp.where(r.krow[...] == b, row_id(w, b), kid)
            qid = jnp.where(r.qrow[...] == b, row_id(w, b), qid)
        rest_pad = jnp.zeros((128 - HEADS * REST, M), F32)
        rest = jnp.concatenate([r.bias[0, at, e, MAIN:, :] for e in range(HEADS)] + [rest_pad], axis=0)
        for e in range(HEADS + 1):
            block = r.bias[0, at, e, :MAIN, :] if e < HEADS else rest
            lanes = slice(128 * e, 128 * (e + 1))
            r.biast[at, :, lanes] = jnp.where(kid == qid[:, lanes], block.T, -1e30)
            yield None
        if edge and w == 0:
            r.gbt[at] = r.gbt_in[0]
        else:
            r.gbt[at] = jnp.zeros((M, LANES), F32)
        yield None

    rest_mask = r.mask[HEADS * 128 :, :].astype(F32)

    def front(t):
        w, n = places[t]
        band = bands.index(w)
        here = slice(t * M, (t + 1) * M)
        for at, to in ((0, r.x), (1, r.c)):
            for name, lead, start, length, slab in window_pieces(w, n, local_rows, cols):
                source = getattr(r, name + "32")
                index = (at,) if lead is None else (at, lead)
                to[t * M + slab : t * M + slab + length, :] = source[index + (slice(start, start + length),)]
            yield None
        x = r.x[here, :]
        r.xb[0, t] = x.astype(BF)
        h = (normalize(x)[0] * gain0).astype(BF)
        r.h[0, t] = h
        yield None
        q = (dot(h, r.wq[...]) * scaling).astype(BF)
        r.q[0, t] = q
        r.qbd[t] = spread_heads(q, r.mask[...])
        yield None
        r.k[0, t] = dot(h, r.wk[...]).astype(BF)
        yield None
        v32 = dot(h, r.wv[...])
        r.v[here, :] = v32.astype(BF)
        vt = v32.T.astype(BF)
        yield None
        for lo, hi in CHUNKS:
            scores = dot_nt(r.k[0, t], r.qbd[t, lo:hi, :]) + r.biast[band, :, lo:hi]
            powers = jnp.exp(scores - jnp.max(scores, axis=0, keepdims=True))
            weights = powers * pl.reciprocal(jnp.sum(powers, axis=0, keepdims=True), approx=True)
            r.p[t, :, lo:hi] = weights
            r.pb[t, :, lo:hi] = weights.astype(BF)
            yield None
        for o in per_query(r.pb.at[t], r.v[here, :], vt, rest_mask):
            yield None
        o = o.astype(BF)
        r.o[here, :] = o
        y = r.x[here, :] + dot(o, r.wp[...]).astype(BF).astype(F32)
        yield None
        n2, r2 = normalize(y)
        r.n2[here, :] = n2
        r.r2[here, :] = r2
        r.g[here, :] = (n2 * gain1).astype(BF)
        r.cb[here, :] = r.c[here, :].astype(BF)
        yield None

    def middle(t):
        here = slice(t * M, (t + 1) * M)
        for lo in range(0, FF, 256):
            part = slice(lo, lo + 256)
            u = dot(r.g[here, :], r.wup[:, part])
            cdf, slope = gelu_parts(u)
            r.act[here, part] = (u * cdf).astype(BF)
            yield None
            r.du[here, part] = (dot(r.cb[here, :], r.wdt[:, part]) * slope).astype(BF)
            yield None

    def back(t):
        w, n = places[t]
        band = bands.index(w)
        here = slice(t * M, (t + 1) * M)
        dg = dot_nt(r.du[here, :], r.wup[...])
        yield None
        dy = r.c[here, :] + norm_back(r.n2[here, :], r.r2[here, :], gain1, dg)
        r.dy[0, t] = dy
        dys = dy.astype(BF)
        r.dys[here, :] = dys
        yield None
        do = dot_nt(dys, r.wp[...]).astype(BF)
        r.dobd[t] = spread_heads(do, r.mask[...])
        yield None
        for lo, hi in CHUNKS:
            weights = r.p[t, :, lo:hi]
            dp = dot_nt(r.v[here, :], r.dobd[t, lo:hi, :]) * weights
            ds = dp - weights * jnp.sum(dp, axis=0, keepdims=True)
            r.gbt[band, :, lo:hi] += ds
            r.ds[0, t, :, lo:hi] = ds.astype(BF)
            yield None
        r.dv[0, t] = dot(r.pb[t], r.dobd[t]).astype(BF)
        yield None

    def sums(t):
        here = slice(t * M, (t + 1) * M)
        for first, left, right in ((0, r.g, r.du), (6, r.cb, r.act)):
            left_t = left[here, :].T
            for lo in range(0, FF, 256):
                part = dot(left_t, right[here, lo : lo + 256])
                r.acc[first + lo // 128] += part[:, :128]
                r.acc[first + lo // 128 + 1] += part[:, 128:]
                yield None

    def proj_sum():
        r.proj[...] += dot_tn(r.o[...], r.dys[...])
        yield None

    def share_bias(at):
        share = M // r.share_out.shape[0]
        gbt = r.gbt.at[at]
        last = gbt[:, HEADS * 128 :].T
        for e in range(HEADS):
            r.bias32[at, M * e : M * e + MAIN, :] = gbt[:, 128 * e : 128 * (e + 1)].T[:, :MAIN]
            r.bias32[at, M * e + MAIN : M * (e + 1), :] = last[REST * e : REST * (e + 1), :MAIN]
            yield None
        far = jnp.concatenate(
            [gbt[MAIN:, 128 * e : 128 * (e + 1)] for e in range(HEADS)]
            + [jnp.zeros((128 - HEADS * REST, 128), F32)],
            axis=0,
        )
        r.bias32[at, M * HEADS : M * HEADS + MAIN, :] = far.T
        r.bias32[at, M * HEADS + MAIN : M * (HEADS + 1), :] = jnp.concatenate(
            [last[REST * e : REST * (e + 1), MAIN:] for e in range(HEADS)]
            + [jnp.zeros((REST, 128 - HEADS * REST), F32)],
            axis=1,
        )
        yield None
        for d in range(r.share_out.shape[0]):
            for e in range(HEADS + 1):
                r.share32[at, d, share * e : share * (e + 1), :] = r.bias32[
                    at, M * e + share * d : M * e + share * (d + 1), :
                ]
            r.share_out[d, 0, at] = r.share32[at, d].astype(BF)
            yield None

    count = len(places)
    length = 31
    events = [(0, 2, widen(bands[0])), (0, 3, bias_rows(0, bands[0]))]
    events += [(1, 2, widen(w)) for w in bands[1:]]
    events += [(2, 2, bias_rows(at, bands[at])) for at in range(1, len(bands))]
    start = [3 + STAGGER * t for t in range(count)]
    for t in range(count):
        events.append((start[t], 1, chain(front(t), middle(t), back(t))))
        events.append((start[t] + 22, 1, sums(t)))
    for at in range(len(bands)):
        last = max(t for t, place in enumerate(places) if place[0] == bands[at])
        if edge:
            events.append((start[last] + length + 1, 2, share_bias(at)))
    events.append((start[-1] + length + 1, 1, proj_sum()))
    run_events(events)

    if not edge:
        r.gbt_out[0] = r.gbt[0]

    @pl.when(step == last_step)
    def _():
        r.acc_out[...] = r.acc[...]
        r.proj_out[...] = r.proj[...]


def whole(shape):
    zeros = (0,) * len(shape)
    return pl.BlockSpec(tuple(shape), lambda p: zeros)


def by_level(shape, at, blocks=2):
    block = list(shape)
    block[at] = shape[at] // blocks
    return pl.BlockSpec(tuple(block), lambda p: tuple(p if i == at else 0 for i in range(len(shape))))


def call(kernel, blocks, ins, outs, scratch, name, share_of, limit, *fixed):
    names = [i[0] for i in ins] + [o[0] for o in outs] + [s[0] for s in scratch]
    return pl.pallas_call(
        functools.partial(kernel, names, *fixed),
        grid=(blocks,),
        in_specs=[i[2] for i in ins],
        out_specs=[o[3] for o in outs],
        out_shape=[jax.ShapeDtypeStruct(tuple(o[1]), o[2]) for o in outs],
        scratch_shapes=[pltpu.VMEM(tuple(s[1]), s[2]) for s in scratch],
        compiler_params=pltpu.CompilerParams(
            vmem_limit_bytes=limit * 1024 * 1024,
            dimension_semantics=("arbitrary",),
        ),
        cost_estimate=pl.CostEstimate(
            flops=int(14e9 * share_of), bytes_accessed=int(10e6 * share_of), transcendentals=int(5e6 * share_of)
        ),
        name=name,
    )(*[i[1] for i in ins])


def head_mask():
    head_of_row = np.concatenate(
        [
            np.repeat(np.arange(HEADS), MAIN),
            np.repeat(np.arange(HEADS), REST),
            np.full(128 - HEADS * REST, -1),
        ]
    )
    return jnp.asarray(head_of_row[:, None] == np.arange(C)[None, :] // HEAD, BF)


def run_forward(places, tokens, cotangent, bias, region_ids, weights, halos=None, before=None, lons=8):
    levels, local_rows, cols, channels = tokens.shape
    blocks = levels // WLEV
    count = len(places)
    rows = count * M
    bands = len({w for w, n in places})
    cell_row = (np.arange(M) // WLON % WLAT).astype(np.int32)
    rest = np.concatenate([np.tile(np.arange(MAIN, M), HEADS), np.zeros(128 - HEADS * REST, int)])
    lane_cell = np.concatenate([np.tile(np.arange(MAIN), HEADS), rest])
    edge = halos is not None
    ins = [
        ("tok", tokens, by_level(tokens.shape, 0)),
        ("cot", cotangent, by_level(tokens.shape, 0)),
        ("bias", bias, pl.BlockSpec((1, bands, HEADS, M, M), lambda p: (p, 0, 0, 0, 0))),
        ("ids", region_ids, pl.BlockSpec(memory_space=pltpu.SMEM)),
        ("krow", jnp.asarray(cell_row[:, None]), whole((M, 1))),
        ("qrow", jnp.asarray(cell_row[lane_cell][None, :]), whole((1, LANES))),
        ("mask", head_mask(), whole((LANES, C))),
    ] + [(name, w, whole(w.shape)) for name, w in weights.items()]
    flat = WLEV * local_rows * cols
    acc = (12, C, 128)
    scratch = [
        ("own32", (2, flat, C), F32),
        ("x", (rows, C), F32),
        ("c", (rows, C), F32),
        ("n2", (rows, C), F32),
        ("r2", (rows, 1), F32),
        ("biast", (bands, M, LANES), F32),
        ("gbt", (bands, M, LANES), F32),
        ("p", (count, M, LANES), F32),
        ("pb", (count, M, LANES), BF),
        ("qbd", (count, LANES, C), BF),
        ("dobd", (count, LANES, C), BF),
        ("acc", acc, F32),
        ("proj", (C, C), F32),
        ("act", (rows, FF), BF),
        ("du", (rows, FF), BF),
    ] + [(name, (rows, C), BF) for name in ("v", "o", "g", "cb", "dys")]
    scratch += [(name, (C, C), BF) for name in ("wq", "wk", "wv")]
    outs = []
    for name in STATE:
        shape = (blocks, count, M, LANES if name == "ds" else C)
        outs.append((name, shape, F32 if name == "dy" else BF, by_level(shape, 0)))
    outs += [("acc_out", acc, F32, whole(acc)), ("proj_out", (C, C), F32, whole((C, C)))]
    if edge:
        for name, value in zip(("halo_lat", "halo_lon", "halo_corner"), halos):
            ins.append((name, value, by_level(value.shape, 1)))
        for name, value in zip(("acc_in", "proj_in", "gbt_in"), before):
            ins.append((name, value, by_level(value.shape, 0) if name == "gbt_in" else whole(value.shape)))
        share = (lons, blocks, bands, 128, 128)
        outs.append(("share_out", share, BF, by_level(share, 1)))
        scratch += [
            ("lat32", (2, WLEV * HALF_LAT * cols, C), F32),
            ("lon32", (2, WLEV * local_rows, HALO_COLS, C), F32),
            ("corner32", (2, WLEV * HALF_LAT, HALO_COLS, C), F32),
            ("bias32", (bands, M * (HEADS + 1), 128), F32),
            ("share32", (bands, lons, 128, 128), F32),
        ]
    else:
        outs.append(("gbt_out", (blocks, M, LANES), F32, by_level((blocks, M, LANES), 0)))
    name = "edge_windows" if edge else "inner_windows"
    got = call(forward_kernel, blocks, ins, outs, scratch, name, count * blocks / 20, 60, places, cols)
    return got[: len(STATE)], got[len(STATE) :]


def attention_kernel(names, parts, *refs):
    r = named(names, refs)
    step = pl.program_id(0)
    last_step = pl.num_programs(0) - 1
    scaling = float(HEAD) ** -0.5
    rest_mask = r.mask[HEADS * 128 :, :].astype(F32)

    @pl.when(step == 0)
    def _():
        r.acc[...] = jnp.zeros_like(r.acc)

    def window(at, part, t):
        here = slice(at * M, (at + 1) * M)
        get = lambda name: getattr(r, name + str(part)).at[0, t]
        r.h[here, :] = get("h")[...]
        r.dv[here, :] = get("dv")[...]
        r.qbd[at % 4] = spread_heads(get("q")[...], r.mask[...])
        yield None
        k = get("k")[...]
        kt = k.astype(F32).T.astype(BF)
        yield None
        dk = dot(get("ds")[...], r.qbd[at % 4]).astype(BF)
        r.dk[here, :] = dk
        getattr(r, "dk_out" + str(part))[0, t] = dk
        yield None
        for dq in per_query(get("ds"), k, kt, rest_mask):
            yield None
        dq = (dq * scaling).astype(BF)
        r.dq[here, :] = dq
        getattr(r, "dq_out" + str(part))[0, t] = dq
        yield None

    order = [(part, t) for part, count in enumerate(parts) for t in range(count)]
    for at in range(0, len(order), 2):
        in_turn(*[(9, window(at + i, *order[at + i])) for i in range(2)])
    ht = r.h[...].T
    for i, right in enumerate((r.dq, r.dk, r.dv)):
        r.acc[i] += dot(ht, right[...])

    @pl.when(step == last_step)
    def _():
        per = r.keep_out.shape[1]
        core = r.core[0]

        def put_rows(half, at, rows):
            for ref, here in ((r.keep_out, core == half), (r.send_out, core != half)):

                @pl.when(here)
                def _():
                    ref[at : at + rows.shape[0]] = rows

        def put(i, tile):
            put_rows(i // 9, C // per * (i % 9), tile.astype(BF).reshape(C // per, per, 128))

        small = (r.acc[0], r.acc[1], r.acc[2], r.proj[...])
        for i in range(2):
            one, two = small[2 * i], small[2 * i + 1]
            put(3 * i, one[:, :128])
            put(3 * i + 1, two[:, :128])
            put(3 * i + 2, jnp.concatenate([one[:, 128:], two[:, 128:]], axis=1))
        for i in range(12):
            put(6 + i, r.dense[i])
        first = jnp.zeros((C, C), F32)
        for i in range(3):
            first = first + r.acc[i] * r.wqkv[:, C * i : C * (i + 1)].astype(F32)
        second = jnp.zeros((C, 128), F32)
        for i in range(6):
            second = second + r.dense[i] * r.wup[:, 128 * i : 128 * (i + 1)].astype(F32)
        sums = [jnp.sum(part.T, axis=0, keepdims=True) for part in (first, second)]
        gains = jnp.concatenate([sums[0] / r.gains[0:1, :], sums[1] / r.gains[1:2, :], jnp.zeros((6, C), F32)], axis=0)
        wide = jnp.concatenate(
            [gains[:, :128], jnp.concatenate([gains[:, 128:], jnp.zeros((8, 64), F32)], axis=1)],
            axis=0,
        )
        wide = jnp.concatenate([wide, jnp.zeros((per - 16, 128), F32)], axis=0)
        put_rows(0, 9 * C // per, wide.astype(BF)[None])


def run_attention(states, sums, weights, core, chips):
    ins, outs = [], []
    blocks = states[0][0].shape[0]
    parts = [state[0].shape[1] for state in states]
    for part, state in enumerate(states):
        for name, value in zip(STATE, state):
            if name not in ("xb", "dy"):
                ins.append((name + str(part), value, by_level(value.shape, 0)))
    mask = head_mask()
    ins += [
        ("dense", sums[0], whole(sums[0].shape)),
        ("proj", sums[1], whole(sums[1].shape)),
        ("mask", mask, whole(mask.shape)),
    ] + [(name, weights[name], whole(weights[name].shape)) for name in ("wqkv", "wup", "gains")]
    for part, count in enumerate(parts):
        shape = (blocks, count, M, C)
        for name in ("dq_out", "dk_out"):
            outs.append((name + str(part), shape, BF, by_level(shape, 0)))
    pack = (chips, 2048 // chips, 128)
    outs += [("keep_out", pack, BF, whole(pack)), ("send_out", pack, BF, whole(pack))]
    ins.append(("core", core, pl.BlockSpec(memory_space=pltpu.SMEM)))
    rows = sum(parts) * M
    scratch = [("acc", (3, C, C), F32), ("qbd", (4, LANES, C), BF)]
    scratch += [(name, (rows, C), BF) for name in ("h", "dq", "dk", "dv")]
    got = call(attention_kernel, blocks, ins, outs, scratch, "query_key_grads", 0.3, 60, parts)
    return [got[0:2], got[2:4]], got[4], got[5]


def finish_kernel(names, parts, cols, *refs):
    r = named(names, refs)
    local_rows = r.gt_out.shape[1]
    gain0 = r.gains[0:1, :]

    @pl.when(pl.program_id(0) == 0)
    def _():
        for i in range(3):
            r.w[i] = r.wqkv[:, C * i : C * (i + 1)]
        for name in ("own32", "lat32", "lon32", "corner32"):
            ref = getattr(r, name)
            ref[...] = jnp.zeros_like(ref)

    def window(at, part, t, place):
        get = lambda name: getattr(r, name + str(part)).at[0, t]
        dh = dot_nt(get("dq")[...], r.w[0]) + dot_nt(get("dk")[...], r.w[1]) + dot_nt(get("dv")[...], r.w[2])
        dh = dh.astype(BF).astype(F32)
        yield None
        n1, r1 = normalize(get("xb")[...].astype(F32))
        yield None
        r.gt[at] = get("dy")[...] + norm_back(n1, r1, gain0, dh)
        yield None
        for name, lead, start, length, slab in window_pieces(*place, local_rows, cols):
            target = getattr(r, name + "32")
            index = () if lead is None else (lead,)
            target[index + (slice(start, start + length),)] = r.gt[at, slab : slab + length, :]
        yield None

    order = [(part, t, place) for part, places in enumerate(parts) for t, place in enumerate(places)]
    for at in range(0, len(order), 2):
        in_turn(*[(4, window(at + i, *order[at + i])) for i in range(2)])
    r.gt_out[...] = r.own32[...].astype(BF).reshape(r.gt_out.shape)
    for i in range(HALF_LAT):
        for a in range(WLEV):
            row = a * HALF_LAT + i
            r.lat_out[a, i] = pack(r.lat32[row * cols : (row + 1) * cols, :])
        r.corner_out[0, i] = pack(jnp.concatenate([r.corner32[a * HALF_LAT + i] for a in range(WLEV)], axis=0))
    for i in range(HALF_LAT, local_rows):
        r.lon_out[0, i - HALF_LAT] = pack(
            jnp.concatenate([r.lon32[a * local_rows + i] for a in range(WLEV)], axis=0)
        )


def run_finish(parts, states, grads, weights, shape):
    levels, local_rows, cols, channels = shape
    blocks = levels // WLEV
    ins = []
    for part, (state, grad) in enumerate(zip(states, grads)):
        for name in ("dv", "xb", "dy"):
            value = state[STATE.index(name)]
            ins.append((name + str(part), value, by_level(value.shape, 0)))
        for name, value in zip(("dq", "dk"), grad):
            ins.append((name + str(part), value, by_level(value.shape, 0)))
    ins += [(name, weights[name], whole(weights[name].shape)) for name in ("wqkv", "gains")]
    outs = []
    for name, out in (
        ("gt_out", shape),
        ("lat_out", (levels, HALF_LAT, cols * 3 // 2, 128)),
        ("lon_out", (blocks, local_rows - HALF_LAT, HALO_ROWS, 128)),
        ("corner_out", (blocks, HALF_LAT, HALO_ROWS, 128)),
    ):
        outs.append((name, out, BF, by_level(out, 0)))
    count = sum(len(places) for places in parts)
    scratch = [
        ("w", (3, C, C), BF),
        ("gt", (count, M, C), F32),
        ("own32", (WLEV * local_rows * cols, C), F32),
        ("lat32", (WLEV * HALF_LAT * cols, C), F32),
        ("lon32", (WLEV * local_rows, HALO_COLS, C), F32),
        ("corner32", (WLEV * HALF_LAT, HALO_COLS, C), F32),
    ]
    return call(finish_kernel, blocks, ins, outs, scratch, "token_grads", 0.1, 60, parts, cols)


def cut_kernel(ids_ref, tok_rows, cot_rows, tok_cols, cot_cols, lat_ref, lon_ref, corner_ref):
    levels, half_lat, cols, channels = tok_rows.shape
    cell = lax.broadcasted_iota(jnp.int32, (cols, C), 0)
    for at, (rows, columns) in enumerate(((tok_rows, tok_cols), (cot_rows, cot_cols))):
        for a in range(levels):
            for i in range(half_lat):
                row = rows[a, i].astype(F32)
                if at == 0:
                    row = jnp.where(cell == 0, ids_ref[i].astype(F32), row)
                lat_ref[at, a, i] = pack(row)
        for p in range(levels // WLEV):
            for i in range(columns.shape[1]):
                both = [columns[WLEV * p + a, i, :HALO_COLS, :].astype(F32) for a in range(WLEV)]
                both = pack(jnp.concatenate(both, axis=0))
                if i < half_lat:
                    corner_ref[at, p, i] = both
                else:
                    lon_ref[at, p, i - half_lat] = both


def cut_halos(tokens, cotangent, region_ids):
    levels, local_rows, cols, channels = tokens.shape
    row_spec = pl.BlockSpec((levels, HALF_LAT, cols, C), lambda i: (0, 0, 0, 0))
    col_spec = pl.BlockSpec((levels, local_rows, 16, C), lambda i: (0, 0, 0, 0))
    blocks = levels // WLEV
    shapes = (
        (2, levels, HALF_LAT, cols * 3 // 2, 128),
        (2, blocks, local_rows - HALF_LAT, HALO_ROWS, 128),
        (2, blocks, HALF_LAT, HALO_ROWS, 128),
    )
    return pl.pallas_call(
        cut_kernel,
        grid=(1,),
        in_specs=[pl.BlockSpec(memory_space=pltpu.SMEM), row_spec, row_spec, col_spec, col_spec],
        out_specs=[whole(shape) for shape in shapes],
        out_shape=[jax.ShapeDtypeStruct(shape, BF) for shape in shapes],
        compiler_params=pltpu.CompilerParams(vmem_limit_bytes=60 * 1024 * 1024),
        name="cut_halos",
    )(region_ids, tokens, cotangent, tokens, cotangent)


def assemble_kernel(own_ref, lat_ref, lon_ref, corner_ref, out_ref):
    levels, local_rows, cols, channels = out_ref.shape
    keep = lax.broadcasted_iota(jnp.int32, (16, C), 0) >= HALF_LON
    pad = jnp.zeros((16 - HALO_COLS, C), F32)
    for p in range(levels // WLEV):
        for i in range(local_rows):
            both = unpack_cells(corner_ref[p, i] if i < HALF_LAT else lon_ref[p, i - HALF_LAT])
            for a in range(WLEV):
                level = WLEV * p + a
                left = jnp.concatenate([both[HALO_COLS * a : HALO_COLS * (a + 1)], pad], axis=0)
                if i < HALF_LAT:
                    row = unpack_cells(lat_ref[level, i])
                    out_ref[level, i, 16:, :] = row[16:].astype(BF)
                    first = row[:16]
                else:
                    out_ref[level, i, 16:, :] = own_ref[level, i, 16:, :]
                    first = own_ref[level, i, 0:16, :].astype(F32)
                out_ref[level, i, 0:16, :] = jnp.where(keep, first, left).astype(BF)


def assemble(own, *received):
    return pl.pallas_call(
        assemble_kernel,
        out_shape=jax.ShapeDtypeStruct(own.shape, BF),
        compiler_params=pltpu.CompilerParams(vmem_limit_bytes=32 * 1024 * 1024),
        name="assemble",
    )(own, *received)


def sum_kernel(in_ref, out_ref):
    total = jnp.sum(in_ref[...].astype(F32), axis=0, keepdims=True).astype(BF)
    out_ref[...] = jnp.broadcast_to(total, out_ref.shape)


def sum_pieces(pieces):
    return pl.pallas_call(
        sum_kernel,
        out_shape=jax.ShapeDtypeStruct(pieces.shape, BF),
        compiler_params=pltpu.CompilerParams(vmem_limit_bytes=32 * 1024 * 1024),
        name="sum_pieces",
    )(pieces)


def sum_bias_kernel(in_ref, out_ref):
    blocks, bands, heads, share, cells = out_ref.shape
    for p in range(blocks):
        for w in range(bands):
            total = jnp.sum(in_ref[:, p, w].astype(F32), axis=0)
            far = total[share * heads : share * (heads + 1)]
            for e in range(heads):
                near = total[share * e : share * (e + 1)]
                out_ref[p, w, e] = jnp.concatenate([near, far[:, REST * e : REST * (e + 1)]], axis=1)


def sum_bias(pieces, shape):
    return pl.pallas_call(
        sum_bias_kernel,
        out_shape=jax.ShapeDtypeStruct(shape, F32),
        compiler_params=pltpu.CompilerParams(vmem_limit_bytes=32 * 1024 * 1024),
        name="sum_bias",
    )(pieces)


def unpack_kernel(scale, core_ref, mine_ref, theirs_ref, qkv_ref, proj_ref, up_ref, down_ref, gains_ref, in_ref):
    core = core_ref[0]
    in_ref[core] = mine_ref[...]
    in_ref[1 - core] = theirs_ref[...]

    def tile(i):
        return in_ref[i // 9, C * (i % 9) : C * (i % 9 + 1), :].astype(F32) * scale

    half_qk, half_vp = tile(2), tile(5)
    qkv_ref[...] = jnp.concatenate(
        [tile(0), half_qk[:, :64], tile(1), half_qk[:, 64:], tile(3), half_vp[:, :64]], axis=1
    )
    proj_ref[...] = jnp.concatenate([tile(4), half_vp[:, 64:]], axis=1)
    for i in range(FF // 128):
        up_ref[:, 128 * i : 128 * (i + 1)] = tile(6 + i)
        down_ref[:, 128 * i : 128 * (i + 1)] = tile(12 + i)
    wide = in_ref[0, 9 * C : 9 * C + 16, :].astype(F32) * scale
    gains_ref[...] = jnp.concatenate([wide[0:2, :], wide[8:10, :64]], axis=1)


def unpack(core, mine, theirs, scale):
    shapes = ((C, 3 * C), (C, C), (C, FF), (C, FF), (2, C))
    return pl.pallas_call(
        functools.partial(unpack_kernel, scale),
        out_shape=[jax.ShapeDtypeStruct(s, F32) for s in shapes],
        in_specs=[pl.BlockSpec(memory_space=pltpu.SMEM), pl.BlockSpec(memory_space=pltpu.VMEM), pl.BlockSpec(memory_space=pltpu.VMEM)],
        scratch_shapes=[pltpu.VMEM((2,) + mine.shape, BF)],
        compiler_params=pltpu.CompilerParams(vmem_limit_bytes=32 * 1024 * 1024),
        name="unpack_sums",
    )(core, mine, theirs)


def local(tokens, cotangent, region_ids, norm_gains, w_qkv, w_proj, w_up, w_down, earth_bias):
    levels, nrows, cols, channels = tokens.shape
    both = ("lon", "lat")
    lons, lats = lax.axis_size("lon"), lax.axis_size("lat")
    devices = lons * lats

    def corner_perm(value, steps):
        pairs = [
            (a * lats + b, (a + steps) % lons * lats + (b + steps) % lats)
            for a in range(lons)
            for b in range(lats)
        ]
        return lax.ppermute(value, both, pairs)

    lat_cut, lon_cut, corner_cut = cut_halos(tokens, cotangent, region_ids)
    halos = (perm(lat_cut, "lat", -1), perm(lon_cut, "lon", -1), corner_perm(corner_cut, -1))

    weights = {"wqkv": w_qkv, "wp": w_proj, "wup": w_up, "wdt": w_down.T, "gains": norm_gains}
    inner, sums = run_forward(INNER, tokens, cotangent, earth_bias, region_ids, weights)
    edge, sums = run_forward(EDGE, tokens, cotangent, earth_bias, region_ids, weights, halos, sums, lons)

    shares = lax.all_to_all(sums[2], "lon", 0, 0, tiled=True)
    states = (inner, edge)
    core = lax.rem(lax.axis_index("lat"), 2)[None]
    cores = [[d for d in range(devices) if d % 2 == c] for c in range(2)]

    def other_core(value):
        return lax.ppermute(value, "lat", [(i, i ^ 1) for i in range(lats)])

    def exchange(value):
        return lax.all_to_all(value, both, 0, 0, axis_index_groups=cores, tiled=True)

    grads, keep, send = run_attention(states, sums, weights, core, devices // 2)
    packed = (keep.astype(F32) + other_core(send).astype(F32)).astype(BF)
    own, *sent = run_finish((INNER, EDGE), states, grads, weights, tokens.shape)
    packed, shares, own, *sent = lax.optimization_barrier((packed, shares, own, *sent))
    pieces = exchange(packed)
    lat_in = perm(sent[0], "lat", 1)
    lon_in = perm(sent[1], "lon", 1)
    corner_in = corner_perm(sent[2], 1)
    summed, lat_in, lon_in, corner_in = lax.optimization_barrier((sum_pieces(pieces), lat_in, lon_in, corner_in))
    mine = exchange(summed).reshape(-1, 128)
    cell_count = levels * nrows * cols * devices
    weight_grads = unpack(core, mine, other_core(mine), 1.0 / math.sqrt(cell_count))
    bias_total = sum_bias(shares, earth_bias.shape[:3] + (M // lons, M))
    qkv, proj, up, down, gains = weight_grads
    return (assemble(own, lat_in, lon_in, corner_in), qkv, proj, up, down.T, gains, bias_total)


def solution(mesh):
    placed = (
        P(None, "lat", "lon", None),
        P(None, "lat", "lon", None),
        P("lat"),
        P(),
        P(),
        P(),
        P(),
        P(),
        P(None, "lat", None, None, None),
    )
    return jax.shard_map(
        local,
        mesh=mesh,
        in_specs=placed,
        out_specs=(
            P(None, "lat", "lon", None),
            P(),
            P(),
            P(),
            P(),
            P(),
            P(None, "lat", None, "lon", None),
        ),
        check_vma=False,
    )
```

```python
import functools
import math

import jax
import jax.numpy as jnp
import numpy as np
from jax import lax
from jax.experimental import pallas as pl
from jax.experimental.pallas import tpu as pltpu
from jax.sharding import PartitionSpec as P

HEADS = 6
HEAD = 32
WLEV = 2
WLAT = 6
WLON = 12
C = HEADS * HEAD
FF = 4 * C
M = WLEV * WLAT * WLON
MAIN = 128
REST = M - MAIN
LANES = (HEADS + 1) * 128
SLABS = WLEV * WLAT

BF = jnp.bfloat16
F32 = jnp.float32
epsilon = 1e-05
inv_root_two = 0.7071067811865476
inv_root_tau = 0.3989422804014327


def perm(value, axis, steps):
    count = lax.axis_size(axis)
    pairs = [(source, (source + steps) % count) for source in range(count)]
    return lax.ppermute(value, axis, pairs)


def dot(left, right):
    return jnp.dot(left, right, preferred_element_type=F32)


def dot_nt(left, right):
    return lax.dot_general(left, right, (((1,), (1,)), ((), ())), preferred_element_type=F32)


def dot_tn(left, right):
    return lax.dot_general(left, right, (((0,), (0,)), ((), ())), preferred_element_type=F32)


def normalize(values):
    centred = values - jnp.mean(values, axis=-1, keepdims=True)
    inverse = lax.rsqrt(jnp.mean(centred * centred, axis=-1, keepdims=True) + epsilon)
    return centred * inverse, inverse


def norm_back(normed, inverse, gain_row, upstream):
    scaled = upstream * gain_row
    return inverse * (
        scaled
        - jnp.mean(scaled, axis=-1, keepdims=True)
        - normed * jnp.mean(scaled * normed, axis=-1, keepdims=True)
    )


def gelu_parts(u):
    cdf = 0.5 + 0.5 * lax.erf(u * inv_root_two)
    bell = jnp.exp2(u * u * (-0.5 * math.log2(math.e)))
    return cdf, cdf + u * (bell * inv_root_tau)


CHUNKS = ((0, 256), (256, 512), (512, 768), (768, 896))


def spread_heads(rows, mask):
    first, last = rows[:MAIN], rows[MAIN:]
    return jnp.concatenate([first] * HEADS + [last] * 8, axis=0) * mask


def per_query(weights_ref, right, right_t, rest_mask):
    parts = []
    for e in range(HEADS):
        parts.append(
            dot(
                right_t[HEAD * e : HEAD * (e + 1), :],
                weights_ref[:, 128 * e : 128 * (e + 1)],
            )
        )
        if e % 2:
            yield None
    first = jnp.concatenate(parts, axis=0).T
    yield None
    last = dot_tn(weights_ref[:, HEADS * 128 :], right) * rest_mask
    total = last[0:REST]
    for e in range(1, HEADS):
        total = total + last[REST * e : REST * (e + 1)]
    yield jnp.concatenate([first, total], axis=0)


def in_turn(*streams):
    streams = [[0, count, pieces] for count, pieces in streams]
    while streams:
        stream = min(streams, key=lambda entry: entry[0] / entry[1])
        stream[0] += 1
        if next(stream[2], streams) is streams:
            streams.remove(stream)


def chain(*streams):
    for stream in streams:
        for piece in stream:
            yield None


def run_events(events):
    tick = 0
    while events:
        for event in list(events):
            start, pieces, stream = event
            for i in range(pieces if start <= tick else 0):
                if next(stream, events) is events:
                    events.remove(event)
                    break
        tick += 1


INNER = ((0, 0), (0, 1), (0, 2))
EDGE = ((0, 3), (1, 0), (1, 1), (1, 2), (1, 3))
STATE = ("ds", "q", "k", "h", "dv", "xb", "dy")
HALF_LAT = WLAT // 2
HALF_LON = WLON // 2
HALO_COLS = 8


HALO_ROWS = 3 * HALO_COLS


class Refs:
    pass


def pack(cells):
    half = cells.shape[0] // 2
    ends = jnp.concatenate([cells[:half, 128:], cells[half:, 128:]], axis=1)
    return jnp.concatenate([cells[:, :128], ends], axis=0).astype(BF)


def unpack_cells(packed):
    packed = packed.astype(F32)
    first = packed.shape[0] * 2 // 3
    ends = jnp.concatenate([packed[first:, :64], packed[first:, 64:]], axis=0)
    return jnp.concatenate([packed[:first], ends], axis=1)


def named(names, refs):
    r = Refs()
    for name, ref in zip(names, refs):
        setattr(r, name, ref)
    return r


def window_pieces(w, n, local_rows, cols):
    for a in range(WLEV):
        for b in range(WLAT):
            slab = (a * WLAT + b) * WLON
            i = HALF_LAT + w * WLAT + b
            j = HALF_LON + n * WLON
            own = min(WLON, cols - j)
            if i < local_rows:
                yield "own", None, (a * local_rows + i) * cols + j, own, slab
                if own < WLON:
                    yield "lon", a * local_rows + i, 0, WLON - own, slab + own
            else:
                i = i - local_rows
                yield "lat", None, (a * HALF_LAT + i) * cols + j, own, slab
                if own < WLON:
                    yield "corner", a * HALF_LAT + i, 0, WLON - own, slab + own


def forward_kernel(names, places, cols, *refs):
    r = named(names, refs)
    edge = hasattr(r, "halo_lat")
    bands = sorted({w for w, n in places})
    step = pl.program_id(0)
    last_step = pl.num_programs(0) - 1

    @pl.when(step == 0)
    def _():
        if edge:
            r.share32[...] = jnp.zeros_like(r.share32)
        r.acc[...] = jnp.zeros_like(r.acc)
        r.proj[...] = jnp.zeros_like(r.proj)
        r.wq[...] = r.wqkv[:, 0:C]
        r.wk[...] = r.wqkv[:, C : 2 * C]
        r.wv[...] = r.wqkv[:, 2 * C : 3 * C]

    gain0 = r.gains[0:1, :]
    gain1 = r.gains[1:2, :]
    scaling = float(HEAD) ** -0.5

    local_rows = r.tok.shape[1]

    def widen(w):
        for at, ref in enumerate((r.tok, r.cot)):
            first = HALF_LAT + w * WLAT
            stop = min(first + WLAT, local_rows)
            for a in range(WLEV):
                for i in range(first, stop):
                    row = a * local_rows + i
                    r.own32[at, row * cols : (row + 1) * cols, :] = ref[a, i].astype(F32)
                yield None
            for i in range(first, stop if edge else first):
                both = unpack_cells(r.halo_lon[at, 0, i - HALF_LAT])
                for a in range(WLEV):
                    r.lon32[at, a * local_rows + i] = both[HALO_COLS * a : HALO_COLS * (a + 1)]
            if stop < first + WLAT:
                for i in range(HALF_LAT):
                    both = unpack_cells(r.halo_corner[at, 0, i])
                    for a in range(WLEV):
                        row = a * HALF_LAT + i
                        r.lat32[at, row * cols : (row + 1) * cols, :] = unpack_cells(r.halo_lat[at, a, i])
                        r.corner32[at, row] = both[HALO_COLS * a : HALO_COLS * (a + 1)]
                yield None

    def row_id(w, b):
        i = HALF_LAT + w * WLAT + b
        if i < local_rows:
            return r.ids[i].astype(F32)
        return r.halo_lat[0, 0, i - local_rows, 0:1, 0:1].astype(F32)

    def bias_rows(at, w):
        kid = jnp.zeros((M, 1), F32)
        qid = jnp.zeros((1, LANES), F32)
        for b in range(WLAT):
            kid = jnp.where(r.krow[...] == b, row_id(w, b), kid)
            qid = jnp.where(r.qrow[...] == b, row_id(w, b), qid)
        rest_pad = jnp.zeros((128 - HEADS * REST, M), F32)
        rest = jnp.concatenate([r.bias[0, at, e, MAIN:, :] for e in range(HEADS)] + [rest_pad], axis=0)
        for e in range(HEADS + 1):
            block = r.bias[0, at, e, :MAIN, :] if e < HEADS else rest
            lanes = slice(128 * e, 128 * (e + 1))
            r.biast[at, :, lanes] = jnp.where(kid == qid[:, lanes], block.T, -1e30)
            yield None
        if edge and w == 0:
            r.gbt[at] = r.gbt_in[0]
        else:
            r.gbt[at] = jnp.zeros((M, LANES), F32)
        yield None

    rest_mask = r.mask[HEADS * 128 :, :].astype(F32)

    def front(t):
        w, n = places[t]
        band = bands.index(w)
        here = slice(t * M, (t + 1) * M)
        for at, to in ((0, r.x), (1, r.c)):
            for name, lead, start, length, slab in window_pieces(w, n, local_rows, cols):
                source = getattr(r, name + "32")
                index = (at,) if lead is None else (at, lead)
                to[t * M + slab : t * M + slab + length, :] = source[index + (slice(start, start + length),)]
            yield None
        x = r.x[here, :]
        r.xb[0, t] = x.astype(BF)
        h = (normalize(x)[0] * gain0).astype(BF)
        r.h[0, t] = h
        yield None
        q = (dot(h, r.wq[...]) * scaling).astype(BF)
        r.q[0, t] = q
        r.qbd[t] = spread_heads(q, r.mask[...])
        yield None
        r.k[0, t] = dot(h, r.wk[...]).astype(BF)
        yield None
        v32 = dot(h, r.wv[...])
        r.v[here, :] = v32.astype(BF)
        vt = v32.T.astype(BF)
        yield None
        for lo, hi in CHUNKS:
            scores = dot_nt(r.k[0, t], r.qbd[t, lo:hi, :]) + r.biast[band, :, lo:hi]
            powers = jnp.exp(scores - jnp.max(scores, axis=0, keepdims=True))
            weights = powers * pl.reciprocal(jnp.sum(powers, axis=0, keepdims=True), approx=True)
            r.p[t, :, lo:hi] = weights
            r.pb[t, :, lo:hi] = weights.astype(BF)
            yield None
        for o in per_query(r.pb.at[t], r.v[here, :], vt, rest_mask):
            yield None
        o = o.astype(BF)
        r.o[here, :] = o
        y = r.x[here, :] + dot(o, r.wp[...]).astype(BF).astype(F32)
        yield None
        n2, r2 = normalize(y)
        r.n2[here, :] = n2
        r.r2[here, :] = r2
        r.g[here, :] = (n2 * gain1).astype(BF)
        r.cb[here, :] = r.c[here, :].astype(BF)
        yield None

    def middle(t):
        here = slice(t * M, (t + 1) * M)
        for lo in range(0, FF, 256):
            part = slice(lo, lo + 256)
            u = dot(r.g[here, :], r.wup[:, part])
            cdf, slope = gelu_parts(u)
            r.act[here, part] = (u * cdf).astype(BF)
            yield None
            r.du[here, part] = (dot(r.cb[here, :], r.wdt[:, part]) * slope).astype(BF)
            yield None

    def back(t):
        w, n = places[t]
        band = bands.index(w)
        here = slice(t * M, (t + 1) * M)
        dg = dot_nt(r.du[here, :], r.wup[...])
        yield None
        dy = r.c[here, :] + norm_back(r.n2[here, :], r.r2[here, :], gain1, dg)
        r.dy[0, t] = dy
        dys = dy.astype(BF)
        r.dys[here, :] = dys
        yield None
        do = dot_nt(dys, r.wp[...]).astype(BF)
        r.dobd[t] = spread_heads(do, r.mask[...])
        yield None
        for lo, hi in CHUNKS:
            weights = r.p[t, :, lo:hi]
            dp = dot_nt(r.v[here, :], r.dobd[t, lo:hi, :]) * weights
            ds = dp - weights * jnp.sum(dp, axis=0, keepdims=True)
            r.gbt[band, :, lo:hi] += ds
            r.ds[0, t, :, lo:hi] = ds.astype(BF)
            yield None
        r.dv[0, t] = dot(r.pb[t], r.dobd[t]).astype(BF)
        yield None

    def sums(t):
        here = slice(t * M, (t + 1) * M)
        for first, left, right in ((0, r.g, r.du), (6, r.cb, r.act)):
            left_t = left[here, :].T
            for lo in range(0, FF, 256):
                part = dot(left_t, right[here, lo : lo + 256])
                r.acc[first + lo // 128] += part[:, :128]
                r.acc[first + lo // 128 + 1] += part[:, 128:]
                yield None

    def proj_sum():
        r.proj[...] += dot_tn(r.o[...], r.dys[...])
        yield None

    def share_bias(at):
        share = M // r.share_out.shape[0]
        gbt = r.gbt.at[at]
        last = gbt[:, HEADS * 128 :].T
        for e in range(HEADS):
            r.bias32[at, M * e : M * e + MAIN, :] = gbt[:, 128 * e : 128 * (e + 1)].T[:, :MAIN]
            r.bias32[at, M * e + MAIN : M * (e + 1), :] = last[REST * e : REST * (e + 1), :MAIN]
            yield None
        far = jnp.concatenate(
            [gbt[MAIN:, 128 * e : 128 * (e + 1)] for e in range(HEADS)]
            + [jnp.zeros((128 - HEADS * REST, 128), F32)],
            axis=0,
        )
        r.bias32[at, M * HEADS : M * HEADS + MAIN, :] = far.T
        r.bias32[at, M * HEADS + MAIN : M * (HEADS + 1), :] = jnp.concatenate(
            [last[REST * e : REST * (e + 1), MAIN:] for e in range(HEADS)]
            + [jnp.zeros((REST, 128 - HEADS * REST), F32)],
            axis=1,
        )
        yield None
        for d in range(r.share_out.shape[0]):
            for e in range(HEADS + 1):
                r.share32[at, d, share * e : share * (e + 1), :] = r.bias32[
                    at, M * e + share * d : M * e + share * (d + 1), :
                ]
            r.share_out[d, 0, at] = r.share32[at, d].astype(BF)
            yield None

    count = len(places)
    length = 31
    events = [(0, 2, widen(bands[0])), (0, 3, bias_rows(0, bands[0]))]
    events += [(1, 2, widen(w)) for w in bands[1:]]
    events += [(2, 2, bias_rows(at, bands[at])) for at in range(1, len(bands))]
    start = [3 + (3 if edge else 2) * t for t in range(count)]
    for t in range(count):
        events.append((start[t], 1, chain(front(t), middle(t), back(t))))
        events.append((start[t] + 22, 1, sums(t)))
    for at in range(len(bands)):
        last = max(t for t, place in enumerate(places) if place[0] == bands[at])
        if edge:
            events.append((start[last] + length + 1, 2, share_bias(at)))
    events.append((start[-1] + length + 1, 1, proj_sum()))
    run_events(events)

    if not edge:
        r.gbt_out[0] = r.gbt[0]

    @pl.when(step == last_step)
    def _():
        r.acc_out[...] = r.acc[...]
        r.proj_out[...] = r.proj[...]


def whole(shape):
    zeros = (0,) * len(shape)
    return pl.BlockSpec(tuple(shape), lambda p: zeros)


def by_level(shape, at, blocks=2):
    block = list(shape)
    block[at] = shape[at] // blocks
    return pl.BlockSpec(tuple(block), lambda p: tuple(p if i == at else 0 for i in range(len(shape))))


def call(kernel, blocks, ins, outs, scratch, name, share_of, limit, *fixed):
    names = [i[0] for i in ins] + [o[0] for o in outs] + [s[0] for s in scratch]
    return pl.pallas_call(
        functools.partial(kernel, names, *fixed),
        grid=(blocks,),
        in_specs=[i[2] for i in ins],
        out_specs=[o[3] for o in outs],
        out_shape=[jax.ShapeDtypeStruct(tuple(o[1]), o[2]) for o in outs],
        scratch_shapes=[pltpu.VMEM(tuple(s[1]), s[2]) for s in scratch],
        compiler_params=pltpu.CompilerParams(
            vmem_limit_bytes=limit * 1024 * 1024,
            dimension_semantics=("arbitrary",),
        ),
        cost_estimate=pl.CostEstimate(
            flops=int(14e9 * share_of), bytes_accessed=int(10e6 * share_of), transcendentals=int(5e6 * share_of)
        ),
        name=name,
    )(*[i[1] for i in ins])


def head_mask():
    head_of_row = np.concatenate(
        [
            np.repeat(np.arange(HEADS), MAIN),
            np.repeat(np.arange(HEADS), REST),
            np.full(128 - HEADS * REST, -1),
        ]
    )
    return jnp.asarray(head_of_row[:, None] == np.arange(C)[None, :] // HEAD, BF)


def run_forward(places, tokens, cotangent, bias, region_ids, weights, halos=None, before=None, lons=8):
    levels, local_rows, cols, channels = tokens.shape
    blocks = levels // WLEV
    count = len(places)
    rows = count * M
    bands = len({w for w, n in places})
    cell_row = (np.arange(M) // WLON % WLAT).astype(np.int32)
    rest = np.concatenate([np.tile(np.arange(MAIN, M), HEADS), np.zeros(128 - HEADS * REST, int)])
    lane_cell = np.concatenate([np.tile(np.arange(MAIN), HEADS), rest])
    edge = halos is not None
    ins = [
        ("tok", tokens, by_level(tokens.shape, 0)),
        ("cot", cotangent, by_level(tokens.shape, 0)),
        ("bias", bias, pl.BlockSpec((1, bands, HEADS, M, M), lambda p: (p, 0, 0, 0, 0))),
        ("ids", region_ids, pl.BlockSpec(memory_space=pltpu.SMEM)),
        ("krow", jnp.asarray(cell_row[:, None]), whole((M, 1))),
        ("qrow", jnp.asarray(cell_row[lane_cell][None, :]), whole((1, LANES))),
        ("mask", head_mask(), whole((LANES, C))),
    ] + [(name, w, whole(w.shape)) for name, w in weights.items()]
    flat = WLEV * local_rows * cols
    acc = (12, C, 128)
    scratch = [
        ("own32", (2, flat, C), F32),
        ("x", (rows, C), F32),
        ("c", (rows, C), F32),
        ("n2", (rows, C), F32),
        ("r2", (rows, 1), F32),
        ("biast", (bands, M, LANES), F32),
        ("gbt", (bands, M, LANES), F32),
        ("p", (count, M, LANES), F32),
        ("pb", (count, M, LANES), BF),
        ("qbd", (count, LANES, C), BF),
        ("dobd", (count, LANES, C), BF),
        ("acc", acc, F32),
        ("proj", (C, C), F32),
        ("act", (rows, FF), BF),
        ("du", (rows, FF), BF),
    ] + [(name, (rows, C), BF) for name in ("v", "o", "g", "cb", "dys")]
    scratch += [(name, (C, C), BF) for name in ("wq", "wk", "wv")]
    outs = []
    for name in STATE:
        shape = (blocks, count, M, LANES if name == "ds" else C)
        outs.append((name, shape, F32 if name == "dy" else BF, by_level(shape, 0)))
    outs += [("acc_out", acc, F32, whole(acc)), ("proj_out", (C, C), F32, whole((C, C)))]
    if edge:
        for name, value in zip(("halo_lat", "halo_lon", "halo_corner"), halos):
            ins.append((name, value, by_level(value.shape, 1)))
        ins.append(("gbt_in", before, by_level(before.shape, 0)))
        share = (lons, blocks, bands, 128, 128)
        outs.append(("share_out", share, BF, by_level(share, 1)))
        scratch += [
            ("lat32", (2, WLEV * HALF_LAT * cols, C), F32),
            ("lon32", (2, WLEV * local_rows, HALO_COLS, C), F32),
            ("corner32", (2, WLEV * HALF_LAT, HALO_COLS, C), F32),
            ("bias32", (bands, M * (HEADS + 1), 128), F32),
            ("share32", (bands, lons, 128, 128), F32),
        ]
    else:
        outs.append(("gbt_out", (blocks, M, LANES), F32, by_level((blocks, M, LANES), 0)))
    name = "edge_windows" if edge else "inner_windows"
    got = call(forward_kernel, blocks, ins, outs, scratch, name, count * blocks / 20, 60, places, cols)
    return got[: len(STATE)], got[len(STATE) :]


def attention_kernel(names, parts, *refs):
    r = named(names, refs)
    step = pl.program_id(0)
    last_step = pl.num_programs(0) - 1
    scaling = float(HEAD) ** -0.5
    rest_mask = r.mask[HEADS * 128 :, :].astype(F32)

    @pl.when(step == 0)
    def _():
        r.acc[...] = jnp.zeros_like(r.acc)

    def window(at, part, t):
        here = slice(at * M, (at + 1) * M)
        get = lambda name: getattr(r, name + str(part)).at[0, t]
        r.h[here, :] = get("h")[...]
        r.dv[here, :] = get("dv")[...]
        r.qbd[at % 4] = spread_heads(get("q")[...], r.mask[...])
        yield None
        k = get("k")[...]
        kt = k.astype(F32).T.astype(BF)
        yield None
        dk = dot(get("ds")[...], r.qbd[at % 4]).astype(BF)
        r.dk[here, :] = dk
        getattr(r, "dk_out" + str(part))[0, t] = dk
        yield None
        for dq in per_query(get("ds"), k, kt, rest_mask):
            yield None
        dq = (dq * scaling).astype(BF)
        r.dq[here, :] = dq
        getattr(r, "dq_out" + str(part))[0, t] = dq
        yield None

    order = [(part, t) for part, count in enumerate(parts) for t in range(count)]
    for at in range(0, len(order), 2):
        in_turn(*[(9, window(at + i, *order[at + i])) for i in range(2)])
    ht = r.h[...].T
    for i, right in enumerate((r.dq, r.dk, r.dv)):
        r.acc[i] += dot(ht, right[...])

    @pl.when(step == last_step)
    def _():
        per = r.keep_out.shape[1]
        core = r.core[0]

        def put_rows(half, at, rows):
            for ref, here in ((r.keep_out, core == half), (r.send_out, core != half)):

                @pl.when(here)
                def _():
                    ref[at : at + rows.shape[0]] = rows

        def put(i, tile):
            put_rows(i // 9, C // per * (i % 9), tile.astype(BF).reshape(C // per, per, 128))

        small = (r.acc[0], r.acc[1], r.acc[2], r.proj0[...] + r.proj1[...])
        for i in range(2):
            one, two = small[2 * i], small[2 * i + 1]
            put(3 * i, one[:, :128])
            put(3 * i + 1, two[:, :128])
            put(3 * i + 2, jnp.concatenate([one[:, 128:], two[:, 128:]], axis=1))
        for i in range(12):
            put(6 + i, r.dense0[i] + r.dense1[i])
        first = jnp.zeros((C, C), F32)
        for i in range(3):
            first = first + r.acc[i] * r.wqkv[:, C * i : C * (i + 1)].astype(F32)
        second = jnp.zeros((C, 128), F32)
        for i in range(6):
            second = second + (r.dense0[i] + r.dense1[i]) * r.wup[:, 128 * i : 128 * (i + 1)].astype(F32)
        sums = [jnp.sum(part.T, axis=0, keepdims=True) for part in (first, second)]
        gains = jnp.concatenate([sums[0] / r.gains[0:1, :], sums[1] / r.gains[1:2, :], jnp.zeros((6, C), F32)], axis=0)
        wide = jnp.concatenate(
            [gains[:, :128], jnp.concatenate([gains[:, 128:], jnp.zeros((8, 64), F32)], axis=1)],
            axis=0,
        )
        wide = jnp.concatenate([wide, jnp.zeros((per - 16, 128), F32)], axis=0)
        put_rows(0, 9 * C // per, wide.astype(BF)[None])


def run_attention(states, sums, weights, core, chips):
    ins, outs = [], []
    blocks = states[0][0].shape[0]
    parts = [state[0].shape[1] for state in states]
    for part, state in enumerate(states):
        for name, value in zip(STATE, state):
            if name not in ("xb", "dy"):
                ins.append((name + str(part), value, by_level(value.shape, 0)))
    mask = head_mask()
    ins += [
        (name + str(part), value, whole(value.shape))
        for part, both in enumerate(sums)
        for name, value in zip(("dense", "proj"), both)
    ]
    ins += [("mask", mask, whole(mask.shape))]
    ins += [(name, weights[name], whole(weights[name].shape)) for name in ("wqkv", "wup", "gains")]
    for part, count in enumerate(parts):
        shape = (blocks, count, M, C)
        for name in ("dq_out", "dk_out"):
            outs.append((name + str(part), shape, BF, by_level(shape, 0)))
    pack = (chips, 2048 // chips, 128)
    outs += [("keep_out", pack, BF, whole(pack)), ("send_out", pack, BF, whole(pack))]
    ins.append(("core", core, pl.BlockSpec(memory_space=pltpu.SMEM)))
    rows = sum(parts) * M
    scratch = [("acc", (3, C, C), F32), ("qbd", (4, LANES, C), BF)]
    scratch += [(name, (rows, C), BF) for name in ("h", "dq", "dk", "dv")]
    got = call(attention_kernel, blocks, ins, outs, scratch, "query_key_grads", 0.3, 60, parts)
    return [got[0:2], got[2:4]], got[4], got[5]


def finish_kernel(names, parts, cols, *refs):
    r = named(names, refs)
    local_rows = r.gt_out.shape[1]
    gain0 = r.gains[0:1, :]

    @pl.when(pl.program_id(0) == 0)
    def _():
        for i in range(3):
            r.w[i] = r.wqkv[:, C * i : C * (i + 1)]
        for name in ("own32", "lat32", "lon32", "corner32"):
            ref = getattr(r, name)
            ref[...] = jnp.zeros_like(ref)

    def window(at, part, t, place):
        get = lambda name: getattr(r, name + str(part)).at[0, t]
        dh = dot_nt(get("dq")[...], r.w[0]) + dot_nt(get("dk")[...], r.w[1]) + dot_nt(get("dv")[...], r.w[2])
        dh = dh.astype(BF).astype(F32)
        yield None
        n1, r1 = normalize(get("xb")[...].astype(F32))
        yield None
        r.gt[at] = get("dy")[...] + norm_back(n1, r1, gain0, dh)
        yield None
        for name, lead, start, length, slab in window_pieces(*place, local_rows, cols):
            target = getattr(r, name + "32")
            index = () if lead is None else (lead,)
            target[index + (slice(start, start + length),)] = r.gt[at, slab : slab + length, :]
        yield None

    order = [(part, t, place) for part, places in enumerate(parts) for t, place in enumerate(places)]
    for at in range(0, len(order), 2):
        in_turn(*[(4, window(at + i, *order[at + i])) for i in range(2)])
    r.gt_out[...] = r.own32[...].astype(BF).reshape(r.gt_out.shape)
    for i in range(HALF_LAT):
        for a in range(WLEV):
            row = a * HALF_LAT + i
            r.lat_out[a, i] = pack(r.lat32[row * cols : (row + 1) * cols, :])
        r.corner_out[0, i] = pack(jnp.concatenate([r.corner32[a * HALF_LAT + i] for a in range(WLEV)], axis=0))
    for i in range(HALF_LAT, local_rows):
        r.lon_out[0, i - HALF_LAT] = pack(
            jnp.concatenate([r.lon32[a * local_rows + i] for a in range(WLEV)], axis=0)
        )


def run_finish(parts, states, grads, weights, shape):
    levels, local_rows, cols, channels = shape
    blocks = levels // WLEV
    ins = []
    for part, (state, grad) in enumerate(zip(states, grads)):
        for name in ("dv", "xb", "dy"):
            value = state[STATE.index(name)]
            ins.append((name + str(part), value, by_level(value.shape, 0)))
        for name, value in zip(("dq", "dk"), grad):
            ins.append((name + str(part), value, by_level(value.shape, 0)))
    ins += [(name, weights[name], whole(weights[name].shape)) for name in ("wqkv", "gains")]
    outs = []
    for name, out in (
        ("gt_out", shape),
        ("lat_out", (levels, HALF_LAT, cols * 3 // 2, 128)),
        ("lon_out", (blocks, local_rows - HALF_LAT, HALO_ROWS, 128)),
        ("corner_out", (blocks, HALF_LAT, HALO_ROWS, 128)),
    ):
        outs.append((name, out, BF, by_level(out, 0)))
    count = sum(len(places) for places in parts)
    scratch = [
        ("w", (3, C, C), BF),
        ("gt", (count, M, C), F32),
        ("own32", (WLEV * local_rows * cols, C), F32),
        ("lat32", (WLEV * HALF_LAT * cols, C), F32),
        ("lon32", (WLEV * local_rows, HALO_COLS, C), F32),
        ("corner32", (WLEV * HALF_LAT, HALO_COLS, C), F32),
    ]
    return call(finish_kernel, blocks, ins, outs, scratch, "token_grads", 0.1, 60, parts, cols)


def cut_kernel(ids_ref, tok_rows, cot_rows, tok_cols, cot_cols, lat_ref, lon_ref, corner_ref):
    levels, half_lat, cols, channels = tok_rows.shape
    cell = lax.broadcasted_iota(jnp.int32, (cols, C), 0)
    for at, (rows, columns) in enumerate(((tok_rows, tok_cols), (cot_rows, cot_cols))):
        for a in range(levels):
            for i in range(half_lat):
                row = rows[a, i].astype(F32)
                if at == 0:
                    row = jnp.where(cell == 0, ids_ref[i].astype(F32), row)
                lat_ref[at, a, i] = pack(row)
        for p in range(levels // WLEV):
            for i in range(columns.shape[1]):
                both = [columns[WLEV * p + a, i, :HALO_COLS, :].astype(F32) for a in range(WLEV)]
                both = pack(jnp.concatenate(both, axis=0))
                if i < half_lat:
                    corner_ref[at, p, i] = both
                else:
                    lon_ref[at, p, i - half_lat] = both


def cut_halos(tokens, cotangent, region_ids):
    levels, local_rows, cols, channels = tokens.shape
    row_spec = pl.BlockSpec((levels, HALF_LAT, cols, C), lambda i: (0, 0, 0, 0))
    col_spec = pl.BlockSpec((levels, local_rows, 16, C), lambda i: (0, 0, 0, 0))
    blocks = levels // WLEV
    shapes = (
        (2, levels, HALF_LAT, cols * 3 // 2, 128),
        (2, blocks, local_rows - HALF_LAT, HALO_ROWS, 128),
        (2, blocks, HALF_LAT, HALO_ROWS, 128),
    )
    return pl.pallas_call(
        cut_kernel,
        grid=(1,),
        in_specs=[pl.BlockSpec(memory_space=pltpu.SMEM), row_spec, row_spec, col_spec, col_spec],
        out_specs=[whole(shape) for shape in shapes],
        out_shape=[jax.ShapeDtypeStruct(shape, BF) for shape in shapes],
        compiler_params=pltpu.CompilerParams(vmem_limit_bytes=60 * 1024 * 1024),
        name="cut_halos",
    )(region_ids, tokens, cotangent, tokens, cotangent)


def assemble_kernel(own_ref, lat_ref, lon_ref, corner_ref, out_ref):
    levels, local_rows, cols, channels = out_ref.shape
    keep = lax.broadcasted_iota(jnp.int32, (16, C), 0) >= HALF_LON
    pad = jnp.zeros((16 - HALO_COLS, C), F32)
    for p in range(levels // WLEV):
        for i in range(local_rows):
            both = unpack_cells(corner_ref[p, i] if i < HALF_LAT else lon_ref[p, i - HALF_LAT])
            for a in range(WLEV):
                level = WLEV * p + a
                left = jnp.concatenate([both[HALO_COLS * a : HALO_COLS * (a + 1)], pad], axis=0)
                if i < HALF_LAT:
                    row = unpack_cells(lat_ref[level, i])
                    out_ref[level, i, 16:, :] = row[16:].astype(BF)
                    first = row[:16]
                else:
                    out_ref[level, i, 16:, :] = own_ref[level, i, 16:, :]
                    first = own_ref[level, i, 0:16, :].astype(F32)
                out_ref[level, i, 0:16, :] = jnp.where(keep, first, left).astype(BF)


def assemble(own, *received):
    return pl.pallas_call(
        assemble_kernel,
        out_shape=jax.ShapeDtypeStruct(own.shape, BF),
        compiler_params=pltpu.CompilerParams(vmem_limit_bytes=32 * 1024 * 1024),
        name="assemble",
    )(own, *received)


def sum_kernel(in_ref, out_ref):
    total = jnp.sum(in_ref[...].astype(F32), axis=0, keepdims=True).astype(BF)
    out_ref[...] = jnp.broadcast_to(total, out_ref.shape)


def sum_pieces(pieces):
    return pl.pallas_call(
        sum_kernel,
        out_shape=jax.ShapeDtypeStruct(pieces.shape, BF),
        compiler_params=pltpu.CompilerParams(vmem_limit_bytes=32 * 1024 * 1024),
        name="sum_pieces",
    )(pieces)


def sum_bias_kernel(in_ref, out_ref):
    blocks, heads, share, bands, cells = out_ref.shape
    for p in range(blocks):
        for w in range(bands):
            total = jnp.sum(in_ref[:, p, w].astype(F32), axis=0)
            far = total[share * heads : share * (heads + 1)]
            for e in range(heads):
                near = total[share * e : share * (e + 1)]
                out_ref[p, e, :, w, :] = jnp.concatenate([near, far[:, REST * e : REST * (e + 1)]], axis=1)


def sum_bias(pieces, shape):
    return pl.pallas_call(
        sum_bias_kernel,
        out_shape=jax.ShapeDtypeStruct(shape, F32),
        compiler_params=pltpu.CompilerParams(vmem_limit_bytes=32 * 1024 * 1024),
        name="sum_bias",
    )(pieces)


def unpack_kernel(scale, core_ref, mine_ref, theirs_ref, qkv_ref, proj_ref, up_ref, down_ref, gains_ref, in_ref):
    core = core_ref[0]
    in_ref[core] = mine_ref[...]
    in_ref[1 - core] = theirs_ref[...]

    def tile(i):
        return in_ref[i // 9, C * (i % 9) : C * (i % 9 + 1), :].astype(F32) * scale

    half_qk, half_vp = tile(2), tile(5)
    qkv_ref[...] = jnp.concatenate(
        [tile(0), half_qk[:, :64], tile(1), half_qk[:, 64:], tile(3), half_vp[:, :64]], axis=1
    )
    proj_ref[...] = jnp.concatenate([tile(4), half_vp[:, 64:]], axis=1)
    for i in range(FF // 128):
        up_ref[:, 128 * i : 128 * (i + 1)] = tile(6 + i)
        down_ref[:, 128 * i : 128 * (i + 1)] = tile(12 + i)
    wide = in_ref[0, 9 * C : 9 * C + 16, :].astype(F32) * scale
    gains_ref[...] = jnp.concatenate([wide[0:2, :], wide[8:10, :64]], axis=1)


def unpack(core, mine, theirs, scale):
    shapes = ((C, 3 * C), (C, C), (C, FF), (C, FF), (2, C))
    return pl.pallas_call(
        functools.partial(unpack_kernel, scale),
        out_shape=[jax.ShapeDtypeStruct(s, F32) for s in shapes],
        in_specs=[pl.BlockSpec(memory_space=pltpu.SMEM), pl.BlockSpec(memory_space=pltpu.VMEM), pl.BlockSpec(memory_space=pltpu.VMEM)],
        scratch_shapes=[pltpu.VMEM((2,) + mine.shape, BF)],
        compiler_params=pltpu.CompilerParams(vmem_limit_bytes=32 * 1024 * 1024),
        name="unpack_sums",
    )(core, mine, theirs)


def local(tokens, cotangent, region_ids, norm_gains, w_qkv, w_proj, w_up, w_down, earth_bias):
    levels, nrows, cols, channels = tokens.shape
    both = ("lon", "lat")
    lons, lats = lax.axis_size("lon"), lax.axis_size("lat")
    devices = lons * lats

    def corner_perm(value, steps):
        pairs = [
            (a * lats + b, (a + steps) % lons * lats + (b + steps) % lats)
            for a in range(lons)
            for b in range(lats)
        ]
        return lax.ppermute(value, both, pairs)

    lat_cut, lon_cut, corner_cut = cut_halos(tokens, cotangent, region_ids)
    halos = (perm(lat_cut, "lat", -1), perm(lon_cut, "lon", -1), corner_perm(corner_cut, -1))

    weights = {"wqkv": w_qkv, "wp": w_proj, "wup": w_up, "wdt": w_down.T, "gains": norm_gains}
    inner, inner_sums = run_forward(INNER, tokens, cotangent, earth_bias, region_ids, weights)
    edge, sums = run_forward(EDGE, tokens, cotangent, earth_bias, region_ids, weights, halos, inner_sums[2], lons)

    shares = lax.all_to_all(sums[2], "lon", 0, 0, tiled=True)
    states = (inner, edge)
    core = lax.rem(lax.axis_index("lat"), 2)[None]
    cores = [[d for d in range(devices) if d % 2 == c] for c in range(2)]

    def other_core(value):
        return lax.ppermute(value, "lat", [(i, i ^ 1) for i in range(lats)])

    def exchange(value):
        return lax.all_to_all(value, both, 0, 0, axis_index_groups=cores, tiled=True)

    grads, keep, send = run_attention(states, (inner_sums[:2], sums[:2]), weights, core, devices // 2)
    packed = (keep.astype(F32) + other_core(send).astype(F32)).astype(BF)
    own, *sent = run_finish((INNER, EDGE), states, grads, weights, tokens.shape)
    packed, shares, own, *sent = lax.optimization_barrier((packed, shares, own, *sent))
    pieces = exchange(packed)
    lat_in = perm(sent[0], "lat", 1)
    lon_in = perm(sent[1], "lon", 1)
    corner_in = corner_perm(sent[2], 1)
    mine = exchange(sum_pieces(pieces)).reshape(-1, 128)
    grad_tokens = assemble(own, lat_in, lon_in, corner_in)
    mine, grad_tokens = lax.optimization_barrier((mine, grad_tokens))
    cell_count = levels * nrows * cols * devices
    weight_grads = unpack(core, mine, other_core(mine), 1.0 / math.sqrt(cell_count))
    blocks, bands = earth_bias.shape[:2]
    bias_total = sum_bias(shares, (blocks, HEADS, M // lons, bands, M)).transpose(0, 3, 1, 2, 4)
    qkv, proj, up, down, gains = weight_grads
    return (grad_tokens, qkv, proj, up, down.T, gains, bias_total)


def solution(mesh):
    placed = (
        P(None, "lat", "lon", None),
        P(None, "lat", "lon", None),
        P("lat"),
        P(),
        P(),
        P(),
        P(),
        P(),
        P(None, "lat", None, None, None),
    )
    return jax.shard_map(
        local,
        mesh=mesh,
        in_specs=placed,
        out_specs=(
            P(None, "lat", "lon", None),
            P(),
            P(),
            P(),
            P(),
            P(),
            P(None, "lat", None, "lon", None),
        ),
        check_vma=False,
    )
```

```python
import functools
import math

import jax
import jax.numpy as jnp
import numpy as np
from jax import lax
from jax.experimental import pallas as pl
from jax.experimental.pallas import tpu as pltpu
from jax.sharding import PartitionSpec as P

HEADS = 6
HEAD = 32
WLEV = 2
WLAT = 6
WLON = 12
C = HEADS * HEAD
FF = 4 * C
M = WLEV * WLAT * WLON
MAIN = 128
REST = M - MAIN
LANES = (HEADS + 1) * 128
SLABS = WLEV * WLAT

BF = jnp.bfloat16
F32 = jnp.float32
epsilon = 1e-05
inv_root_two = 0.7071067811865476
inv_root_tau = 0.3989422804014327


def perm(value, axis, steps):
    count = lax.axis_size(axis)
    pairs = [(source, (source + steps) % count) for source in range(count)]
    return lax.ppermute(value, axis, pairs)


def dot(left, right):
    return jnp.dot(left, right, preferred_element_type=F32)


def dot_nt(left, right):
    return lax.dot_general(left, right, (((1,), (1,)), ((), ())), preferred_element_type=F32)


def dot_tn(left, right):
    return lax.dot_general(left, right, (((0,), (0,)), ((), ())), preferred_element_type=F32)


def normalize(values):
    centred = values - jnp.mean(values, axis=-1, keepdims=True)
    inverse = lax.rsqrt(jnp.mean(centred * centred, axis=-1, keepdims=True) + epsilon)
    return centred * inverse, inverse


def norm_back(normed, inverse, gain_row, upstream):
    scaled = upstream * gain_row
    return inverse * (
        scaled
        - jnp.mean(scaled, axis=-1, keepdims=True)
        - normed * jnp.mean(scaled * normed, axis=-1, keepdims=True)
    )


def gelu_parts(u):
    cdf = 0.5 + 0.5 * lax.erf(u * inv_root_two)
    bell = jnp.exp2(u * u * (-0.5 * math.log2(math.e)))
    return cdf, cdf + u * (bell * inv_root_tau)


CHUNKS = ((0, 256), (256, 512), (512, 768), (768, 896))


def spread_heads(rows, mask):
    first, last = rows[:MAIN], rows[MAIN:]
    return jnp.concatenate([first] * HEADS + [last] * 8, axis=0) * mask


def per_query(weights_ref, right, right_t, rest_mask):
    parts = []
    for e in range(HEADS):
        parts.append(
            dot(
                right_t[HEAD * e : HEAD * (e + 1), :],
                weights_ref[:, 128 * e : 128 * (e + 1)],
            )
        )
        if e % 2:
            yield None
    first = jnp.concatenate(parts, axis=0).T
    yield None
    last = dot_tn(weights_ref[:, HEADS * 128 :], right) * rest_mask
    total = last[0:REST]
    for e in range(1, HEADS):
        total = total + last[REST * e : REST * (e + 1)]
    yield jnp.concatenate([first, total], axis=0)


def in_turn(*streams):
    streams = [[0, count, pieces] for count, pieces in streams]
    while streams:
        stream = min(streams, key=lambda entry: entry[0] / entry[1])
        stream[0] += 1
        if next(stream[2], streams) is streams:
            streams.remove(stream)


def chain(*streams):
    for stream in streams:
        for piece in stream:
            yield None


def run_events(events):
    tick = 0
    while events:
        for event in list(events):
            start, pieces, stream = event
            for i in range(pieces if start <= tick else 0):
                if next(stream, events) is events:
                    events.remove(event)
                    break
        tick += 1


INNER = ((0, 0), (0, 1), (0, 2))
EDGE = ((0, 3), (1, 0), (1, 1), (1, 2), (1, 3))
STATE = ("ds", "q", "k", "h", "dv", "xb", "dy")
HALF_LAT = WLAT // 2
HALF_LON = WLON // 2
HALO_COLS = 8


HALO_ROWS = 3 * HALO_COLS


class Refs:
    pass


def pack(cells):
    half = cells.shape[0] // 2
    ends = jnp.concatenate([cells[:half, 128:], cells[half:, 128:]], axis=1)
    return jnp.concatenate([cells[:, :128], ends], axis=0).astype(BF)


def unpack_cells(packed):
    packed = packed.astype(F32)
    first = packed.shape[0] * 2 // 3
    ends = jnp.concatenate([packed[first:, :64], packed[first:, 64:]], axis=0)
    return jnp.concatenate([packed[:first], ends], axis=1)


def named(names, refs):
    r = Refs()
    for name, ref in zip(names, refs):
        setattr(r, name, ref)
    return r


def window_pieces(w, n, local_rows, cols):
    for a in range(WLEV):
        for b in range(WLAT):
            slab = (a * WLAT + b) * WLON
            i = HALF_LAT + w * WLAT + b
            j = HALF_LON + n * WLON
            own = min(WLON, cols - j)
            if i < local_rows:
                yield "own", None, (a * local_rows + i) * cols + j, own, slab
                if own < WLON:
                    yield "lon", a * local_rows + i, 0, WLON - own, slab + own
            else:
                i = i - local_rows
                yield "lat", None, (a * HALF_LAT + i) * cols + j, own, slab
                if own < WLON:
                    yield "corner", a * HALF_LAT + i, 0, WLON - own, slab + own


def forward_kernel(names, places, cols, *refs):
    r = named(names, refs)
    edge = hasattr(r, "halo_lat")
    bands = sorted({w for w, n in places})
    step = pl.program_id(0)
    last_step = pl.num_programs(0) - 1

    @pl.when(step == 0)
    def _():
        if edge:
            r.share32[...] = jnp.zeros_like(r.share32)
        r.acc[...] = jnp.zeros_like(r.acc)
        r.proj[...] = jnp.zeros_like(r.proj)
        r.wq[...] = r.wqkv[:, 0:C]
        r.wk[...] = r.wqkv[:, C : 2 * C]
        r.wv[...] = r.wqkv[:, 2 * C : 3 * C]

    gain0 = r.gains[0:1, :]
    gain1 = r.gains[1:2, :]
    scaling = float(HEAD) ** -0.5

    local_rows = r.tok.shape[1]

    def widen(w):
        for at, ref in enumerate((r.tok, r.cot)):
            first = HALF_LAT + w * WLAT
            stop = min(first + WLAT, local_rows)
            for a in range(WLEV):
                for i in range(first, stop):
                    row = a * local_rows + i
                    r.own32[at, row * cols : (row + 1) * cols, :] = ref[a, i].astype(F32)
                yield None
            for i in range(first, stop if edge else first):
                both = unpack_cells(r.halo_lon[at, 0, i - HALF_LAT])
                for a in range(WLEV):
                    r.lon32[at, a * local_rows + i] = both[HALO_COLS * a : HALO_COLS * (a + 1)]
            if stop < first + WLAT:
                for i in range(HALF_LAT):
                    both = unpack_cells(r.halo_corner[at, 0, i])
                    for a in range(WLEV):
                        row = a * HALF_LAT + i
                        r.lat32[at, row * cols : (row + 1) * cols, :] = unpack_cells(r.halo_lat[at, a, i])
                        r.corner32[at, row] = both[HALO_COLS * a : HALO_COLS * (a + 1)]
                yield None

    def row_id(w, b):
        i = HALF_LAT + w * WLAT + b
        if i < local_rows:
            return r.ids[i].astype(F32)
        return r.halo_lat[0, 0, i - local_rows, 0:1, 0:1].astype(F32)

    def bias_rows(at, w):
        kid = jnp.zeros((M, 1), F32)
        qid = jnp.zeros((1, LANES), F32)
        for b in range(WLAT):
            kid = jnp.where(r.krow[...] == b, row_id(w, b), kid)
            qid = jnp.where(r.qrow[...] == b, row_id(w, b), qid)
        rest_pad = jnp.zeros((128 - HEADS * REST, M), F32)
        rest = jnp.concatenate([r.bias[0, at, e, MAIN:, :] for e in range(HEADS)] + [rest_pad], axis=0)
        for e in range(HEADS + 1):
            block = r.bias[0, at, e, :MAIN, :] if e < HEADS else rest
            lanes = slice(128 * e, 128 * (e + 1))
            r.biast[at, :, lanes] = jnp.where(kid == qid[:, lanes], block.T, -1e30)
            yield None
        if edge and w == 0:
            r.gbt[at] = r.gbt_in[0]
        else:
            r.gbt[at] = jnp.zeros((M, LANES), F32)
        yield None

    rest_mask = r.mask[HEADS * 128 :, :].astype(F32)

    def front(t):
        w, n = places[t]
        band = bands.index(w)
        here = slice(t * M, (t + 1) * M)
        for at, to in ((0, r.x), (1, r.c)):
            for name, lead, start, length, slab in window_pieces(w, n, local_rows, cols):
                source = getattr(r, name + "32")
                index = (at,) if lead is None else (at, lead)
                to[t * M + slab : t * M + slab + length, :] = source[index + (slice(start, start + length),)]
            yield None
        x = r.x[here, :]
        r.xb[0, t] = x.astype(BF)
        h = (normalize(x)[0] * gain0).astype(BF)
        r.h[0, t] = h
        yield None
        q = (dot(h, r.wq[...]) * scaling).astype(BF)
        r.q[0, t] = q
        r.qbd[t] = spread_heads(q, r.mask[...])
        yield None
        r.k[0, t] = dot(h, r.wk[...]).astype(BF)
        yield None
        v32 = dot(h, r.wv[...])
        r.v[here, :] = v32.astype(BF)
        vt = v32.T.astype(BF)
        yield None
        for lo, hi in CHUNKS:
            scores = dot_nt(r.k[0, t], r.qbd[t, lo:hi, :]) + r.biast[band, :, lo:hi]
            powers = jnp.exp(scores - jnp.max(scores, axis=0, keepdims=True))
            weights = powers * pl.reciprocal(jnp.sum(powers, axis=0, keepdims=True), approx=True)
            r.p[t, :, lo:hi] = weights
            r.pb[t, :, lo:hi] = weights.astype(BF)
            yield None
        for o in per_query(r.pb.at[t], r.v[here, :], vt, rest_mask):
            yield None
        o = o.astype(BF)
        r.o[here, :] = o
        y = r.x[here, :] + dot(o, r.wp[...]).astype(BF).astype(F32)
        yield None
        n2, r2 = normalize(y)
        r.n2[here, :] = n2
        r.r2[here, :] = r2
        r.g[here, :] = (n2 * gain1).astype(BF)
        r.cb[here, :] = r.c[here, :].astype(BF)
        yield None

    def middle(t):
        here = slice(t * M, (t + 1) * M)
        for lo in range(0, FF, 256):
            part = slice(lo, lo + 256)
            u = dot(r.g[here, :], r.wup[:, part])
            cdf, slope = gelu_parts(u)
            r.act[here, part] = (u * cdf).astype(BF)
            yield None
            r.du[here, part] = (dot(r.cb[here, :], r.wdt[:, part]) * slope).astype(BF)
            yield None

    def back(t):
        w, n = places[t]
        band = bands.index(w)
        here = slice(t * M, (t + 1) * M)
        dg = dot_nt(r.du[here, :], r.wup[...])
        yield None
        dy = r.c[here, :] + norm_back(r.n2[here, :], r.r2[here, :], gain1, dg)
        r.dy[0, t] = dy
        dys = dy.astype(BF)
        r.dys[here, :] = dys
        yield None
        do = dot_nt(dys, r.wp[...]).astype(BF)
        r.dobd[t] = spread_heads(do, r.mask[...])
        yield None
        for lo, hi in CHUNKS:
            weights = r.p[t, :, lo:hi]
            dp = dot_nt(r.v[here, :], r.dobd[t, lo:hi, :]) * weights
            ds = dp - weights * jnp.sum(dp, axis=0, keepdims=True)
            r.gbt[band, :, lo:hi] += ds
            r.ds[0, t, :, lo:hi] = ds.astype(BF)
            yield None
        r.dv[0, t] = dot(r.pb[t], r.dobd[t]).astype(BF)
        yield None

    def sums(t):
        here = slice(t * M, (t + 1) * M)
        for first, left, right in ((0, r.g, r.du), (6, r.cb, r.act)):
            left_t = left[here, :].T
            for lo in range(0, FF, 256):
                part = dot(left_t, right[here, lo : lo + 256])
                r.acc[first + lo // 128] += part[:, :128]
                r.acc[first + lo // 128 + 1] += part[:, 128:]
                yield None

    def proj_sum():
        r.proj[...] += dot_tn(r.o[...], r.dys[...])
        yield None

    def share_bias(at):
        share = M // r.share_out.shape[0]
        gbt = r.gbt.at[at]
        last = gbt[:, HEADS * 128 :].T
        for e in range(HEADS):
            r.bias32[at, M * e : M * e + MAIN, :] = gbt[:, 128 * e : 128 * (e + 1)].T[:, :MAIN]
            r.bias32[at, M * e + MAIN : M * (e + 1), :] = last[REST * e : REST * (e + 1), :MAIN]
            yield None
        far = jnp.concatenate(
            [gbt[MAIN:, 128 * e : 128 * (e + 1)] for e in range(HEADS)]
            + [jnp.zeros((128 - HEADS * REST, 128), F32)],
            axis=0,
        )
        r.bias32[at, M * HEADS : M * HEADS + MAIN, :] = far.T
        r.bias32[at, M * HEADS + MAIN : M * (HEADS + 1), :] = jnp.concatenate(
            [last[REST * e : REST * (e + 1), MAIN:] for e in range(HEADS)]
            + [jnp.zeros((REST, 128 - HEADS * REST), F32)],
            axis=1,
        )
        yield None
        for d in range(r.share_out.shape[0]):
            for e in range(HEADS + 1):
                r.share32[at, d, share * e : share * (e + 1), :] = r.bias32[
                    at, M * e + share * d : M * e + share * (d + 1), :
                ]
            r.share_out[d, 0, at] = r.share32[at, d].astype(BF)
            yield None

    count = len(places)
    length = 31
    events = [(0, 2, widen(bands[0])), (0, 3, bias_rows(0, bands[0]))]
    events += [(1, 2, widen(w)) for w in bands[1:]]
    events += [(2, 2, bias_rows(at, bands[at])) for at in range(1, len(bands))]
    start = [3 + (3 if edge else 2) * t for t in range(count)]
    for t in range(count):
        events.append((start[t], 1, chain(front(t), middle(t), back(t))))
        events.append((start[t] + 22, 1, sums(t)))
    for at in range(len(bands)):
        last = max(t for t, place in enumerate(places) if place[0] == bands[at])
        if edge:
            events.append((start[last] + length + 1, 2, share_bias(at)))
    events.append((start[-1] + length + 1, 1, proj_sum()))
    run_events(events)

    if not edge:
        r.gbt_out[0] = r.gbt[0]

    @pl.when(step == last_step)
    def _():
        r.acc_out[...] = r.acc[...]
        r.proj_out[...] = r.proj[...]


def whole(shape):
    zeros = (0,) * len(shape)
    return pl.BlockSpec(tuple(shape), lambda p: zeros)


def by_level(shape, at, blocks=2):
    block = list(shape)
    block[at] = shape[at] // blocks
    return pl.BlockSpec(tuple(block), lambda p: tuple(p if i == at else 0 for i in range(len(shape))))


def call(kernel, blocks, ins, outs, scratch, name, share_of, limit, *fixed):
    names = [i[0] for i in ins] + [o[0] for o in outs] + [s[0] for s in scratch]
    return pl.pallas_call(
        functools.partial(kernel, names, *fixed),
        grid=(blocks,),
        in_specs=[i[2] for i in ins],
        out_specs=[o[3] for o in outs],
        out_shape=[jax.ShapeDtypeStruct(tuple(o[1]), o[2]) for o in outs],
        scratch_shapes=[pltpu.VMEM(tuple(s[1]), s[2]) for s in scratch],
        compiler_params=pltpu.CompilerParams(
            vmem_limit_bytes=limit * 1024 * 1024,
            dimension_semantics=("arbitrary",),
        ),
        cost_estimate=pl.CostEstimate(
            flops=int(14e9 * share_of), bytes_accessed=int(10e6 * share_of), transcendentals=int(5e6 * share_of)
        ),
        name=name,
    )(*[i[1] for i in ins])


def head_mask():
    head_of_row = np.concatenate(
        [
            np.repeat(np.arange(HEADS), MAIN),
            np.repeat(np.arange(HEADS), REST),
            np.full(128 - HEADS * REST, -1),
        ]
    )
    return jnp.asarray(head_of_row[:, None] == np.arange(C)[None, :] // HEAD, BF)


def run_forward(places, tokens, cotangent, bias, region_ids, weights, halos=None, before=None, lons=8):
    levels, local_rows, cols, channels = tokens.shape
    blocks = levels // WLEV
    count = len(places)
    rows = count * M
    bands = len({w for w, n in places})
    cell_row = (np.arange(M) // WLON % WLAT).astype(np.int32)
    rest = np.concatenate([np.tile(np.arange(MAIN, M), HEADS), np.zeros(128 - HEADS * REST, int)])
    lane_cell = np.concatenate([np.tile(np.arange(MAIN), HEADS), rest])
    edge = halos is not None
    ins = [
        ("tok", tokens, by_level(tokens.shape, 0)),
        ("cot", cotangent, by_level(tokens.shape, 0)),
        ("bias", bias, pl.BlockSpec((1, bands, HEADS, M, M), lambda p: (p, 0, 0, 0, 0))),
        ("ids", region_ids, pl.BlockSpec(memory_space=pltpu.SMEM)),
        ("krow", jnp.asarray(cell_row[:, None]), whole((M, 1))),
        ("qrow", jnp.asarray(cell_row[lane_cell][None, :]), whole((1, LANES))),
        ("mask", head_mask(), whole((LANES, C))),
    ] + [(name, w, whole(w.shape)) for name, w in weights.items()]
    flat = WLEV * local_rows * cols
    acc = (12, C, 128)
    scratch = [
        ("own32", (2, flat, C), F32),
        ("x", (rows, C), F32),
        ("c", (rows, C), F32),
        ("n2", (rows, C), F32),
        ("r2", (rows, 1), F32),
        ("biast", (bands, M, LANES), F32),
        ("gbt", (bands, M, LANES), F32),
        ("p", (count, M, LANES), F32),
        ("pb", (count, M, LANES), BF),
        ("qbd", (count, LANES, C), BF),
        ("dobd", (count, LANES, C), BF),
        ("acc", acc, F32),
        ("proj", (C, C), F32),
        ("act", (rows, FF), BF),
        ("du", (rows, FF), BF),
    ] + [(name, (rows, C), BF) for name in ("v", "o", "g", "cb", "dys")]
    scratch += [(name, (C, C), BF) for name in ("wq", "wk", "wv")]
    outs = []
    for name in STATE:
        shape = (blocks, count, M, LANES if name == "ds" else C)
        outs.append((name, shape, F32 if name == "dy" else BF, by_level(shape, 0)))
    outs += [("acc_out", acc, F32, whole(acc)), ("proj_out", (C, C), F32, whole((C, C)))]
    if edge:
        for name, value in zip(("halo_lat", "halo_lon", "halo_corner"), halos):
            ins.append((name, value, by_level(value.shape, 1)))
        ins.append(("gbt_in", before, by_level(before.shape, 0)))
        share = (lons, blocks, bands, 128, 128)
        outs.append(("share_out", share, BF, by_level(share, 1)))
        scratch += [
            ("lat32", (2, WLEV * HALF_LAT * cols, C), F32),
            ("lon32", (2, WLEV * local_rows, HALO_COLS, C), F32),
            ("corner32", (2, WLEV * HALF_LAT, HALO_COLS, C), F32),
            ("bias32", (bands, M * (HEADS + 1), 128), F32),
            ("share32", (bands, lons, 128, 128), F32),
        ]
    else:
        outs.append(("gbt_out", (blocks, M, LANES), F32, by_level((blocks, M, LANES), 0)))
    name = "edge_windows" if edge else "inner_windows"
    got = call(forward_kernel, blocks, ins, outs, scratch, name, count * blocks / 20, 60, places, cols)
    return got[: len(STATE)], got[len(STATE) :]


def attention_kernel(names, parts, *refs):
    r = named(names, refs)
    step = pl.program_id(0)
    last_step = pl.num_programs(0) - 1
    scaling = float(HEAD) ** -0.5
    rest_mask = r.mask[HEADS * 128 :, :].astype(F32)

    @pl.when(step == 0)
    def _():
        r.acc[...] = jnp.zeros_like(r.acc)

    def window(at, part, t):
        here = slice(at * M, (at + 1) * M)
        get = lambda name: getattr(r, name + str(part)).at[0, t]
        r.h[here, :] = get("h")[...]
        r.dv[here, :] = get("dv")[...]
        r.qbd[at % 4] = spread_heads(get("q")[...], r.mask[...])
        yield None
        k = get("k")[...]
        kt = k.astype(F32).T.astype(BF)
        yield None
        dk = dot(get("ds")[...], r.qbd[at % 4]).astype(BF)
        r.dk[here, :] = dk
        getattr(r, "dk_out" + str(part))[0, t] = dk
        yield None
        for dq in per_query(get("ds"), k, kt, rest_mask):
            yield None
        dq = (dq * scaling).astype(BF)
        r.dq[here, :] = dq
        getattr(r, "dq_out" + str(part))[0, t] = dq
        yield None

    order = [(part, t) for part, count in enumerate(parts) for t in range(count)]
    for at in range(0, len(order), 2):
        in_turn(*[(9, window(at + i, *order[at + i])) for i in range(2)])
    ht = r.h[...].T
    for i, right in enumerate((r.dq, r.dk, r.dv)):
        r.acc[i] += dot(ht, right[...])

    @pl.when(step == last_step)
    def _():
        per = r.keep_out.shape[1]
        core = r.core[0]

        def put_rows(half, at, rows):
            for ref, here in ((r.keep_out, core == half), (r.send_out, core != half)):

                @pl.when(here)
                def _():
                    ref[at : at + rows.shape[0]] = rows

        def put(i, tile):
            put_rows(i // 9, C // per * (i % 9), tile.astype(BF).reshape(C // per, per, 128))

        small = (r.acc[0], r.acc[1], r.acc[2], r.proj0[...] + r.proj1[...])
        for i in range(2):
            one, two = small[2 * i], small[2 * i + 1]
            put(3 * i, one[:, :128])
            put(3 * i + 1, two[:, :128])
            put(3 * i + 2, jnp.concatenate([one[:, 128:], two[:, 128:]], axis=1))
        for i in range(12):
            put(6 + i, r.dense0[i] + r.dense1[i])
        first = jnp.zeros((C, C), F32)
        for i in range(3):
            first = first + r.acc[i] * r.wqkv[:, C * i : C * (i + 1)].astype(F32)
        second = jnp.zeros((C, 128), F32)
        for i in range(6):
            second = second + (r.dense0[i] + r.dense1[i]) * r.wup[:, 128 * i : 128 * (i + 1)].astype(F32)
        sums = [jnp.sum(part.T, axis=0, keepdims=True) for part in (first, second)]
        gains = jnp.concatenate([sums[0] / r.gains[0:1, :], sums[1] / r.gains[1:2, :], jnp.zeros((6, C), F32)], axis=0)
        wide = jnp.concatenate(
            [gains[:, :128], jnp.concatenate([gains[:, 128:], jnp.zeros((8, 64), F32)], axis=1)],
            axis=0,
        )
        wide = jnp.concatenate([wide, jnp.zeros((per - 16, 128), F32)], axis=0)
        put_rows(0, 9 * C // per, wide.astype(BF)[None])


def run_attention(states, sums, weights, core, chips):
    ins, outs = [], []
    blocks = states[0][0].shape[0]
    parts = [state[0].shape[1] for state in states]
    for part, state in enumerate(states):
        for name, value in zip(STATE, state):
            if name not in ("xb", "dy"):
                ins.append((name + str(part), value, by_level(value.shape, 0)))
    mask = head_mask()
    ins += [
        (name + str(part), value, whole(value.shape))
        for part, both in enumerate(sums)
        for name, value in zip(("dense", "proj"), both)
    ]
    ins += [("mask", mask, whole(mask.shape))]
    ins += [(name, weights[name], whole(weights[name].shape)) for name in ("wqkv", "wup", "gains")]
    for part, count in enumerate(parts):
        shape = (blocks, count, M, C)
        for name in ("dq_out", "dk_out"):
            outs.append((name + str(part), shape, BF, by_level(shape, 0)))
    pack = (chips, 2048 // chips, 128)
    outs += [("keep_out", pack, BF, whole(pack)), ("send_out", pack, BF, whole(pack))]
    ins.append(("core", core, pl.BlockSpec(memory_space=pltpu.SMEM)))
    rows = sum(parts) * M
    scratch = [("acc", (3, C, C), F32), ("qbd", (4, LANES, C), BF)]
    scratch += [(name, (rows, C), BF) for name in ("h", "dq", "dk", "dv")]
    got = call(attention_kernel, blocks, ins, outs, scratch, "query_key_grads", 0.3, 60, parts)
    return [got[0:2], got[2:4]], got[4], got[5]


def finish_kernel(names, parts, cols, *refs):
    r = named(names, refs)
    local_rows = r.gt_out.shape[1]
    gain0 = r.gains[0:1, :]

    @pl.when(pl.program_id(0) == 0)
    def _():
        for i in range(3):
            r.w[i] = r.wqkv[:, C * i : C * (i + 1)]
        for name in ("own32", "lat32", "lon32", "corner32"):
            ref = getattr(r, name)
            ref[...] = jnp.zeros_like(ref)

    def window(at, part, t, place):
        get = lambda name: getattr(r, name + str(part)).at[0, t]
        dh = dot_nt(get("dq")[...], r.w[0]) + dot_nt(get("dk")[...], r.w[1]) + dot_nt(get("dv")[...], r.w[2])
        dh = dh.astype(BF).astype(F32)
        yield None
        n1, r1 = normalize(get("xb")[...].astype(F32))
        yield None
        r.gt[at] = get("dy")[...] + norm_back(n1, r1, gain0, dh)
        yield None
        for name, lead, start, length, slab in window_pieces(*place, local_rows, cols):
            target = getattr(r, name + "32")
            index = () if lead is None else (lead,)
            target[index + (slice(start, start + length),)] = r.gt[at, slab : slab + length, :]
        yield None

    order = [(part, t, place) for part, places in enumerate(parts) for t, place in enumerate(places)]
    for at in range(0, len(order), 2):
        in_turn(*[(4, window(at + i, *order[at + i])) for i in range(2)])
    r.gt_out[...] = r.own32[...].astype(BF).reshape(r.gt_out.shape)
    for i in range(HALF_LAT):
        for a in range(WLEV):
            row = a * HALF_LAT + i
            r.lat_out[a, i] = pack(r.lat32[row * cols : (row + 1) * cols, :])
        r.corner_out[0, i] = pack(jnp.concatenate([r.corner32[a * HALF_LAT + i] for a in range(WLEV)], axis=0))
    for i in range(HALF_LAT, local_rows):
        r.lon_out[0, i - HALF_LAT] = pack(
            jnp.concatenate([r.lon32[a * local_rows + i] for a in range(WLEV)], axis=0)
        )


def run_finish(parts, states, grads, weights, shape):
    levels, local_rows, cols, channels = shape
    blocks = levels // WLEV
    ins = []
    for part, (state, grad) in enumerate(zip(states, grads)):
        for name in ("dv", "xb", "dy"):
            value = state[STATE.index(name)]
            ins.append((name + str(part), value, by_level(value.shape, 0)))
        for name, value in zip(("dq", "dk"), grad):
            ins.append((name + str(part), value, by_level(value.shape, 0)))
    ins += [(name, weights[name], whole(weights[name].shape)) for name in ("wqkv", "gains")]
    outs = []
    for name, out in (
        ("gt_out", shape),
        ("lat_out", (levels, HALF_LAT, cols * 3 // 2, 128)),
        ("lon_out", (blocks, local_rows - HALF_LAT, HALO_ROWS, 128)),
        ("corner_out", (blocks, HALF_LAT, HALO_ROWS, 128)),
    ):
        outs.append((name, out, BF, by_level(out, 0)))
    count = sum(len(places) for places in parts)
    scratch = [
        ("w", (3, C, C), BF),
        ("gt", (count, M, C), F32),
        ("own32", (WLEV * local_rows * cols, C), F32),
        ("lat32", (WLEV * HALF_LAT * cols, C), F32),
        ("lon32", (WLEV * local_rows, HALO_COLS, C), F32),
        ("corner32", (WLEV * HALF_LAT, HALO_COLS, C), F32),
    ]
    return call(finish_kernel, blocks, ins, outs, scratch, "token_grads", 0.1, 60, parts, cols)


def cut_kernel(ids_ref, tok_rows, cot_rows, tok_cols, cot_cols, lat_ref, lon_ref, corner_ref):
    levels, half_lat, cols, channels = tok_rows.shape
    cell = lax.broadcasted_iota(jnp.int32, (cols, C), 0)
    for at, (rows, columns) in enumerate(((tok_rows, tok_cols), (cot_rows, cot_cols))):
        for a in range(levels):
            for i in range(half_lat):
                row = rows[a, i].astype(F32)
                if at == 0:
                    row = jnp.where(cell == 0, ids_ref[i].astype(F32), row)
                lat_ref[at, a, i] = pack(row)
        for p in range(levels // WLEV):
            for i in range(columns.shape[1]):
                both = [columns[WLEV * p + a, i, :HALO_COLS, :].astype(F32) for a in range(WLEV)]
                both = pack(jnp.concatenate(both, axis=0))
                if i < half_lat:
                    corner_ref[at, p, i] = both
                else:
                    lon_ref[at, p, i - half_lat] = both


def cut_halos(tokens, cotangent, region_ids):
    levels, local_rows, cols, channels = tokens.shape
    row_spec = pl.BlockSpec((levels, HALF_LAT, cols, C), lambda i: (0, 0, 0, 0))
    col_spec = pl.BlockSpec((levels, local_rows, 16, C), lambda i: (0, 0, 0, 0))
    blocks = levels // WLEV
    shapes = (
        (2, levels, HALF_LAT, cols * 3 // 2, 128),
        (2, blocks, local_rows - HALF_LAT, HALO_ROWS, 128),
        (2, blocks, HALF_LAT, HALO_ROWS, 128),
    )
    return pl.pallas_call(
        cut_kernel,
        grid=(1,),
        in_specs=[pl.BlockSpec(memory_space=pltpu.SMEM), row_spec, row_spec, col_spec, col_spec],
        out_specs=[whole(shape) for shape in shapes],
        out_shape=[jax.ShapeDtypeStruct(shape, BF) for shape in shapes],
        compiler_params=pltpu.CompilerParams(vmem_limit_bytes=60 * 1024 * 1024),
        name="cut_halos",
    )(region_ids, tokens, cotangent, tokens, cotangent)


def assemble_kernel(own_ref, lat_ref, lon_ref, corner_ref, out_ref):
    levels, local_rows, cols, channels = out_ref.shape
    keep = lax.broadcasted_iota(jnp.int32, (16, C), 0) >= HALF_LON
    pad = jnp.zeros((16 - HALO_COLS, C), F32)
    for p in range(levels // WLEV):
        for i in range(local_rows):
            both = unpack_cells(corner_ref[p, i] if i < HALF_LAT else lon_ref[p, i - HALF_LAT])
            for a in range(WLEV):
                level = WLEV * p + a
                left = jnp.concatenate([both[HALO_COLS * a : HALO_COLS * (a + 1)], pad], axis=0)
                if i < HALF_LAT:
                    row = unpack_cells(lat_ref[level, i])
                    out_ref[level, i, 16:, :] = row[16:].astype(BF)
                    first = row[:16]
                else:
                    out_ref[level, i, 16:, :] = own_ref[level, i, 16:, :]
                    first = own_ref[level, i, 0:16, :].astype(F32)
                out_ref[level, i, 0:16, :] = jnp.where(keep, first, left).astype(BF)


def assemble(own, *received):
    return pl.pallas_call(
        assemble_kernel,
        out_shape=jax.ShapeDtypeStruct(own.shape, BF),
        compiler_params=pltpu.CompilerParams(vmem_limit_bytes=32 * 1024 * 1024),
        name="assemble",
    )(own, *received)


def sum_kernel(in_ref, out_ref):
    total = jnp.sum(in_ref[...].astype(F32), axis=0, keepdims=True).astype(BF)
    out_ref[...] = jnp.broadcast_to(total, out_ref.shape)


def sum_pieces(pieces):
    return pl.pallas_call(
        sum_kernel,
        out_shape=jax.ShapeDtypeStruct(pieces.shape, BF),
        compiler_params=pltpu.CompilerParams(vmem_limit_bytes=32 * 1024 * 1024),
        name="sum_pieces",
    )(pieces)


def sum_bias_kernel(in_ref, out_ref):
    blocks, heads, share, bands, cells = out_ref.shape
    for p in range(blocks):
        for w in range(bands):
            total = jnp.sum(in_ref[:, p, w].astype(F32), axis=0)
            far = total[share * heads : share * (heads + 1)]
            for e in range(heads):
                near = total[share * e : share * (e + 1)]
                out_ref[p, e, :, w, :] = jnp.concatenate([near, far[:, REST * e : REST * (e + 1)]], axis=1)


def sum_bias(pieces, shape):
    return pl.pallas_call(
        sum_bias_kernel,
        out_shape=jax.ShapeDtypeStruct(shape, F32),
        compiler_params=pltpu.CompilerParams(vmem_limit_bytes=32 * 1024 * 1024),
        name="sum_bias",
    )(pieces)


def unpack_kernel(scale, core_ref, mine_ref, theirs_ref, qkv_ref, proj_ref, up_ref, down_ref, gains_ref, in_ref):
    core = core_ref[0]
    in_ref[core] = mine_ref[...]
    in_ref[1 - core] = theirs_ref[...]

    def tile(i):
        return in_ref[i // 9, C * (i % 9) : C * (i % 9 + 1), :].astype(F32) * scale

    half_qk, half_vp = tile(2), tile(5)
    qkv_ref[...] = jnp.concatenate(
        [tile(0), half_qk[:, :64], tile(1), half_qk[:, 64:], tile(3), half_vp[:, :64]], axis=1
    )
    proj_ref[...] = jnp.concatenate([tile(4), half_vp[:, 64:]], axis=1)
    for i in range(FF // 128):
        up_ref[:, 128 * i : 128 * (i + 1)] = tile(6 + i)
        down_ref[:, 128 * i : 128 * (i + 1)] = tile(12 + i)
    wide = in_ref[0, 9 * C : 9 * C + 16, :].astype(F32) * scale
    gains_ref[...] = jnp.concatenate([wide[0:2, :], wide[8:10, :64]], axis=1)


def unpack(core, mine, theirs, scale):
    shapes = ((C, 3 * C), (C, C), (C, FF), (C, FF), (2, C))
    return pl.pallas_call(
        functools.partial(unpack_kernel, scale),
        out_shape=[jax.ShapeDtypeStruct(s, F32) for s in shapes],
        in_specs=[pl.BlockSpec(memory_space=pltpu.SMEM), pl.BlockSpec(memory_space=pltpu.VMEM), pl.BlockSpec(memory_space=pltpu.VMEM)],
        scratch_shapes=[pltpu.VMEM((2,) + mine.shape, BF)],
        compiler_params=pltpu.CompilerParams(vmem_limit_bytes=32 * 1024 * 1024),
        name="unpack_sums",
    )(core, mine, theirs)


def local(tokens, cotangent, region_ids, norm_gains, w_qkv, w_proj, w_up, w_down, earth_bias):
    levels, nrows, cols, channels = tokens.shape
    both = ("lon", "lat")
    lons, lats = lax.axis_size("lon"), lax.axis_size("lat")
    devices = lons * lats

    def corner_perm(value, steps):
        pairs = [
            (a * lats + b, (a + steps) % lons * lats + (b + steps) % lats)
            for a in range(lons)
            for b in range(lats)
        ]
        return lax.ppermute(value, both, pairs)

    lat_cut, lon_cut, corner_cut = cut_halos(tokens, cotangent, region_ids)
    halos = (perm(lat_cut, "lat", -1), perm(lon_cut, "lon", -1), corner_perm(corner_cut, -1))

    weights = {"wqkv": w_qkv, "wp": w_proj, "wup": w_up, "wdt": w_down.T, "gains": norm_gains}
    inner, inner_sums = run_forward(INNER, tokens, cotangent, earth_bias, region_ids, weights)
    edge, sums = run_forward(EDGE, tokens, cotangent, earth_bias, region_ids, weights, halos, inner_sums[2], lons)

    shares = lax.all_to_all(sums[2], "lon", 0, 0, tiled=True)
    states = (inner, edge)
    core = lax.rem(lax.axis_index("lat"), 2)[None]
    cores = [[d for d in range(devices) if d % 2 == c] for c in range(2)]

    def other_core(value):
        return lax.ppermute(value, "lat", [(i, i ^ 1) for i in range(lats)])

    def exchange(value):
        return lax.all_to_all(value, both, 0, 0, axis_index_groups=cores, tiled=True)

    grads, keep, send = run_attention(states, (inner_sums[:2], sums[:2]), weights, core, devices // 2)
    packed = (keep.astype(F32) + other_core(send).astype(F32)).astype(BF)
    own, *sent = run_finish((INNER, EDGE), states, grads, weights, tokens.shape)
    packed, shares = lax.optimization_barrier((packed, shares))
    pieces = exchange(packed)
    lat_in = perm(sent[0], "lat", 1)
    lon_in = perm(sent[1], "lon", 1)
    corner_in = corner_perm(sent[2], 1)
    summed, own = lax.optimization_barrier((sum_pieces(pieces), own))
    mine = exchange(summed).reshape(-1, 128)
    grad_tokens = assemble(own, lat_in, lon_in, corner_in)
    mine, grad_tokens = lax.optimization_barrier((mine, grad_tokens))
    cell_count = levels * nrows * cols * devices
    weight_grads = unpack(core, mine, other_core(mine), 1.0 / math.sqrt(cell_count))
    blocks, bands = earth_bias.shape[:2]
    bias_total = sum_bias(shares, (blocks, HEADS, M // lons, bands, M)).transpose(0, 3, 1, 2, 4)
    qkv, proj, up, down, gains = weight_grads
    return (grad_tokens, qkv, proj, up, down.T, gains, bias_total)


def solution(mesh):
    placed = (
        P(None, "lat", "lon", None),
        P(None, "lat", "lon", None),
        P("lat"),
        P(),
        P(),
        P(),
        P(),
        P(),
        P(None, "lat", None, None, None),
    )
    return jax.shard_map(
        local,
        mesh=mesh,
        in_specs=placed,
        out_specs=(
            P(None, "lat", "lon", None),
            P(),
            P(),
            P(),
            P(),
            P(),
            P(None, "lat", None, "lon", None),
        ),
        check_vma=False,
    )
```

```python
import functools
import math

import jax
import jax.numpy as jnp
import numpy as np
from jax import lax
from jax.experimental import pallas as pl
from jax.experimental.pallas import tpu as pltpu
from jax.sharding import PartitionSpec as P

HEADS = 6
HEAD = 32
WLEV = 2
WLAT = 6
WLON = 12
C = HEADS * HEAD
FF = 4 * C
M = WLEV * WLAT * WLON
MAIN = 128
REST = M - MAIN
LANES = (HEADS + 1) * 128
SLABS = WLEV * WLAT

BF = jnp.bfloat16
F32 = jnp.float32
epsilon = 1e-05
inv_root_two = 0.7071067811865476
inv_root_tau = 0.3989422804014327


def perm(value, axis, steps):
    count = lax.axis_size(axis)
    pairs = [(source, (source + steps) % count) for source in range(count)]
    return lax.ppermute(value, axis, pairs)


def dot(left, right):
    return jnp.dot(left, right, preferred_element_type=F32)


def dot_nt(left, right):
    return lax.dot_general(left, right, (((1,), (1,)), ((), ())), preferred_element_type=F32)


def dot_tn(left, right):
    return lax.dot_general(left, right, (((0,), (0,)), ((), ())), preferred_element_type=F32)


def normalize(values):
    centred = values - jnp.mean(values, axis=-1, keepdims=True)
    inverse = lax.rsqrt(jnp.mean(centred * centred, axis=-1, keepdims=True) + epsilon)
    return centred * inverse, inverse


def norm_back(normed, inverse, gain_row, upstream):
    scaled = upstream * gain_row
    return inverse * (
        scaled
        - jnp.mean(scaled, axis=-1, keepdims=True)
        - normed * jnp.mean(scaled * normed, axis=-1, keepdims=True)
    )


def gelu_parts(u):
    cdf = 0.5 + 0.5 * lax.erf(u * inv_root_two)
    bell = jnp.exp2(u * u * (-0.5 * math.log2(math.e)))
    return cdf, cdf + u * (bell * inv_root_tau)


CHUNKS = ((0, 256), (256, 512), (512, 768), (768, 896))


def spread_heads(rows, mask):
    first, last = rows[:MAIN], rows[MAIN:]
    return jnp.concatenate([first] * HEADS + [last] * 8, axis=0) * mask


def per_query(weights_ref, right, right_t, rest_mask):
    parts = []
    for e in range(HEADS):
        parts.append(
            dot(
                right_t[HEAD * e : HEAD * (e + 1), :],
                weights_ref[:, 128 * e : 128 * (e + 1)],
            )
        )
        if e % 2:
            yield None
    first = jnp.concatenate(parts, axis=0).T
    yield None
    last = dot_tn(weights_ref[:, HEADS * 128 :], right) * rest_mask
    total = last[0:REST]
    for e in range(1, HEADS):
        total = total + last[REST * e : REST * (e + 1)]
    yield jnp.concatenate([first, total], axis=0)


def in_turn(*streams):
    streams = [[0, count, pieces] for count, pieces in streams]
    while streams:
        stream = min(streams, key=lambda entry: entry[0] / entry[1])
        stream[0] += 1
        if next(stream[2], streams) is streams:
            streams.remove(stream)


def chain(*streams):
    for stream in streams:
        for piece in stream:
            yield None


def run_events(events):
    tick = 0
    while events:
        for event in list(events):
            start, pieces, stream = event
            for i in range(pieces if start <= tick else 0):
                if next(stream, events) is events:
                    events.remove(event)
                    break
        tick += 1


INNER = ((0, 0), (0, 1), (0, 2))
EDGE = ((0, 3), (1, 0), (1, 1), (1, 2), (1, 3))
STATE = ("ds", "q", "k", "h", "dv", "xb", "dy")
HALF_LAT = WLAT // 2
HALF_LON = WLON // 2
HALO_COLS = 8


HALO_ROWS = 3 * HALO_COLS


class Refs:
    pass


def pack(cells):
    half = cells.shape[0] // 2
    ends = jnp.concatenate([cells[:half, 128:], cells[half:, 128:]], axis=1)
    return jnp.concatenate([cells[:, :128], ends], axis=0).astype(BF)


def unpack_cells(packed):
    packed = packed.astype(F32)
    first = packed.shape[0] * 2 // 3
    ends = jnp.concatenate([packed[first:, :64], packed[first:, 64:]], axis=0)
    return jnp.concatenate([packed[:first], ends], axis=1)


def named(names, refs):
    r = Refs()
    for name, ref in zip(names, refs):
        setattr(r, name, ref)
    return r


def window_pieces(w, n, local_rows, cols):
    for a in range(WLEV):
        for b in range(WLAT):
            slab = (a * WLAT + b) * WLON
            i = HALF_LAT + w * WLAT + b
            j = HALF_LON + n * WLON
            own = min(WLON, cols - j)
            if i < local_rows:
                yield "own", None, (a * local_rows + i) * cols + j, own, slab
                if own < WLON:
                    yield "lon", a * local_rows + i, 0, WLON - own, slab + own
            else:
                i = i - local_rows
                yield "lat", None, (a * HALF_LAT + i) * cols + j, own, slab
                if own < WLON:
                    yield "corner", a * HALF_LAT + i, 0, WLON - own, slab + own


def forward_kernel(names, places, cols, *refs):
    r = named(names, refs)
    edge = hasattr(r, "halo_lat")
    bands = sorted({w for w, n in places})
    step = pl.program_id(0)
    last_step = pl.num_programs(0) - 1

    @pl.when(step == 0)
    def _():
        if edge:
            r.share32[...] = jnp.zeros_like(r.share32)
        r.acc[...] = jnp.zeros_like(r.acc)
        r.proj[...] = jnp.zeros_like(r.proj)
        r.wq[...] = r.wqkv[:, 0:C]
        r.wk[...] = r.wqkv[:, C : 2 * C]
        r.wv[...] = r.wqkv[:, 2 * C : 3 * C]

    gain0 = r.gains[0:1, :]
    gain1 = r.gains[1:2, :]
    scaling = float(HEAD) ** -0.5

    local_rows = r.tok.shape[1]

    def widen(w):
        for at, ref in enumerate((r.tok, r.cot)):
            first = HALF_LAT + w * WLAT
            stop = min(first + WLAT, local_rows)
            for a in range(WLEV):
                for i in range(first, stop):
                    row = a * local_rows + i
                    r.own32[at, row * cols : (row + 1) * cols, :] = ref[a, i].astype(F32)
                yield None
            for i in range(first, stop if edge else first):
                both = unpack_cells(r.halo_lon[at, 0, i - HALF_LAT])
                for a in range(WLEV):
                    r.lon32[at, a * local_rows + i] = both[HALO_COLS * a : HALO_COLS * (a + 1)]
            if stop < first + WLAT:
                for i in range(HALF_LAT):
                    both = unpack_cells(r.halo_corner[at, 0, i])
                    for a in range(WLEV):
                        row = a * HALF_LAT + i
                        r.lat32[at, row * cols : (row + 1) * cols, :] = unpack_cells(r.halo_lat[at, a, i])
                        r.corner32[at, row] = both[HALO_COLS * a : HALO_COLS * (a + 1)]
                yield None

    def row_id(w, b):
        i = HALF_LAT + w * WLAT + b
        if i < local_rows:
            return r.ids[i].astype(F32)
        return r.halo_lat[0, 0, i - local_rows, 0:1, 0:1].astype(F32)

    def bias_rows(at, w):
        kid = jnp.zeros((M, 1), F32)
        qid = jnp.zeros((1, LANES), F32)
        for b in range(WLAT):
            kid = jnp.where(r.krow[...] == b, row_id(w, b), kid)
            qid = jnp.where(r.qrow[...] == b, row_id(w, b), qid)
        rest_pad = jnp.zeros((128 - HEADS * REST, M), F32)
        rest = jnp.concatenate([r.bias[0, at, e, MAIN:, :] for e in range(HEADS)] + [rest_pad], axis=0)
        for e in range(HEADS + 1):
            block = r.bias[0, at, e, :MAIN, :] if e < HEADS else rest
            lanes = slice(128 * e, 128 * (e + 1))
            r.biast[at, :, lanes] = jnp.where(kid == qid[:, lanes], block.T, -1e30)
            yield None
        if edge and w == 0:
            r.gbt[at] = r.gbt_in[0]
        else:
            r.gbt[at] = jnp.zeros((M, LANES), F32)
        yield None

    rest_mask = r.mask[HEADS * 128 :, :].astype(F32)

    def front(t):
        w, n = places[t]
        band = bands.index(w)
        here = slice(t * M, (t + 1) * M)
        for at, to in ((0, r.x), (1, r.c)):
            for name, lead, start, length, slab in window_pieces(w, n, local_rows, cols):
                source = getattr(r, name + "32")
                index = (at,) if lead is None else (at, lead)
                to[t * M + slab : t * M + slab + length, :] = source[index + (slice(start, start + length),)]
            yield None
        x = r.x[here, :]
        r.xb[0, t] = x.astype(BF)
        h = (normalize(x)[0] * gain0).astype(BF)
        r.h[0, t] = h
        yield None
        q = (dot(h, r.wq[...]) * scaling).astype(BF)
        r.q[0, t] = q
        r.qbd[t] = spread_heads(q, r.mask[...])
        yield None
        r.k[0, t] = dot(h, r.wk[...]).astype(BF)
        yield None
        v32 = dot(h, r.wv[...])
        r.v[here, :] = v32.astype(BF)
        vt = v32.T.astype(BF)
        yield None
        for lo, hi in CHUNKS:
            scores = dot_nt(r.k[0, t], r.qbd[t, lo:hi, :]) + r.biast[band, :, lo:hi]
            powers = jnp.exp(scores - jnp.max(scores, axis=0, keepdims=True))
            weights = powers * pl.reciprocal(jnp.sum(powers, axis=0, keepdims=True), approx=True)
            r.p[t, :, lo:hi] = weights
            r.pb[t, :, lo:hi] = weights.astype(BF)
            yield None
        for o in per_query(r.pb.at[t], r.v[here, :], vt, rest_mask):
            yield None
        o = o.astype(BF)
        r.o[here, :] = o
        y = r.x[here, :] + dot(o, r.wp[...]).astype(BF).astype(F32)
        yield None
        n2, r2 = normalize(y)
        r.n2[here, :] = n2
        r.r2[here, :] = r2
        r.g[here, :] = (n2 * gain1).astype(BF)
        r.cb[here, :] = r.c[here, :].astype(BF)
        yield None

    def middle(t):
        here = slice(t * M, (t + 1) * M)
        for lo in range(0, FF, 256):
            part = slice(lo, lo + 256)
            u = dot(r.g[here, :], r.wup[:, part])
            cdf, slope = gelu_parts(u)
            r.act[here, part] = (u * cdf).astype(BF)
            yield None
            r.du[here, part] = (dot(r.cb[here, :], r.wdt[:, part]) * slope).astype(BF)
            yield None

    def back(t):
        w, n = places[t]
        band = bands.index(w)
        here = slice(t * M, (t + 1) * M)
        dg = dot_nt(r.du[here, :], r.wup[...])
        yield None
        dy = r.c[here, :] + norm_back(r.n2[here, :], r.r2[here, :], gain1, dg)
        r.dy[0, t] = dy
        dys = dy.astype(BF)
        r.dys[here, :] = dys
        yield None
        do = dot_nt(dys, r.wp[...]).astype(BF)
        r.dobd[t] = spread_heads(do, r.mask[...])
        yield None
        for lo, hi in CHUNKS:
            weights = r.p[t, :, lo:hi]
            dp = dot_nt(r.v[here, :], r.dobd[t, lo:hi, :]) * weights
            ds = dp - weights * jnp.sum(dp, axis=0, keepdims=True)
            r.gbt[band, :, lo:hi] += ds
            r.ds[0, t, :, lo:hi] = ds.astype(BF)
            yield None
        r.dv[0, t] = dot(r.pb[t], r.dobd[t]).astype(BF)
        yield None

    def sums(t):
        here = slice(t * M, (t + 1) * M)
        for first, left, right in ((0, r.g, r.du), (6, r.cb, r.act)):
            left_t = left[here, :].T
            for lo in range(0, FF, 256):
                part = dot(left_t, right[here, lo : lo + 256])
                r.acc[first + lo // 128] += part[:, :128]
                r.acc[first + lo // 128 + 1] += part[:, 128:]
                yield None

    def proj_sum():
        r.proj[...] += dot_tn(r.o[...], r.dys[...])
        yield None

    def share_bias(at):
        share = M // r.share_out.shape[0]
        gbt = r.gbt.at[at]
        last = gbt[:, HEADS * 128 :].T
        for e in range(HEADS):
            r.bias32[at, M * e : M * e + MAIN, :] = gbt[:, 128 * e : 128 * (e + 1)].T[:, :MAIN]
            r.bias32[at, M * e + MAIN : M * (e + 1), :] = last[REST * e : REST * (e + 1), :MAIN]
            yield None
        far = jnp.concatenate(
            [gbt[MAIN:, 128 * e : 128 * (e + 1)] for e in range(HEADS)]
            + [jnp.zeros((128 - HEADS * REST, 128), F32)],
            axis=0,
        )
        r.bias32[at, M * HEADS : M * HEADS + MAIN, :] = far.T
        r.bias32[at, M * HEADS + MAIN : M * (HEADS + 1), :] = jnp.concatenate(
            [last[REST * e : REST * (e + 1), MAIN:] for e in range(HEADS)]
            + [jnp.zeros((REST, 128 - HEADS * REST), F32)],
            axis=1,
        )
        yield None
        for d in range(r.share_out.shape[0]):
            for e in range(HEADS + 1):
                r.share32[at, d, share * e : share * (e + 1), :] = r.bias32[
                    at, M * e + share * d : M * e + share * (d + 1), :
                ]
            r.share_out[d, 0, at] = r.share32[at, d].astype(BF)
            yield None

    count = len(places)
    length = 31
    events = [(0, 2, widen(bands[0])), (0, 3, bias_rows(0, bands[0]))]
    events += [(1, 2, widen(w)) for w in bands[1:]]
    events += [(2, 2, bias_rows(at, bands[at])) for at in range(1, len(bands))]
    start = [3 + (3 if edge else 2) * t for t in range(count)]
    for t in range(count):
        events.append((start[t], 1, chain(front(t), middle(t), back(t))))
        events.append((start[t] + 22, 1, sums(t)))
    for at in range(len(bands)):
        last = max(t for t, place in enumerate(places) if place[0] == bands[at])
        if edge:
            events.append((start[last] + length + 1, 2, share_bias(at)))
    events.append((start[-1] + length + 1, 1, proj_sum()))
    run_events(events)

    if not edge:
        r.gbt_out[0] = r.gbt[0]

    @pl.when(step == last_step)
    def _():
        r.acc_out[...] = r.acc[...]
        r.proj_out[...] = r.proj[...]


def whole(shape):
    zeros = (0,) * len(shape)
    return pl.BlockSpec(tuple(shape), lambda p: zeros)


def by_level(shape, at, blocks=2):
    block = list(shape)
    block[at] = shape[at] // blocks
    return pl.BlockSpec(tuple(block), lambda p: tuple(p if i == at else 0 for i in range(len(shape))))


def call(kernel, blocks, ins, outs, scratch, name, share_of, limit, *fixed):
    names = [i[0] for i in ins] + [o[0] for o in outs] + [s[0] for s in scratch]
    return pl.pallas_call(
        functools.partial(kernel, names, *fixed),
        grid=(blocks,),
        in_specs=[i[2] for i in ins],
        out_specs=[o[3] for o in outs],
        out_shape=[jax.ShapeDtypeStruct(tuple(o[1]), o[2]) for o in outs],
        scratch_shapes=[pltpu.VMEM(tuple(s[1]), s[2]) for s in scratch],
        compiler_params=pltpu.CompilerParams(
            vmem_limit_bytes=limit * 1024 * 1024,
            dimension_semantics=("arbitrary",),
        ),
        cost_estimate=pl.CostEstimate(
            flops=int(14e9 * share_of), bytes_accessed=int(10e6 * share_of), transcendentals=int(5e6 * share_of)
        ),
        name=name,
    )(*[i[1] for i in ins])


def head_mask():
    head_of_row = np.concatenate(
        [
            np.repeat(np.arange(HEADS), MAIN),
            np.repeat(np.arange(HEADS), REST),
            np.full(128 - HEADS * REST, -1),
        ]
    )
    return jnp.asarray(head_of_row[:, None] == np.arange(C)[None, :] // HEAD, BF)


def run_forward(places, tokens, cotangent, bias, region_ids, weights, halos=None, before=None, lons=8):
    levels, local_rows, cols, channels = tokens.shape
    blocks = levels // WLEV
    count = len(places)
    rows = count * M
    bands = len({w for w, n in places})
    cell_row = (np.arange(M) // WLON % WLAT).astype(np.int32)
    rest = np.concatenate([np.tile(np.arange(MAIN, M), HEADS), np.zeros(128 - HEADS * REST, int)])
    lane_cell = np.concatenate([np.tile(np.arange(MAIN), HEADS), rest])
    edge = halos is not None
    ins = [
        ("tok", tokens, by_level(tokens.shape, 0)),
        ("cot", cotangent, by_level(tokens.shape, 0)),
        ("bias", bias, pl.BlockSpec((1, bands, HEADS, M, M), lambda p: (p, 0, 0, 0, 0))),
        ("ids", region_ids, pl.BlockSpec(memory_space=pltpu.SMEM)),
        ("krow", jnp.asarray(cell_row[:, None]), whole((M, 1))),
        ("qrow", jnp.asarray(cell_row[lane_cell][None, :]), whole((1, LANES))),
        ("mask", head_mask(), whole((LANES, C))),
    ] + [(name, w, whole(w.shape)) for name, w in weights.items()]
    flat = WLEV * local_rows * cols
    acc = (12, C, 128)
    scratch = [
        ("own32", (2, flat, C), F32),
        ("x", (rows, C), F32),
        ("c", (rows, C), F32),
        ("n2", (rows, C), F32),
        ("r2", (rows, 1), F32),
        ("biast", (bands, M, LANES), F32),
        ("gbt", (bands, M, LANES), F32),
        ("p", (count, M, LANES), F32),
        ("pb", (count, M, LANES), BF),
        ("qbd", (count, LANES, C), BF),
        ("dobd", (count, LANES, C), BF),
        ("acc", acc, F32),
        ("proj", (C, C), F32),
        ("act", (rows, FF), BF),
        ("du", (rows, FF), BF),
    ] + [(name, (rows, C), BF) for name in ("v", "o", "g", "cb", "dys")]
    scratch += [(name, (C, C), BF) for name in ("wq", "wk", "wv")]
    outs = []
    for name in STATE:
        shape = (blocks, count, M, LANES if name == "ds" else C)
        outs.append((name, shape, F32 if name == "dy" else BF, by_level(shape, 0)))
    outs += [("acc_out", acc, F32, whole(acc)), ("proj_out", (C, C), F32, whole((C, C)))]
    if edge:
        for name, value in zip(("halo_lat", "halo_lon", "halo_corner"), halos):
            ins.append((name, value, by_level(value.shape, 1)))
        ins.append(("gbt_in", before, by_level(before.shape, 0)))
        share = (lons, blocks, bands, 128, 128)
        outs.append(("share_out", share, BF, by_level(share, 1)))
        scratch += [
            ("lat32", (2, WLEV * HALF_LAT * cols, C), F32),
            ("lon32", (2, WLEV * local_rows, HALO_COLS, C), F32),
            ("corner32", (2, WLEV * HALF_LAT, HALO_COLS, C), F32),
            ("bias32", (bands, M * (HEADS + 1), 128), F32),
            ("share32", (bands, lons, 128, 128), F32),
        ]
    else:
        outs.append(("gbt_out", (blocks, M, LANES), F32, by_level((blocks, M, LANES), 0)))
    name = "edge_windows" if edge else "inner_windows"
    got = call(forward_kernel, blocks, ins, outs, scratch, name, count * blocks / 20, 60, places, cols)
    return got[: len(STATE)], got[len(STATE) :]


def attention_kernel(names, parts, *refs):
    r = named(names, refs)
    step = pl.program_id(0)
    last_step = pl.num_programs(0) - 1
    scaling = float(HEAD) ** -0.5
    rest_mask = r.mask[HEADS * 128 :, :].astype(F32)

    @pl.when(step == 0)
    def _():
        r.acc[...] = jnp.zeros_like(r.acc)

    def window(at, part, t):
        here = slice(at * M, (at + 1) * M)
        get = lambda name: getattr(r, name + str(part)).at[0, t]
        r.h[here, :] = get("h")[...]
        r.dv[here, :] = get("dv")[...]
        r.qbd[at % 4] = spread_heads(get("q")[...], r.mask[...])
        yield None
        k = get("k")[...]
        kt = k.astype(F32).T.astype(BF)
        yield None
        dk = dot(get("ds")[...], r.qbd[at % 4]).astype(BF)
        r.dk[here, :] = dk
        getattr(r, "dk_out" + str(part))[0, t] = dk
        yield None
        for dq in per_query(get("ds"), k, kt, rest_mask):
            yield None
        dq = (dq * scaling).astype(BF)
        r.dq[here, :] = dq
        getattr(r, "dq_out" + str(part))[0, t] = dq
        yield None

    order = [(part, t) for part, count in enumerate(parts) for t in range(count)]
    for at in range(0, len(order), 2):
        in_turn(*[(9, window(at + i, *order[at + i])) for i in range(2)])
    ht = r.h[...].T
    for i, right in enumerate((r.dq, r.dk, r.dv)):
        r.acc[i] += dot(ht, right[...])

    @pl.when(step == last_step)
    def _():
        per = r.keep_out.shape[1]
        core = r.core[0]

        def put_rows(half, at, rows):
            for ref, here in ((r.keep_out, core == half), (r.send_out, core != half)):

                @pl.when(here)
                def _():
                    ref[at : at + rows.shape[0]] = rows

        def put(i, tile):
            put_rows(i // 9, C // per * (i % 9), tile.astype(BF).reshape(C // per, per, 128))

        small = (r.acc[0], r.acc[1], r.acc[2], r.proj0[...] + r.proj1[...])
        for i in range(2):
            one, two = small[2 * i], small[2 * i + 1]
            put(3 * i, one[:, :128])
            put(3 * i + 1, two[:, :128])
            put(3 * i + 2, jnp.concatenate([one[:, 128:], two[:, 128:]], axis=1))
        for i in range(12):
            put(6 + i, r.dense0[i] + r.dense1[i])
        first = jnp.zeros((C, C), F32)
        for i in range(3):
            first = first + r.acc[i] * r.wqkv[:, C * i : C * (i + 1)].astype(F32)
        second = jnp.zeros((C, 128), F32)
        for i in range(6):
            second = second + (r.dense0[i] + r.dense1[i]) * r.wup[:, 128 * i : 128 * (i + 1)].astype(F32)
        sums = [jnp.sum(part.T, axis=0, keepdims=True) for part in (first, second)]
        gains = jnp.concatenate([sums[0] / r.gains[0:1, :], sums[1] / r.gains[1:2, :], jnp.zeros((6, C), F32)], axis=0)
        wide = jnp.concatenate(
            [gains[:, :128], jnp.concatenate([gains[:, 128:], jnp.zeros((8, 64), F32)], axis=1)],
            axis=0,
        )
        wide = jnp.concatenate([wide, jnp.zeros((per - 16, 128), F32)], axis=0)
        put_rows(0, 9 * C // per, wide.astype(BF)[None])


def run_attention(states, sums, weights, core, chips):
    ins, outs = [], []
    blocks = states[0][0].shape[0]
    parts = [state[0].shape[1] for state in states]
    for part, state in enumerate(states):
        for name, value in zip(STATE, state):
            if name not in ("xb", "dy"):
                ins.append((name + str(part), value, by_level(value.shape, 0)))
    mask = head_mask()
    ins += [
        (name + str(part), value, whole(value.shape))
        for part, both in enumerate(sums)
        for name, value in zip(("dense", "proj"), both)
    ]
    ins += [("mask", mask, whole(mask.shape))]
    ins += [(name, weights[name], whole(weights[name].shape)) for name in ("wqkv", "wup", "gains")]
    for part, count in enumerate(parts):
        shape = (blocks, count, M, C)
        for name in ("dq_out", "dk_out"):
            outs.append((name + str(part), shape, BF, by_level(shape, 0)))
    pack = (chips, 2048 // chips, 128)
    outs += [("keep_out", pack, BF, whole(pack)), ("send_out", pack, BF, whole(pack))]
    ins.append(("core", core, pl.BlockSpec(memory_space=pltpu.SMEM)))
    rows = sum(parts) * M
    scratch = [("acc", (3, C, C), F32), ("qbd", (4, LANES, C), BF)]
    scratch += [(name, (rows, C), BF) for name in ("h", "dq", "dk", "dv")]
    got = call(attention_kernel, blocks, ins, outs, scratch, "query_key_grads", 0.3, 60, parts)
    return [got[0:2], got[2:4]], got[4], got[5]


def finish_kernel(names, parts, cols, *refs):
    r = named(names, refs)
    local_rows = r.gt_out.shape[1]
    gain0 = r.gains[0:1, :]

    @pl.when(pl.program_id(0) == 0)
    def _():
        for i in range(3):
            r.w[i] = r.wqkv[:, C * i : C * (i + 1)]
        for name in ("own32", "lat32", "lon32", "corner32"):
            ref = getattr(r, name)
            ref[...] = jnp.zeros_like(ref)

    def window(at, part, t, place):
        get = lambda name: getattr(r, name + str(part)).at[0, t]
        dh = dot_nt(get("dq")[...], r.w[0]) + dot_nt(get("dk")[...], r.w[1]) + dot_nt(get("dv")[...], r.w[2])
        dh = dh.astype(BF).astype(F32)
        yield None
        n1, r1 = normalize(get("xb")[...].astype(F32))
        yield None
        r.gt[at] = get("dy")[...] + norm_back(n1, r1, gain0, dh)
        yield None
        for name, lead, start, length, slab in window_pieces(*place, local_rows, cols):
            target = getattr(r, name + "32")
            index = () if lead is None else (lead,)
            target[index + (slice(start, start + length),)] = r.gt[at, slab : slab + length, :]
        yield None

    order = [(part, t, place) for part, places in enumerate(parts) for t, place in enumerate(places)]
    for at in range(0, len(order), 2):
        in_turn(*[(4, window(at + i, *order[at + i])) for i in range(2)])
    r.gt_out[...] = r.own32[...].astype(BF).reshape(r.gt_out.shape)
    for i in range(HALF_LAT):
        for a in range(WLEV):
            row = a * HALF_LAT + i
            r.lat_out[a, i] = pack(r.lat32[row * cols : (row + 1) * cols, :])
        r.corner_out[0, i] = pack(jnp.concatenate([r.corner32[a * HALF_LAT + i] for a in range(WLEV)], axis=0))
    for i in range(HALF_LAT, local_rows):
        r.lon_out[0, i - HALF_LAT] = pack(
            jnp.concatenate([r.lon32[a * local_rows + i] for a in range(WLEV)], axis=0)
        )


def run_finish(parts, states, grads, weights, shape):
    levels, local_rows, cols, channels = shape
    blocks = levels // WLEV
    ins = []
    for part, (state, grad) in enumerate(zip(states, grads)):
        for name in ("dv", "xb", "dy"):
            value = state[STATE.index(name)]
            ins.append((name + str(part), value, by_level(value.shape, 0)))
        for name, value in zip(("dq", "dk"), grad):
            ins.append((name + str(part), value, by_level(value.shape, 0)))
    ins += [(name, weights[name], whole(weights[name].shape)) for name in ("wqkv", "gains")]
    outs = []
    for name, out in (
        ("gt_out", shape),
        ("lat_out", (levels, HALF_LAT, cols * 3 // 2, 128)),
        ("lon_out", (blocks, local_rows - HALF_LAT, HALO_ROWS, 128)),
        ("corner_out", (blocks, HALF_LAT, HALO_ROWS, 128)),
    ):
        outs.append((name, out, BF, by_level(out, 0)))
    count = sum(len(places) for places in parts)
    scratch = [
        ("w", (3, C, C), BF),
        ("gt", (count, M, C), F32),
        ("own32", (WLEV * local_rows * cols, C), F32),
        ("lat32", (WLEV * HALF_LAT * cols, C), F32),
        ("lon32", (WLEV * local_rows, HALO_COLS, C), F32),
        ("corner32", (WLEV * HALF_LAT, HALO_COLS, C), F32),
    ]
    return call(finish_kernel, blocks, ins, outs, scratch, "token_grads", 0.1, 60, parts, cols)


def cut_kernel(ids_ref, tok_rows, cot_rows, tok_cols, cot_cols, lat_ref, lon_ref, corner_ref):
    levels, half_lat, cols, channels = tok_rows.shape
    cell = lax.broadcasted_iota(jnp.int32, (cols, C), 0)
    for at, (rows, columns) in enumerate(((tok_rows, tok_cols), (cot_rows, cot_cols))):
        for a in range(levels):
            for i in range(half_lat):
                row = rows[a, i].astype(F32)
                if at == 0:
                    row = jnp.where(cell == 0, ids_ref[i].astype(F32), row)
                lat_ref[at, a, i] = pack(row)
        for p in range(levels // WLEV):
            for i in range(columns.shape[1]):
                both = [columns[WLEV * p + a, i, :HALO_COLS, :].astype(F32) for a in range(WLEV)]
                both = pack(jnp.concatenate(both, axis=0))
                if i < half_lat:
                    corner_ref[at, p, i] = both
                else:
                    lon_ref[at, p, i - half_lat] = both


def cut_halos(tokens, cotangent, region_ids):
    levels, local_rows, cols, channels = tokens.shape
    row_spec = pl.BlockSpec((levels, HALF_LAT, cols, C), lambda i: (0, 0, 0, 0))
    col_spec = pl.BlockSpec((levels, local_rows, 16, C), lambda i: (0, 0, 0, 0))
    blocks = levels // WLEV
    shapes = (
        (2, levels, HALF_LAT, cols * 3 // 2, 128),
        (2, blocks, local_rows - HALF_LAT, HALO_ROWS, 128),
        (2, blocks, HALF_LAT, HALO_ROWS, 128),
    )
    return pl.pallas_call(
        cut_kernel,
        grid=(1,),
        in_specs=[pl.BlockSpec(memory_space=pltpu.SMEM), row_spec, row_spec, col_spec, col_spec],
        out_specs=[whole(shape) for shape in shapes],
        out_shape=[jax.ShapeDtypeStruct(shape, BF) for shape in shapes],
        compiler_params=pltpu.CompilerParams(vmem_limit_bytes=60 * 1024 * 1024),
        name="cut_halos",
    )(region_ids, tokens, cotangent, tokens, cotangent)


def assemble_kernel(own_ref, lat_ref, lon_ref, corner_ref, out_ref):
    levels, local_rows, cols, channels = out_ref.shape
    keep = lax.broadcasted_iota(jnp.int32, (16, C), 0) >= HALF_LON
    pad = jnp.zeros((16 - HALO_COLS, C), F32)
    for p in range(levels // WLEV):
        for i in range(local_rows):
            both = unpack_cells(corner_ref[p, i] if i < HALF_LAT else lon_ref[p, i - HALF_LAT])
            for a in range(WLEV):
                level = WLEV * p + a
                left = jnp.concatenate([both[HALO_COLS * a : HALO_COLS * (a + 1)], pad], axis=0)
                if i < HALF_LAT:
                    row = unpack_cells(lat_ref[level, i])
                    out_ref[level, i, 16:, :] = row[16:].astype(BF)
                    first = row[:16]
                else:
                    out_ref[level, i, 16:, :] = own_ref[level, i, 16:, :]
                    first = own_ref[level, i, 0:16, :].astype(F32)
                out_ref[level, i, 0:16, :] = jnp.where(keep, first, left).astype(BF)


def assemble(own, *received):
    return pl.pallas_call(
        assemble_kernel,
        out_shape=jax.ShapeDtypeStruct(own.shape, BF),
        compiler_params=pltpu.CompilerParams(vmem_limit_bytes=32 * 1024 * 1024),
        name="assemble",
    )(own, *received)


def add_kernel(one_ref, two_ref, out_ref):
    out_ref[...] = (one_ref[...].astype(F32) + two_ref[...].astype(F32)).astype(BF)


def add_halves(one, two):
    return pl.pallas_call(
        add_kernel,
        out_shape=jax.ShapeDtypeStruct(one.shape, BF),
        compiler_params=pltpu.CompilerParams(vmem_limit_bytes=32 * 1024 * 1024),
        name="add_halves",
    )(one, two)


def sum_kernel(in_ref, out_ref):
    total = jnp.sum(in_ref[...].astype(F32), axis=0, keepdims=True).astype(BF)
    out_ref[...] = jnp.broadcast_to(total, out_ref.shape)


def sum_pieces(pieces):
    return pl.pallas_call(
        sum_kernel,
        out_shape=jax.ShapeDtypeStruct(pieces.shape, BF),
        compiler_params=pltpu.CompilerParams(vmem_limit_bytes=32 * 1024 * 1024),
        name="sum_pieces",
    )(pieces)


def sum_bias_kernel(in_ref, out_ref):
    blocks, heads, share, bands, cells = out_ref.shape
    for p in range(blocks):
        for w in range(bands):
            total = jnp.sum(in_ref[:, p, w].astype(F32), axis=0)
            far = total[share * heads : share * (heads + 1)]
            for e in range(heads):
                near = total[share * e : share * (e + 1)]
                out_ref[p, e, :, w, :] = jnp.concatenate([near, far[:, REST * e : REST * (e + 1)]], axis=1)


def sum_bias(pieces, shape):
    return pl.pallas_call(
        sum_bias_kernel,
        out_shape=jax.ShapeDtypeStruct(shape, F32),
        compiler_params=pltpu.CompilerParams(vmem_limit_bytes=32 * 1024 * 1024),
        name="sum_bias",
    )(pieces)


def unpack_kernel(scale, core_ref, mine_ref, theirs_ref, qkv_ref, proj_ref, up_ref, down_ref, gains_ref, in_ref):
    core = core_ref[0]
    in_ref[core] = mine_ref[...]
    in_ref[1 - core] = theirs_ref[...]

    def tile(i):
        return in_ref[i // 9, C * (i % 9) : C * (i % 9 + 1), :].astype(F32) * scale

    half_qk, half_vp = tile(2), tile(5)
    qkv_ref[...] = jnp.concatenate(
        [tile(0), half_qk[:, :64], tile(1), half_qk[:, 64:], tile(3), half_vp[:, :64]], axis=1
    )
    proj_ref[...] = jnp.concatenate([tile(4), half_vp[:, 64:]], axis=1)
    for i in range(FF // 128):
        up_ref[:, 128 * i : 128 * (i + 1)] = tile(6 + i)
        down_ref[:, 128 * i : 128 * (i + 1)] = tile(12 + i)
    wide = in_ref[0, 9 * C : 9 * C + 16, :].astype(F32) * scale
    gains_ref[...] = jnp.concatenate([wide[0:2, :], wide[8:10, :64]], axis=1)


def unpack(core, mine, theirs, scale):
    shapes = ((C, 3 * C), (C, C), (C, FF), (C, FF), (2, C))
    return pl.pallas_call(
        functools.partial(unpack_kernel, scale),
        out_shape=[jax.ShapeDtypeStruct(s, F32) for s in shapes],
        in_specs=[pl.BlockSpec(memory_space=pltpu.SMEM), pl.BlockSpec(memory_space=pltpu.VMEM), pl.BlockSpec(memory_space=pltpu.VMEM)],
        scratch_shapes=[pltpu.VMEM((2,) + mine.shape, BF)],
        compiler_params=pltpu.CompilerParams(vmem_limit_bytes=32 * 1024 * 1024),
        name="unpack_sums",
    )(core, mine, theirs)


def local(tokens, cotangent, region_ids, norm_gains, w_qkv, w_proj, w_up, w_down, earth_bias):
    levels, nrows, cols, channels = tokens.shape
    both = ("lon", "lat")
    lons, lats = lax.axis_size("lon"), lax.axis_size("lat")
    devices = lons * lats

    def corner_perm(value, steps):
        pairs = [
            (a * lats + b, (a + steps) % lons * lats + (b + steps) % lats)
            for a in range(lons)
            for b in range(lats)
        ]
        return lax.ppermute(value, both, pairs)

    lat_cut, lon_cut, corner_cut = cut_halos(tokens, cotangent, region_ids)
    halos = (perm(lat_cut, "lat", -1), perm(lon_cut, "lon", -1), corner_perm(corner_cut, -1))

    weights = {"wqkv": w_qkv, "wp": w_proj, "wup": w_up, "wdt": w_down.T, "gains": norm_gains}
    inner, inner_sums = run_forward(INNER, tokens, cotangent, earth_bias, region_ids, weights)
    edge, sums = run_forward(EDGE, tokens, cotangent, earth_bias, region_ids, weights, halos, inner_sums[2], lons)

    shares = lax.all_to_all(sums[2], "lon", 0, 0, tiled=True)
    states = (inner, edge)
    core = lax.rem(lax.axis_index("lat"), 2)[None]
    cores = [[d for d in range(devices) if d % 2 == c] for c in range(2)]

    def other_core(value):
        return lax.ppermute(value, "lat", [(i, i ^ 1) for i in range(lats)])

    def exchange(value):
        return lax.all_to_all(value, both, 0, 0, axis_index_groups=cores, tiled=True)

    grads, keep, send = run_attention(states, (inner_sums[:2], sums[:2]), weights, core, devices // 2)
    packed = add_halves(keep, other_core(send))
    own, *sent = run_finish((INNER, EDGE), states, grads, weights, tokens.shape)
    packed, shares = lax.optimization_barrier((packed, shares))
    pieces = exchange(packed)
    lat_in = perm(sent[0], "lat", 1)
    lon_in = perm(sent[1], "lon", 1)
    corner_in = corner_perm(sent[2], 1)
    summed, own = lax.optimization_barrier((sum_pieces(pieces), own))
    mine = exchange(summed).reshape(-1, 128)
    grad_tokens = assemble(own, lat_in, lon_in, corner_in)
    mine, grad_tokens = lax.optimization_barrier((mine, grad_tokens))
    cell_count = levels * nrows * cols * devices
    weight_grads = unpack(core, mine, other_core(mine), 1.0 / math.sqrt(cell_count))
    blocks, bands = earth_bias.shape[:2]
    bias_total = sum_bias(shares, (blocks, HEADS, M // lons, bands, M)).transpose(0, 3, 1, 2, 4)
    qkv, proj, up, down, gains = weight_grads
    return (grad_tokens, qkv, proj, up, down.T, gains, bias_total)


def solution(mesh):
    placed = (
        P(None, "lat", "lon", None),
        P(None, "lat", "lon", None),
        P("lat"),
        P(),
        P(),
        P(),
        P(),
        P(),
        P(None, "lat", None, None, None),
    )
    return jax.shard_map(
        local,
        mesh=mesh,
        in_specs=placed,
        out_specs=(
            P(None, "lat", "lon", None),
            P(),
            P(),
            P(),
            P(),
            P(),
            P(None, "lat", None, "lon", None),
        ),
        check_vma=False,
    )
```

```python
import functools
import math

import jax
import jax.numpy as jnp
import numpy as np
from jax import lax
from jax.experimental import pallas as pl
from jax.experimental.pallas import tpu as pltpu
from jax.sharding import PartitionSpec as P

HEADS = 6
HEAD = 32
WLEV = 2
WLAT = 6
WLON = 12
C = HEADS * HEAD
FF = 4 * C
M = WLEV * WLAT * WLON
MAIN = 128
REST = M - MAIN
LANES = (HEADS + 1) * 128
SLABS = WLEV * WLAT

BF = jnp.bfloat16
F32 = jnp.float32
epsilon = 1e-05
inv_root_two = 0.7071067811865476
inv_root_tau = 0.3989422804014327


def perm(value, axis, steps):
    count = lax.axis_size(axis)
    pairs = [(source, (source + steps) % count) for source in range(count)]
    return lax.ppermute(value, axis, pairs)


def dot(left, right):
    return jnp.dot(left, right, preferred_element_type=F32)


def dot_nt(left, right):
    return lax.dot_general(left, right, (((1,), (1,)), ((), ())), preferred_element_type=F32)


def dot_tn(left, right):
    return lax.dot_general(left, right, (((0,), (0,)), ((), ())), preferred_element_type=F32)


def normalize(values):
    centred = values - jnp.mean(values, axis=-1, keepdims=True)
    inverse = lax.rsqrt(jnp.mean(centred * centred, axis=-1, keepdims=True) + epsilon)
    return centred * inverse, inverse


def norm_back(normed, inverse, gain_row, upstream):
    scaled = upstream * gain_row
    return inverse * (
        scaled
        - jnp.mean(scaled, axis=-1, keepdims=True)
        - normed * jnp.mean(scaled * normed, axis=-1, keepdims=True)
    )


def gelu_parts(u):
    cdf = 0.5 + 0.5 * lax.erf(u * inv_root_two)
    bell = jnp.exp2(u * u * (-0.5 * math.log2(math.e)))
    return cdf, cdf + u * (bell * inv_root_tau)


CHUNKS = ((0, 256), (256, 512), (512, 768), (768, 896))


def spread_heads(rows, mask):
    first, last = rows[:MAIN], rows[MAIN:]
    return jnp.concatenate([first] * HEADS + [last] * 8, axis=0) * mask


def per_query(weights_ref, right, right_t, rest_mask):
    parts = []
    for e in range(HEADS):
        parts.append(
            dot(
                right_t[HEAD * e : HEAD * (e + 1), :],
                weights_ref[:, 128 * e : 128 * (e + 1)],
            )
        )
        if e % 2:
            yield None
    first = jnp.concatenate(parts, axis=0).T
    yield None
    last = dot_tn(weights_ref[:, HEADS * 128 :], right) * rest_mask
    total = last[0:REST]
    for e in range(1, HEADS):
        total = total + last[REST * e : REST * (e + 1)]
    yield jnp.concatenate([first, total], axis=0)


def in_turn(*streams):
    streams = [[0, count, pieces] for count, pieces in streams]
    while streams:
        stream = min(streams, key=lambda entry: entry[0] / entry[1])
        stream[0] += 1
        if next(stream[2], streams) is streams:
            streams.remove(stream)


def chain(*streams):
    for stream in streams:
        for piece in stream:
            yield None


def run_events(events):
    tick = 0
    while events:
        for event in list(events):
            start, pieces, stream = event
            for i in range(pieces if start <= tick else 0):
                if next(stream, events) is events:
                    events.remove(event)
                    break
        tick += 1


INNER = ((0, 0), (0, 1), (0, 2))
EDGE = ((0, 3), (1, 0), (1, 1), (1, 2), (1, 3))
STATE = ("ds", "q", "k", "h", "dv", "xb", "dy")
HALF_LAT = WLAT // 2
HALF_LON = WLON // 2
HALO_COLS = 8


HALO_ROWS = 3 * HALO_COLS


class Refs:
    pass


def pack(cells):
    half = cells.shape[0] // 2
    ends = jnp.concatenate([cells[:half, 128:], cells[half:, 128:]], axis=1)
    return jnp.concatenate([cells[:, :128], ends], axis=0).astype(BF)


def unpack_cells(packed):
    packed = packed.astype(F32)
    first = packed.shape[0] * 2 // 3
    ends = jnp.concatenate([packed[first:, :64], packed[first:, 64:]], axis=0)
    return jnp.concatenate([packed[:first], ends], axis=1)


def named(names, refs):
    r = Refs()
    for name, ref in zip(names, refs):
        setattr(r, name, ref)
    return r


def window_pieces(w, n, local_rows, cols):
    for a in range(WLEV):
        for b in range(WLAT):
            slab = (a * WLAT + b) * WLON
            i = HALF_LAT + w * WLAT + b
            j = HALF_LON + n * WLON
            own = min(WLON, cols - j)
            if i < local_rows:
                yield "own", None, (a * local_rows + i) * cols + j, own, slab
                if own < WLON:
                    yield "lon", a * local_rows + i, 0, WLON - own, slab + own
            else:
                i = i - local_rows
                yield "lat", None, (a * HALF_LAT + i) * cols + j, own, slab
                if own < WLON:
                    yield "corner", a * HALF_LAT + i, 0, WLON - own, slab + own


def forward_kernel(names, places, cols, *refs):
    r = named(names, refs)
    edge = hasattr(r, "halo_lat")
    bands = sorted({w for w, n in places})
    step = pl.program_id(0)
    last_step = pl.num_programs(0) - 1

    @pl.when(step == 0)
    def _():
        if edge:
            r.share32[...] = jnp.zeros_like(r.share32)
        r.acc[...] = jnp.zeros_like(r.acc)
        r.proj[...] = jnp.zeros_like(r.proj)
        r.wq[...] = r.wqkv[:, 0:C]
        r.wk[...] = r.wqkv[:, C : 2 * C]
        r.wv[...] = r.wqkv[:, 2 * C : 3 * C]

    gain0 = r.gains[0:1, :]
    gain1 = r.gains[1:2, :]
    scaling = float(HEAD) ** -0.5

    local_rows = r.tok.shape[1]

    def widen(w):
        for at, ref in enumerate((r.tok, r.cot)):
            first = HALF_LAT + w * WLAT
            stop = min(first + WLAT, local_rows)
            for a in range(WLEV):
                for i in range(first, stop):
                    row = a * local_rows + i
                    r.own32[at, row * cols : (row + 1) * cols, :] = ref[a, i].astype(F32)
                yield None
            for i in range(first, stop if edge else first):
                both = unpack_cells(r.halo_lon[at, 0, i - HALF_LAT])
                for a in range(WLEV):
                    r.lon32[at, a * local_rows + i] = both[HALO_COLS * a : HALO_COLS * (a + 1)]
            if stop < first + WLAT:
                for i in range(HALF_LAT):
                    both = unpack_cells(r.halo_corner[at, 0, i])
                    for a in range(WLEV):
                        row = a * HALF_LAT + i
                        r.lat32[at, row * cols : (row + 1) * cols, :] = unpack_cells(r.halo_lat[at, a, i])
                        r.corner32[at, row] = both[HALO_COLS * a : HALO_COLS * (a + 1)]
                yield None

    def row_id(w, b):
        i = HALF_LAT + w * WLAT + b
        if i < local_rows:
            return r.ids[i].astype(F32)
        return r.halo_lat[0, 0, i - local_rows, 0:1, 0:1].astype(F32)

    def bias_rows(at, w):
        kid = jnp.zeros((M, 1), F32)
        qid = jnp.zeros((1, LANES), F32)
        for b in range(WLAT):
            kid = jnp.where(r.krow[...] == b, row_id(w, b), kid)
            qid = jnp.where(r.qrow[...] == b, row_id(w, b), qid)
        rest_pad = jnp.zeros((128 - HEADS * REST, M), F32)
        rest = jnp.concatenate([r.bias[0, at, e, MAIN:, :] for e in range(HEADS)] + [rest_pad], axis=0)
        for e in range(HEADS + 1):
            block = r.bias[0, at, e, :MAIN, :] if e < HEADS else rest
            lanes = slice(128 * e, 128 * (e + 1))
            r.biast[at, :, lanes] = jnp.where(kid == qid[:, lanes], block.T, -1e30)
            yield None
        if edge and w == 0:
            r.gbt[at] = r.gbt_in[0]
        else:
            r.gbt[at] = jnp.zeros((M, LANES), F32)
        yield None

    rest_mask = r.mask[HEADS * 128 :, :].astype(F32)

    def front(t):
        w, n = places[t]
        band = bands.index(w)
        here = slice(t * M, (t + 1) * M)
        for at, to in ((0, r.x), (1, r.c)):
            for name, lead, start, length, slab in window_pieces(w, n, local_rows, cols):
                source = getattr(r, name + "32")
                index = (at,) if lead is None else (at, lead)
                to[t * M + slab : t * M + slab + length, :] = source[index + (slice(start, start + length),)]
            yield None
        x = r.x[here, :]
        r.xb[0, t] = x.astype(BF)
        h = (normalize(x)[0] * gain0).astype(BF)
        r.h[0, t] = h
        yield None
        q = (dot(h, r.wq[...]) * scaling).astype(BF)
        r.q[0, t] = q
        r.qbd[t] = spread_heads(q, r.mask[...])
        yield None
        r.k[0, t] = dot(h, r.wk[...]).astype(BF)
        yield None
        v32 = dot(h, r.wv[...])
        r.v[here, :] = v32.astype(BF)
        vt = v32.T.astype(BF)
        yield None
        for lo, hi in CHUNKS:
            scores = dot_nt(r.k[0, t], r.qbd[t, lo:hi, :]) + r.biast[band, :, lo:hi]
            powers = jnp.exp(scores - jnp.max(scores, axis=0, keepdims=True))
            weights = powers * pl.reciprocal(jnp.sum(powers, axis=0, keepdims=True), approx=True)
            r.p[t, :, lo:hi] = weights
            r.pb[t, :, lo:hi] = weights.astype(BF)
            yield None
        for o in per_query(r.pb.at[t], r.v[here, :], vt, rest_mask):
            yield None
        o = o.astype(BF)
        r.o[here, :] = o
        y = r.x[here, :] + dot(o, r.wp[...]).astype(BF).astype(F32)
        yield None
        n2, r2 = normalize(y)
        r.n2[here, :] = n2
        r.r2[here, :] = r2
        r.g[here, :] = (n2 * gain1).astype(BF)
        r.cb[here, :] = r.c[here, :].astype(BF)
        yield None

    def middle(t):
        here = slice(t * M, (t + 1) * M)
        for lo in range(0, FF, 256):
            part = slice(lo, lo + 256)
            u = dot(r.g[here, :], r.wup[:, part])
            cdf, slope = gelu_parts(u)
            r.act[here, part] = (u * cdf).astype(BF)
            yield None
            r.du[here, part] = (dot(r.cb[here, :], r.wdt[:, part]) * slope).astype(BF)
            yield None

    def back(t):
        w, n = places[t]
        band = bands.index(w)
        here = slice(t * M, (t + 1) * M)
        dg = dot_nt(r.du[here, :], r.wup[...])
        yield None
        dy = r.c[here, :] + norm_back(r.n2[here, :], r.r2[here, :], gain1, dg)
        r.dy[0, t] = dy
        dys = dy.astype(BF)
        r.dys[here, :] = dys
        yield None
        do = dot_nt(dys, r.wp[...]).astype(BF)
        r.dobd[t] = spread_heads(do, r.mask[...])
        yield None
        for lo, hi in CHUNKS:
            weights = r.p[t, :, lo:hi]
            dp = dot_nt(r.v[here, :], r.dobd[t, lo:hi, :]) * weights
            ds = dp - weights * jnp.sum(dp, axis=0, keepdims=True)
            r.gbt[band, :, lo:hi] += ds
            r.ds[0, t, :, lo:hi] = ds.astype(BF)
            yield None
        r.dv[0, t] = dot(r.pb[t], r.dobd[t]).astype(BF)
        yield None

    def sums(t):
        here = slice(t * M, (t + 1) * M)
        for first, left, right in ((0, r.g, r.du), (6, r.cb, r.act)):
            left_t = left[here, :].T
            for lo in range(0, FF, 256):
                part = dot(left_t, right[here, lo : lo + 256])
                r.acc[first + lo // 128] += part[:, :128]
                r.acc[first + lo // 128 + 1] += part[:, 128:]
                yield None

    def proj_sum():
        r.proj[...] += dot_tn(r.o[...], r.dys[...])
        yield None

    def share_bias(at):
        share = M // r.share_out.shape[0]
        gbt = r.gbt.at[at]
        last = gbt[:, HEADS * 128 :].T
        for e in range(HEADS):
            r.bias32[at, M * e : M * e + MAIN, :] = gbt[:, 128 * e : 128 * (e + 1)].T[:, :MAIN]
            r.bias32[at, M * e + MAIN : M * (e + 1), :] = last[REST * e : REST * (e + 1), :MAIN]
            yield None
        far = jnp.concatenate(
            [gbt[MAIN:, 128 * e : 128 * (e + 1)] for e in range(HEADS)]
            + [jnp.zeros((128 - HEADS * REST, 128), F32)],
            axis=0,
        )
        r.bias32[at, M * HEADS : M * HEADS + MAIN, :] = far.T
        r.bias32[at, M * HEADS + MAIN : M * (HEADS + 1), :] = jnp.concatenate(
            [last[REST * e : REST * (e + 1), MAIN:] for e in range(HEADS)]
            + [jnp.zeros((REST, 128 - HEADS * REST), F32)],
            axis=1,
        )
        yield None
        for d in range(r.share_out.shape[0]):
            for e in range(HEADS + 1):
                r.share32[at, d, share * e : share * (e + 1), :] = r.bias32[
                    at, M * e + share * d : M * e + share * (d + 1), :
                ]
            r.share_out[d, 0, at] = r.share32[at, d].astype(BF)
            yield None

    count = len(places)
    length = 31
    events = [(0, 2, widen(bands[0])), (0, 3, bias_rows(0, bands[0]))]
    events += [(1, 2, widen(w)) for w in bands[1:]]
    events += [(2, 2, bias_rows(at, bands[at])) for at in range(1, len(bands))]
    start = [3 + (3 if edge else 2) * t for t in range(count)]
    for t in range(count):
        events.append((start[t], 1, chain(front(t), middle(t), back(t))))
        events.append((start[t] + 22, 1, sums(t)))
    for at in range(len(bands)):
        last = max(t for t, place in enumerate(places) if place[0] == bands[at])
        if edge:
            events.append((start[last] + length + 1, 2, share_bias(at)))
    events.append((start[-1] + length + 1, 1, proj_sum()))
    run_events(events)

    if not edge:
        r.gbt_out[0] = r.gbt[0]

    @pl.when(step == last_step)
    def _():
        r.acc_out[...] = r.acc[...]
        r.proj_out[...] = r.proj[...]


def whole(shape):
    zeros = (0,) * len(shape)
    return pl.BlockSpec(tuple(shape), lambda p: zeros)


def by_level(shape, at, blocks=2):
    block = list(shape)
    block[at] = shape[at] // blocks
    return pl.BlockSpec(tuple(block), lambda p: tuple(p if i == at else 0 for i in range(len(shape))))


def call(kernel, blocks, ins, outs, scratch, name, share_of, limit, *fixed):
    names = [i[0] for i in ins] + [o[0] for o in outs] + [s[0] for s in scratch]
    return pl.pallas_call(
        functools.partial(kernel, names, *fixed),
        grid=(blocks,),
        in_specs=[i[2] for i in ins],
        out_specs=[o[3] for o in outs],
        out_shape=[jax.ShapeDtypeStruct(tuple(o[1]), o[2]) for o in outs],
        scratch_shapes=[pltpu.VMEM(tuple(s[1]), s[2]) for s in scratch],
        compiler_params=pltpu.CompilerParams(
            vmem_limit_bytes=limit * 1024 * 1024,
            dimension_semantics=("arbitrary",),
        ),
        cost_estimate=pl.CostEstimate(
            flops=int(14e9 * share_of), bytes_accessed=int(10e6 * share_of), transcendentals=int(5e6 * share_of)
        ),
        name=name,
    )(*[i[1] for i in ins])


def head_mask():
    head_of_row = np.concatenate(
        [
            np.repeat(np.arange(HEADS), MAIN),
            np.repeat(np.arange(HEADS), REST),
            np.full(128 - HEADS * REST, -1),
        ]
    )
    return jnp.asarray(head_of_row[:, None] == np.arange(C)[None, :] // HEAD, BF)


def run_forward(places, tokens, cotangent, bias, region_ids, weights, halos=None, before=None, lons=8):
    levels, local_rows, cols, channels = tokens.shape
    blocks = levels // WLEV
    count = len(places)
    rows = count * M
    bands = len({w for w, n in places})
    cell_row = (np.arange(M) // WLON % WLAT).astype(np.int32)
    rest = np.concatenate([np.tile(np.arange(MAIN, M), HEADS), np.zeros(128 - HEADS * REST, int)])
    lane_cell = np.concatenate([np.tile(np.arange(MAIN), HEADS), rest])
    edge = halos is not None
    ins = [
        ("tok", tokens, by_level(tokens.shape, 0)),
        ("cot", cotangent, by_level(tokens.shape, 0)),
        ("bias", bias, pl.BlockSpec((1, bands, HEADS, M, M), lambda p: (p, 0, 0, 0, 0))),
        ("ids", region_ids, pl.BlockSpec(memory_space=pltpu.SMEM)),
        ("krow", jnp.asarray(cell_row[:, None]), whole((M, 1))),
        ("qrow", jnp.asarray(cell_row[lane_cell][None, :]), whole((1, LANES))),
        ("mask", head_mask(), whole((LANES, C))),
    ] + [(name, w, whole(w.shape)) for name, w in weights.items()]
    flat = WLEV * local_rows * cols
    acc = (12, C, 128)
    scratch = [
        ("own32", (2, flat, C), F32),
        ("x", (rows, C), F32),
        ("c", (rows, C), F32),
        ("n2", (rows, C), F32),
        ("r2", (rows, 1), F32),
        ("biast", (bands, M, LANES), F32),
        ("gbt", (bands, M, LANES), F32),
        ("p", (count, M, LANES), F32),
        ("pb", (count, M, LANES), BF),
        ("qbd", (count, LANES, C), BF),
        ("dobd", (count, LANES, C), BF),
        ("acc", acc, F32),
        ("proj", (C, C), F32),
        ("act", (rows, FF), BF),
        ("du", (rows, FF), BF),
    ] + [(name, (rows, C), BF) for name in ("v", "o", "g", "cb", "dys")]
    scratch += [(name, (C, C), BF) for name in ("wq", "wk", "wv")]
    outs = []
    for name in STATE:
        shape = (blocks, count, M, LANES if name == "ds" else C)
        outs.append((name, shape, F32 if name == "dy" else BF, by_level(shape, 0)))
    outs += [("acc_out", acc, F32, whole(acc)), ("proj_out", (C, C), F32, whole((C, C)))]
    if edge:
        for name, value in zip(("halo_lat", "halo_lon", "halo_corner"), halos):
            ins.append((name, value, by_level(value.shape, 1)))
        ins.append(("gbt_in", before, by_level(before.shape, 0)))
        share = (lons, blocks, bands, 128, 128)
        outs.append(("share_out", share, BF, by_level(share, 1)))
        scratch += [
            ("lat32", (2, WLEV * HALF_LAT * cols, C), F32),
            ("lon32", (2, WLEV * local_rows, HALO_COLS, C), F32),
            ("corner32", (2, WLEV * HALF_LAT, HALO_COLS, C), F32),
            ("bias32", (bands, M * (HEADS + 1), 128), F32),
            ("share32", (bands, lons, 128, 128), F32),
        ]
    else:
        outs.append(("gbt_out", (blocks, M, LANES), F32, by_level((blocks, M, LANES), 0)))
    name = "edge_windows" if edge else "inner_windows"
    got = call(forward_kernel, blocks, ins, outs, scratch, name, count * blocks / 20, 60, places, cols)
    return got[: len(STATE)], got[len(STATE) :]


def attention_kernel(names, parts, *refs):
    r = named(names, refs)
    step = pl.program_id(0)
    last_step = pl.num_programs(0) - 1
    scaling = float(HEAD) ** -0.5
    rest_mask = r.mask[HEADS * 128 :, :].astype(F32)

    @pl.when(step == 0)
    def _():
        r.acc[...] = jnp.zeros_like(r.acc)

    def window(at, part, t):
        here = slice(at * M, (at + 1) * M)
        get = lambda name: getattr(r, name + str(part)).at[0, t]
        r.h[here, :] = get("h")[...]
        r.dv[here, :] = get("dv")[...]
        r.qbd[at % 4] = spread_heads(get("q")[...], r.mask[...])
        yield None
        k = get("k")[...]
        kt = k.astype(F32).T.astype(BF)
        yield None
        dk = dot(get("ds")[...], r.qbd[at % 4]).astype(BF)
        r.dk[here, :] = dk
        getattr(r, "dk_out" + str(part))[0, t] = dk
        yield None
        for dq in per_query(get("ds"), k, kt, rest_mask):
            yield None
        dq = (dq * scaling).astype(BF)
        r.dq[here, :] = dq
        getattr(r, "dq_out" + str(part))[0, t] = dq
        yield None

    order = [(part, t) for part, count in enumerate(parts) for t in range(count)]
    for at in range(0, len(order), 2):
        in_turn(*[(9, window(at + i, *order[at + i])) for i in range(2)])
    ht = r.h[...].T
    for i, right in enumerate((r.dq, r.dk, r.dv)):
        r.acc[i] += dot(ht, right[...])

    @pl.when(step == last_step)
    def _():
        per = r.keep_out.shape[1]
        core = r.core[0]

        def put_rows(half, at, rows):
            for ref, here in ((r.keep_out, core == half), (r.send_out, core != half)):

                @pl.when(here)
                def _():
                    ref[at : at + rows.shape[0]] = rows

        def put(i, tile):
            put_rows(i // 9, C // per * (i % 9), tile.astype(BF).reshape(C // per, per, 128))

        small = (r.acc[0], r.acc[1], r.acc[2], r.proj0[...] + r.proj1[...])
        for i in range(2):
            one, two = small[2 * i], small[2 * i + 1]
            put(3 * i, one[:, :128])
            put(3 * i + 1, two[:, :128])
            put(3 * i + 2, jnp.concatenate([one[:, 128:], two[:, 128:]], axis=1))
        for i in range(12):
            put(6 + i, r.dense0[i] + r.dense1[i])
        first = jnp.zeros((C, C), F32)
        for i in range(3):
            first = first + r.acc[i] * r.wqkv[:, C * i : C * (i + 1)].astype(F32)
        second = jnp.zeros((C, 128), F32)
        for i in range(6):
            second = second + (r.dense0[i] + r.dense1[i]) * r.wup[:, 128 * i : 128 * (i + 1)].astype(F32)
        sums = [jnp.sum(part.T, axis=0, keepdims=True) for part in (first, second)]
        gains = jnp.concatenate([sums[0] / r.gains[0:1, :], sums[1] / r.gains[1:2, :], jnp.zeros((6, C), F32)], axis=0)
        wide = jnp.concatenate(
            [gains[:, :128], jnp.concatenate([gains[:, 128:], jnp.zeros((8, 64), F32)], axis=1)],
            axis=0,
        )
        wide = jnp.concatenate([wide, jnp.zeros((per - 16, 128), F32)], axis=0)
        put_rows(0, 9 * C // per, wide.astype(BF)[None])


def run_attention(states, sums, weights, core, chips):
    ins, outs = [], []
    blocks = states[0][0].shape[0]
    parts = [state[0].shape[1] for state in states]
    for part, state in enumerate(states):
        for name, value in zip(STATE, state):
            if name not in ("xb", "dy"):
                ins.append((name + str(part), value, by_level(value.shape, 0)))
    mask = head_mask()
    ins += [
        (name + str(part), value, whole(value.shape))
        for part, both in enumerate(sums)
        for name, value in zip(("dense", "proj"), both)
    ]
    ins += [("mask", mask, whole(mask.shape))]
    ins += [(name, weights[name], whole(weights[name].shape)) for name in ("wqkv", "wup", "gains")]
    for part, count in enumerate(parts):
        shape = (blocks, count, M, C)
        for name in ("dq_out", "dk_out"):
            outs.append((name + str(part), shape, BF, by_level(shape, 0)))
    pack = (chips, 2048 // chips, 128)
    outs += [("keep_out", pack, BF, whole(pack)), ("send_out", pack, BF, whole(pack))]
    ins.append(("core", core, pl.BlockSpec(memory_space=pltpu.SMEM)))
    rows = sum(parts) * M
    scratch = [("acc", (3, C, C), F32), ("qbd", (4, LANES, C), BF)]
    scratch += [(name, (rows, C), BF) for name in ("h", "dq", "dk", "dv")]
    got = call(attention_kernel, blocks, ins, outs, scratch, "query_key_grads", 0.3, 60, parts)
    return [got[0:2], got[2:4]], got[4], got[5]


def finish_kernel(names, parts, cols, *refs):
    r = named(names, refs)
    local_rows = r.gt_out.shape[1]
    gain0 = r.gains[0:1, :]

    @pl.when(pl.program_id(0) == 0)
    def _():
        for i in range(3):
            r.w[i] = r.wqkv[:, C * i : C * (i + 1)]
        for name in ("own32", "lat32", "lon32", "corner32"):
            ref = getattr(r, name)
            ref[...] = jnp.zeros_like(ref)

    def window(at, part, t, place):
        get = lambda name: getattr(r, name + str(part)).at[0, t]
        dh = dot_nt(get("dq")[...], r.w[0]) + dot_nt(get("dk")[...], r.w[1]) + dot_nt(get("dv")[...], r.w[2])
        dh = dh.astype(BF).astype(F32)
        yield None
        n1, r1 = normalize(get("xb")[...].astype(F32))
        yield None
        r.gt[at] = get("dy")[...] + norm_back(n1, r1, gain0, dh)
        yield None
        for name, lead, start, length, slab in window_pieces(*place, local_rows, cols):
            target = getattr(r, name + "32")
            index = () if lead is None else (lead,)
            target[index + (slice(start, start + length),)] = r.gt[at, slab : slab + length, :]
        yield None

    order = [(part, t, place) for part, places in enumerate(parts) for t, place in enumerate(places)]
    for at in range(0, len(order), 2):
        in_turn(*[(4, window(at + i, *order[at + i])) for i in range(2)])
    r.gt_out[...] = r.own32[...].astype(BF).reshape(r.gt_out.shape)
    for i in range(HALF_LAT):
        for a in range(WLEV):
            row = a * HALF_LAT + i
            r.lat_out[a, i] = pack(r.lat32[row * cols : (row + 1) * cols, :])
        r.corner_out[0, i] = pack(jnp.concatenate([r.corner32[a * HALF_LAT + i] for a in range(WLEV)], axis=0))
    for i in range(HALF_LAT, local_rows):
        r.lon_out[0, i - HALF_LAT] = pack(
            jnp.concatenate([r.lon32[a * local_rows + i] for a in range(WLEV)], axis=0)
        )


def run_finish(parts, states, grads, weights, shape):
    levels, local_rows, cols, channels = shape
    blocks = levels // WLEV
    ins = []
    for part, (state, grad) in enumerate(zip(states, grads)):
        for name in ("dv", "xb", "dy"):
            value = state[STATE.index(name)]
            ins.append((name + str(part), value, by_level(value.shape, 0)))
        for name, value in zip(("dq", "dk"), grad):
            ins.append((name + str(part), value, by_level(value.shape, 0)))
    ins += [(name, weights[name], whole(weights[name].shape)) for name in ("wqkv", "gains")]
    outs = []
    for name, out in (
        ("gt_out", shape),
        ("lat_out", (levels, HALF_LAT, cols * 3 // 2, 128)),
        ("lon_out", (blocks, local_rows - HALF_LAT, HALO_ROWS, 128)),
        ("corner_out", (blocks, HALF_LAT, HALO_ROWS, 128)),
    ):
        outs.append((name, out, BF, by_level(out, 0)))
    count = sum(len(places) for places in parts)
    scratch = [
        ("w", (3, C, C), BF),
        ("gt", (count, M, C), F32),
        ("own32", (WLEV * local_rows * cols, C), F32),
        ("lat32", (WLEV * HALF_LAT * cols, C), F32),
        ("lon32", (WLEV * local_rows, HALO_COLS, C), F32),
        ("corner32", (WLEV * HALF_LAT, HALO_COLS, C), F32),
    ]
    return call(finish_kernel, blocks, ins, outs, scratch, "token_grads", 0.1, 60, parts, cols)


def cut_kernel(ids_ref, tok_rows, cot_rows, tok_cols, cot_cols, lat_ref, lon_ref, corner_ref):
    levels, half_lat, cols, channels = tok_rows.shape
    cell = lax.broadcasted_iota(jnp.int32, (cols, C), 0)
    for at, (rows, columns) in enumerate(((tok_rows, tok_cols), (cot_rows, cot_cols))):
        for a in range(levels):
            for i in range(half_lat):
                row = rows[a, i].astype(F32)
                if at == 0:
                    row = jnp.where(cell == 0, ids_ref[i].astype(F32), row)
                lat_ref[at, a, i] = pack(row)
        for p in range(levels // WLEV):
            for i in range(columns.shape[1]):
                both = [columns[WLEV * p + a, i, :HALO_COLS, :].astype(F32) for a in range(WLEV)]
                both = pack(jnp.concatenate(both, axis=0))
                if i < half_lat:
                    corner_ref[at, p, i] = both
                else:
                    lon_ref[at, p, i - half_lat] = both


def cut_halos(tokens, cotangent, region_ids):
    levels, local_rows, cols, channels = tokens.shape
    row_spec = pl.BlockSpec((levels, HALF_LAT, cols, C), lambda i: (0, 0, 0, 0))
    col_spec = pl.BlockSpec((levels, local_rows, HALO_COLS, C), lambda i: (0, 0, 0, 0))
    blocks = levels // WLEV
    shapes = (
        (2, levels, HALF_LAT, cols * 3 // 2, 128),
        (2, blocks, local_rows - HALF_LAT, HALO_ROWS, 128),
        (2, blocks, HALF_LAT, HALO_ROWS, 128),
    )
    return pl.pallas_call(
        cut_kernel,
        grid=(1,),
        in_specs=[pl.BlockSpec(memory_space=pltpu.SMEM), row_spec, row_spec, col_spec, col_spec],
        out_specs=[whole(shape) for shape in shapes],
        out_shape=[jax.ShapeDtypeStruct(shape, BF) for shape in shapes],
        compiler_params=pltpu.CompilerParams(vmem_limit_bytes=60 * 1024 * 1024),
        name="cut_halos",
    )(region_ids, tokens, cotangent, tokens, cotangent)


def assemble_kernel(own_ref, lat_ref, lon_ref, corner_ref, out_ref):
    levels, local_rows, cols, channels = out_ref.shape
    keep = lax.broadcasted_iota(jnp.int32, (16, C), 0) >= HALF_LON
    pad = jnp.zeros((16 - HALO_COLS, C), F32)
    for p in range(levels // WLEV):
        for i in range(local_rows):
            both = unpack_cells(corner_ref[p, i] if i < HALF_LAT else lon_ref[p, i - HALF_LAT])
            for a in range(WLEV):
                level = WLEV * p + a
                left = jnp.concatenate([both[HALO_COLS * a : HALO_COLS * (a + 1)], pad], axis=0)
                if i < HALF_LAT:
                    row = unpack_cells(lat_ref[level, i])
                    out_ref[level, i, 16:, :] = row[16:].astype(BF)
                    first = row[:16]
                else:
                    out_ref[level, i, 16:, :] = own_ref[level, i, 16:, :]
                    first = own_ref[level, i, 0:16, :].astype(F32)
                out_ref[level, i, 0:16, :] = jnp.where(keep, first, left).astype(BF)


def assemble(own, *received):
    return pl.pallas_call(
        assemble_kernel,
        out_shape=jax.ShapeDtypeStruct(own.shape, BF),
        compiler_params=pltpu.CompilerParams(vmem_limit_bytes=32 * 1024 * 1024),
        name="assemble",
    )(own, *received)


def sum_kernel(in_ref, out_ref):
    total = jnp.sum(in_ref[...].astype(F32), axis=0, keepdims=True).astype(BF)
    out_ref[...] = jnp.broadcast_to(total, out_ref.shape)


def sum_pieces(pieces):
    return pl.pallas_call(
        sum_kernel,
        out_shape=jax.ShapeDtypeStruct(pieces.shape, BF),
        compiler_params=pltpu.CompilerParams(vmem_limit_bytes=32 * 1024 * 1024),
        name="sum_pieces",
    )(pieces)


def sum_bias_kernel(in_ref, out_ref):
    blocks, heads, share, bands, cells = out_ref.shape
    for p in range(blocks):
        for w in range(bands):
            total = jnp.sum(in_ref[:, p, w].astype(F32), axis=0)
            far = total[share * heads : share * (heads + 1)]
            for e in range(heads):
                near = total[share * e : share * (e + 1)]
                out_ref[p, e, :, w, :] = jnp.concatenate([near, far[:, REST * e : REST * (e + 1)]], axis=1)


def sum_bias(pieces, shape):
    return pl.pallas_call(
        sum_bias_kernel,
        out_shape=jax.ShapeDtypeStruct(shape, F32),
        compiler_params=pltpu.CompilerParams(vmem_limit_bytes=32 * 1024 * 1024),
        name="sum_bias",
    )(pieces)


def unpack_kernel(scale, core_ref, mine_ref, theirs_ref, qkv_ref, proj_ref, up_ref, down_ref, gains_ref, in_ref):
    core = core_ref[0]
    in_ref[core] = mine_ref[...]
    in_ref[1 - core] = theirs_ref[...]

    def tile(i):
        return in_ref[i // 9, C * (i % 9) : C * (i % 9 + 1), :].astype(F32) * scale

    half_qk, half_vp = tile(2), tile(5)
    qkv_ref[...] = jnp.concatenate(
        [tile(0), half_qk[:, :64], tile(1), half_qk[:, 64:], tile(3), half_vp[:, :64]], axis=1
    )
    proj_ref[...] = jnp.concatenate([tile(4), half_vp[:, 64:]], axis=1)
    for i in range(FF // 128):
        up_ref[:, 128 * i : 128 * (i + 1)] = tile(6 + i)
        down_ref[:, 128 * i : 128 * (i + 1)] = tile(12 + i)
    wide = in_ref[0, 9 * C : 9 * C + 16, :].astype(F32) * scale
    gains_ref[...] = jnp.concatenate([wide[0:2, :], wide[8:10, :64]], axis=1)


def unpack(core, mine, theirs, scale):
    shapes = ((C, 3 * C), (C, C), (C, FF), (C, FF), (2, C))
    return pl.pallas_call(
        functools.partial(unpack_kernel, scale),
        out_shape=[jax.ShapeDtypeStruct(s, F32) for s in shapes],
        in_specs=[pl.BlockSpec(memory_space=pltpu.SMEM), pl.BlockSpec(memory_space=pltpu.VMEM), pl.BlockSpec(memory_space=pltpu.VMEM)],
        scratch_shapes=[pltpu.VMEM((2,) + mine.shape, BF)],
        compiler_params=pltpu.CompilerParams(vmem_limit_bytes=32 * 1024 * 1024),
        name="unpack_sums",
    )(core, mine, theirs)


def local(tokens, cotangent, region_ids, norm_gains, w_qkv, w_proj, w_up, w_down, earth_bias):
    levels, nrows, cols, channels = tokens.shape
    both = ("lon", "lat")
    lons, lats = lax.axis_size("lon"), lax.axis_size("lat")
    devices = lons * lats

    def corner_perm(value, steps):
        pairs = [
            (a * lats + b, (a + steps) % lons * lats + (b + steps) % lats)
            for a in range(lons)
            for b in range(lats)
        ]
        return lax.ppermute(value, both, pairs)

    lat_cut, lon_cut, corner_cut = cut_halos(tokens, cotangent, region_ids)
    halos = (perm(lat_cut, "lat", -1), perm(lon_cut, "lon", -1), corner_perm(corner_cut, -1))

    weights = {"wqkv": w_qkv, "wp": w_proj, "wup": w_up, "wdt": w_down.T, "gains": norm_gains}
    inner, inner_sums = run_forward(INNER, tokens, cotangent, earth_bias, region_ids, weights)
    edge, sums = run_forward(EDGE, tokens, cotangent, earth_bias, region_ids, weights, halos, inner_sums[2], lons)

    shares = lax.all_to_all(sums[2], "lon", 0, 0, tiled=True)
    states = (inner, edge)
    core = lax.rem(lax.axis_index("lat"), 2)[None]
    cores = [[d for d in range(devices) if d % 2 == c] for c in range(2)]

    def other_core(value):
        return lax.ppermute(value, "lat", [(i, i ^ 1) for i in range(lats)])

    def exchange(value):
        return lax.all_to_all(value, both, 0, 0, axis_index_groups=cores, tiled=True)

    grads, keep, send = run_attention(states, (inner_sums[:2], sums[:2]), weights, core, devices // 2)
    packed = (keep.astype(F32) + other_core(send).astype(F32)).astype(BF)
    own, *sent = run_finish((INNER, EDGE), states, grads, weights, tokens.shape)
    packed, shares = lax.optimization_barrier((packed, shares))
    pieces = exchange(packed)
    lat_in = perm(sent[0], "lat", 1)
    lon_in = perm(sent[1], "lon", 1)
    corner_in = corner_perm(sent[2], 1)
    summed, own = lax.optimization_barrier((sum_pieces(pieces), own))
    mine = exchange(summed).reshape(-1, 128)
    grad_tokens = assemble(own, lat_in, lon_in, corner_in)
    mine, grad_tokens = lax.optimization_barrier((mine, grad_tokens))
    cell_count = levels * nrows * cols * devices
    weight_grads = unpack(core, mine, other_core(mine), 1.0 / math.sqrt(cell_count))
    blocks, bands = earth_bias.shape[:2]
    bias_total = sum_bias(shares, (blocks, HEADS, M // lons, bands, M)).transpose(0, 3, 1, 2, 4)
    qkv, proj, up, down, gains = weight_grads
    return (grad_tokens, qkv, proj, up, down.T, gains, bias_total)


def solution(mesh):
    placed = (
        P(None, "lat", "lon", None),
        P(None, "lat", "lon", None),
        P("lat"),
        P(),
        P(),
        P(),
        P(),
        P(),
        P(None, "lat", None, None, None),
    )
    return jax.shard_map(
        local,
        mesh=mesh,
        in_specs=placed,
        out_specs=(
            P(None, "lat", "lon", None),
            P(),
            P(),
            P(),
            P(),
            P(),
            P(None, "lat", None, "lon", None),
        ),
        check_vma=False,
    )
```
